32 devices in a mesh: dp: 8 (over z, y), tensor: 4 (over x, core).
Axes of the slice: x: 2, y: 2, z: 4, core: 2. Of those that a mesh axis runs over, the one named last changes fastest.
Arguments:
- inputs: bfloat16 [8192, 768], P(('dp', 'tensor')), may hold values from -6 to 6
- cotangent: bfloat16 [8192, 768], P(('dp', 'tensor')), may hold values from -6 to 6
- norm_gains: bfloat16 [2, 2, 768], replicated, may hold values from 0.099609375 to 1.8984375
- in_weight: bfloat16 [2, 2, 768, 384], P(None, None, None, 'tensor'), may hold values from -0.21875 to 0.21875
- forget_weight: bfloat16 [2, 768, 384], P(None, None, 'tensor'), may hold values from -0.21875 to 0.21875
- gate_weight: bfloat16 [2, 2, 768, 384], P(None, None, None, 'tensor'), may hold values from -0.21875 to 0.21875
- out_weight: bfloat16 [2, 2, 384, 768], P(None, None, 'tensor'), may hold values from -0.3125 to 0.3125
- phase: float32 [2, 384], P(None, 'tensor'), may hold values from -3.140625 to 3.140625
- bound_logit: float32 [2, 384], P(None, 'tensor'), may hold values from -3 to 3
- group_gain: bfloat16 [2, 2, 384], P(None, None, 'tensor'), may hold values from 0.099609375 to 1.8984375
- ffn_weight: bfloat16 [2, 2, 768, 1536], P(None, None, None, 'tensor'), may hold values from -0.21875 to 0.21875
- down_weight: bfloat16 [2, 1536, 768], P(None, 'tensor'), may hold values from -0.21875 to 0.21875
Outputs:
- outputs: bfloat16 [8192, 768], P(('dp', 'tensor'))
- input_grad: bfloat16 [8192, 768], P(('dp', 'tensor'))
- norm_gains_grad: float32 [2, 2, 768], P(None, None, 'tensor')
- in_weight_grad: float32 [2, 2, 768, 384], P(None, None, None, 'tensor')
- forget_weight_grad: float32 [2, 768, 384], P(None, None, 'tensor')
- gate_weight_grad: float32 [2, 2, 768, 384], P(None, None, None, 'tensor')
- out_weight_grad: float32 [2, 2, 384, 768], P(None, None, 'tensor')
- phase_grad: float32 [2, 384], P(None, 'tensor')
- bound_logit_grad: float32 [2, 384], P(None, 'tensor')
- group_gain_grad: float32 [2, 2, 384], P(None, None, 'tensor')
- ffn_weight_grad: float32 [2, 2, 768, 1536], P(None, None, None, 'tensor')
- down_weight_grad: float32 [2, 1536, 768], P(None, 'tensor')
The draws below stay inside these ranges and needn't reach their ends.
All inputs are finite; a program needn't handle non-finite values.
Results may differ from the reference program's by a relative error of at most 0.029.
Values may be sent and summed in bfloat16 or wider, within the bound.
A program may use at most 128 MiB of HBM per device.

```python
import math
import jax
import jax.numpy as jnp
from jax import lax

D = 768
C = 384
FF = 1536
GROUP_CH = 48
LAYERS = 2
SEQ = 1024
TOKENS = 8192
N_DP = 8


def steps_of(rng, extent, shards, smallest, top_value):
    level = 1.0
    for dim, blocks in shards:
        heights = jax.random.uniform(jax.random.fold_in(jax.random.fold_in(rng, 6), dim), (blocks,), jnp.float32, smallest / len(shards), top_value / len(shards))
        level = level * jnp.repeat(jnp.exp(heights), extent[dim] // blocks).reshape((-1,) + (1,) * (len(extent) - 1 - dim))
    return level


def normal_values(rng, dims, width, most, shards=(), held_as=jnp.bfloat16):
    drawn = width * jax.random.normal(rng, dims, jnp.float32)
    if shards:
        drawn = drawn * steps_of(rng, dims, shards, -0.22, 0.18)
    return jnp.clip(drawn, -most, most).astype(held_as)


def setup_inputs(seed: int = 0) -> dict:
    arg_keys = jax.random.split(jax.random.key(seed), 13)
    inputs = normal_values(arg_keys[0], (TOKENS, D), 1.0, 6.0, ((0, 32),))
    cotangent = normal_values(arg_keys[1], (TOKENS, D), 1.0, 6.0, ((0, 32),))
    norm_gains = jnp.clip(1.0 + 0.18 * jax.random.normal(arg_keys[2], (LAYERS, 2, D), jnp.float32), 0.099609375, 1.8984375).astype(jnp.bfloat16)
    in_weight = normal_values(arg_keys[3], (LAYERS, 2, D, C), D ** -0.5, 0.21875, ((3, 4),))
    forget_weight = normal_values(arg_keys[4], (LAYERS, D, C), D ** -0.5, 0.21875, ((2, 4),))
    gate_weight = normal_values(arg_keys[5], (LAYERS, 2, D, C), D ** -0.5, 0.21875, ((3, 4),))
    out_weight = normal_values(arg_keys[6], (LAYERS, 2, C, D), C ** -0.5, 0.3125, ((2, 4),))
    phase = jnp.clip(jax.random.uniform(arg_keys[7], (LAYERS, C), jnp.float32, -3.140625, 3.140625), -3.140625, 3.140625)
    bound_logit = jnp.clip(jax.random.uniform(arg_keys[8], (LAYERS, C), jnp.float32, -3.0, 3.0) * steps_of(arg_keys[8], (LAYERS, C), ((1, 4),), -0.4, 0.0), -3.0, 3.0)
    group_gain = jnp.clip(1.0 + 0.18 * jax.random.normal(arg_keys[9], (LAYERS, 2, C), jnp.float32), 0.099609375, 1.8984375).astype(jnp.bfloat16)
    ffn_weight = normal_values(arg_keys[10], (LAYERS, 2, D, FF), D ** -0.5, 0.21875, ((3, 4),))
    down_weight = normal_values(arg_keys[11], (LAYERS, FF, D), (FF // 2) ** -0.5, 0.21875, ((1, 4),))
    return dict(inputs=inputs, cotangent=cotangent, norm_gains=norm_gains, in_weight=in_weight, forget_weight=forget_weight, gate_weight=gate_weight, out_weight=out_weight, phase=phase, bound_logit=bound_logit, group_gain=group_gain, ffn_weight=ffn_weight, down_weight=down_weight)


eps_norm = 1e-06
eps_group = 1e-05

@jax.custom_vjp
def low(v):
    return lax.optimization_barrier(v.astype(jnp.bfloat16)).astype(jnp.float32)

@jax.custom_vjp
def low_back(v):
    return v

def low_keep(v):
    return (low(v), None)

def low_pass(kept, grad):
    return (grad,)

def back_keep(v):
    return (v, None)

def back_low(kept, grad):
    return (low(grad),)
low.defvjp(low_keep, low_pass)
low_back.defvjp(back_keep, back_low)

def matmul_high(left, right, form):
    return jnp.einsum(form, left, right, precision=lax.Precision.HIGHEST)

def norm_apply(values, gain_row):
    inv_scale = lax.rsqrt(lax.optimization_barrier(jnp.mean(values * values, axis=-1, keepdims=True)) + eps_norm)
    return values * inv_scale * gain_row

def combine(earlier, latter):
    first_re, first_im, lift_re, lift_im = earlier
    second_re, second_im, push_re, push_im = latter
    return (second_re * first_re - second_im * first_im, second_re * first_im + second_im * first_re, second_re * lift_re - second_im * lift_im + push_re, second_re * lift_im + second_im * lift_re + push_im)

def mixer_branch(normed, in_pair, forget_mat, gate_pair, out_pair, angle_row, bound_row, gain_pair):
    in_re = low_back(matmul_high(normed, in_pair[0], 'bsd,dc->bsc'))
    in_im = low_back(matmul_high(normed, in_pair[1], 'bsd,dc->bsc'))
    forget_pre = low_back(matmul_high(normed, forget_mat, 'bsd,dc->bsc'))
    gate_re = low_back(matmul_high(normed, gate_pair[0], 'bsd,dc->bsc'))
    gate_im = low_back(matmul_high(normed, gate_pair[1], 'bsd,dc->bsc'))
    lower_bound = jax.nn.sigmoid(bound_row)
    keep_rate = lower_bound + (1.0 - lower_bound) * jax.nn.sigmoid(forget_pre)
    states = lax.associative_scan(combine, (keep_rate * jnp.cos(angle_row), keep_rate * jnp.sin(angle_row), (1.0 - keep_rate) * jax.nn.silu(in_re), (1.0 - keep_rate) * jax.nn.silu(in_im)), axis=1)
    state_re = states[2]
    state_im = states[3]
    batch_size, length, channels = state_re.shape
    grid_shape = (batch_size, length, channels // GROUP_CH, GROUP_CH)
    joined = jnp.concatenate([state_re.reshape(grid_shape), state_im.reshape(grid_shape)], axis=-1)
    centre = lax.optimization_barrier(jnp.mean(joined, axis=-1, keepdims=True))
    deviation = joined - centre
    inv_scale = lax.rsqrt(lax.optimization_barrier(jnp.mean(deviation * deviation, axis=-1, keepdims=True)) + eps_group)
    unit_all = deviation * inv_scale
    unit_re = unit_all[..., :GROUP_CH].reshape(batch_size, length, channels)
    unit_im = unit_all[..., GROUP_CH:].reshape(batch_size, length, channels)
    mixed_re = low(unit_re * gain_pair[0] * jax.nn.sigmoid(gate_re))
    mixed_im = low(unit_im * gain_pair[1] * jax.nn.sigmoid(gate_im))
    return matmul_high(mixed_re, out_pair[0], 'bsc,cd->bsd') + matmul_high(mixed_im, out_pair[1], 'bsc,cd->bsd')

def feed_branch(normed, ffn_pair, down_mat):
    gate_val = low_back(matmul_high(normed, ffn_pair[0], 'bsd,df->bsf'))
    up_val = low_back(matmul_high(normed, ffn_pair[1], 'bsd,df->bsf'))
    hidden = low(jax.nn.silu(gate_val) * up_val)
    return matmul_high(hidden, down_mat, 'bsf,fd->bsd')

def forward(stream, norm_gains, in_weight, forget_weight, gate_weight, out_weight, phase, bound_logit, group_gain, ffn_weight, down_weight):
    for layer_idx in range(LAYERS):
        normed = low(norm_apply(stream, norm_gains[layer_idx, 0]))
        stream = stream + low_back(mixer_branch(normed, in_weight[layer_idx], forget_weight[layer_idx], gate_weight[layer_idx], out_weight[layer_idx], phase[layer_idx], bound_logit[layer_idx], group_gain[layer_idx]))
        normed = low(norm_apply(stream, norm_gains[layer_idx, 1]))
        stream = stream + low_back(feed_branch(normed, ffn_weight[layer_idx], down_weight[layer_idx]))
    return stream

def reference(inputs, cotangent, norm_gains, in_weight, forget_weight, gate_weight, out_weight, phase, bound_logit, group_gain, ffn_weight, down_weight):
    params = tuple((param.astype(jnp.float32) for param in (norm_gains, in_weight, forget_weight, gate_weight, out_weight, phase, bound_logit, group_gain, ffn_weight, down_weight)))
    per_step = math.gcd(N_DP, max(1, 4096 // SEQ))
    steps_count = N_DP // per_step
    stream_groups = inputs.astype(jnp.float32).reshape(steps_count, per_step, SEQ, D)
    cotangent_groups = cotangent.astype(jnp.float32).reshape(steps_count, per_step, SEQ, D)

    def one_group(totals, pieces):
        stream_in, cotangent_in = pieces
        result, pullback = jax.vjp(forward, stream_in, *params)
        grads_all = pullback(cotangent_in)
        totals = tuple((total + extra for total, extra in zip(totals, grads_all[1:])))
        return (totals, (result, grads_all[0]))
    start_totals = tuple((jnp.zeros(param.shape, jnp.float32) for param in params))
    totals, (results, input_grads) = lax.scan(one_group, start_totals, (stream_groups, cotangent_groups))
    outputs = results.reshape(TOKENS, D).astype(jnp.bfloat16)
    input_grad = input_grads.reshape(TOKENS, D).astype(jnp.bfloat16)
    return (outputs, input_grad, totals[0], totals[1], totals[2], totals[3], totals[4], totals[5], totals[6], totals[7], totals[8], totals[9])
```

```python
import functools
import types

import jax
import jax.numpy as jnp
from jax import lax
from jax.experimental import pallas as pl
from jax.experimental.pallas import tpu as pltpu
from jax.sharding import PartitionSpec as P

MESH = pl.DeviceIdType.MESH
F32 = jnp.float32
BF16 = jnp.bfloat16

GROUP_CH = 48
EPS_NORM = 1e-06
EPS_GROUP = 1e-05
LANES = 128
SEGS = 8
CHUNKS = 4
VMEM_BYTES = 63 * 1024 * 1024


def sigmoid(v):
    return 0.5 * jnp.tanh(0.5 * v) + 0.5


def mm(left, right):
    return jnp.dot(left, right, preferred_element_type=F32)


def mm_nt(left, right):
    return lax.dot_general(left, right, (((1,), (1,)), ((), ())), preferred_element_type=F32)


def mm_tn(left, right):
    return lax.dot_general(left, right, (((0,), (0,)), ((), ())), preferred_element_type=F32)


def loop(count, body):
    def step(index, carry):
        body(index)
        return carry

    lax.fori_loop(0, count, step, 0)


def iota(shape, dim):
    return lax.broadcasted_iota(jnp.int32, shape, dim)


def scratch_of(z):
    L, D, C, F, R, N = z.L, z.D, z.C, z.F, z.R, CHUNKS
    rows = (2, N, 2, R)
    own = (N, R)
    bufs = dict(
        wmix=((L, D, 5 * C), BF16),
        wout=((L, 2 * C, D), BF16),
        wffn=((L, D, 2 * F), BF16),
        par=((L, 8, C), F32),
        ngf=((L, 2, D), F32),
        gsum=((C, C), BF16),
        st=((L + 1, 2, *own, D), F32),
        mixfull=((L, *rows, D), BF16),
        ffnfull=((L, *rows, D), BF16),
        gfull=((L, 2, *rows, D), BF16),
        proj=((L, *rows, 5 * C), F32),
        state=((L, 2, 2, 2, SEGS + N * R, C), F32),
        unit=((L, 2, *rows, C), F32),
        inv=((L, *rows, C), F32),
        mixed=((L, *rows, 2 * C), BF16),
        gup=((L, *rows, 2 * F), BF16),
        hidden=((L, *rows, F), BF16),
        keep=((*rows, C), F32),
        drive=((2, *rows, C), F32),
        seg=((3, 2, 2, SEGS, C), F32),
        segk=((L, 2, 2, SEGS, C), F32),
        cur=((2, 2, 2, SEGS, C), F32),
        tot=((2, 2, R, C), F32),
        dgu=((*rows, 2 * F), BF16),
        dproj=((*rows, 5 * C), BF16),
        psc=((2, R, D), F32),
        xpart=((*own, D), F32),
        opart=((*own, D), F32),
        grad=((*own, D), F32),
        stage=((3, *own, D), BF16),
        land=((2, 3, *own, D), BF16),
        gacc=((L, 2, SEGS, D), F32),
        sacc=((L, 4, SEGS, C), F32),
    )
    sems = dict(
        ags=(4 * L, 3, N),
        agr=(4 * L, 3, N),
        rss=(4 * L, 3, N),
        rsr=(4 * L, 3, N),
        wsem=(L, 2),
    )
    names = list(bufs) + list(sems)
    shapes = [pltpu.VMEM(s, d) for s, d in bufs.values()]
    shapes += [pltpu.SemaphoreType.DMA(s) for s in sems.values()]
    return names, shapes


IN_NAMES = ("x", "ct", "ng", "inw", "fw", "gw", "ow", "ph", "bl", "gg", "ffw", "dw")
OUT_NAMES = ("out", "ig", "gffn", "gdown", "gmix", "gout", "small", "gains")


def mega(z, names, *refs):
    r = types.SimpleNamespace(**dict(zip(IN_NAMES + OUT_NAMES + tuple(names), refs)))
    L, D, C, F, R, N = z.L, z.D, z.C, z.F, z.R, CHUNKS
    ch = z.ch
    Q = R // SEGS
    dp = lax.axis_index("dp")
    me = lax.axis_index("tensor")
    core = lax.rem(me, 2)
    xi = me // 2
    other = 1 - xi
    sib = xi * 2 + 1 - core
    xnb = other * 2 + core

    barrier = pltpu.get_barrier_semaphore()
    for peer in (sib, xnb):
        pl.semaphore_signal(barrier, inc=1, device_id=(dp, peer), device_id_type=MESH)
    pl.semaphore_wait(barrier, 2)

    def remote(src, dst, send, recv, peer):
        return pltpu.make_async_remote_copy(
            src_ref=src,
            dst_ref=dst,
            send_sem=send,
            recv_sem=recv,
            device_id=(dp, peer),
            device_id_type=MESH,
        )

    def ag_copy(e, full, c, kind):
        chip = other if kind == 2 else xi
        peer = xnb if kind == 0 else sib
        ref = full.at[chip, c, core]
        return remote(ref, ref, r.ags.at[e, kind, c], r.agr.at[e, kind, c], peer)

    def ag_landing(e, full, c, kind):
        chip = xi if kind == 1 else other
        col = core if kind == 0 else 1 - core
        ref = full.at[chip, c, col]
        return remote(ref, ref, r.ags.at[e, kind, c], r.agr.at[e, kind, c], sib)

    def ag_start(e, full, c):
        ag_copy(e, full, c, 0).start()
        ag_copy(e, full, c, 1).start()

    def ag_take_x(e, full, c):
        ag_landing(e, full, c, 0).wait_recv()
        ag_copy(e, full, c, 2).start()

    def rs_copy(e, c, kind):
        side = 0 if z.single_side else None
        return remote(
            r.stage.at[kind, c],
            r.land.at[r_side(e), kind, c],
            r.rss.at[e, kind, c],
            r.rsr.at[e, kind, c],
            xnb if kind == 1 else sib,
        )

    def r_side(e):
        return e // (2 * L)

    def rs_other(e, c):
        r.stage[0, c] = r.psc[1 - core].astype(BF16)
        rs_copy(e, c, 0).start()
        r.xpart[c] = r.psc[core]

    def rs_pass(e, c):
        rs_copy(e, c, 0).wait_recv()
        r.stage[1, c] = (r.xpart[c] + r.land[r_side(e), 0, c].astype(F32)).astype(BF16)
        rs_copy(e, c, 1).start()

    def rs_own(e, c):
        r.stage[2, c] = r.psc[1 - core].astype(BF16)
        rs_copy(e, c, 2).start()
        r.opart[c] = r.psc[core]

    def rs_final(e, full, c):
        rs_copy(e, c, 2).wait_recv()
        rs_copy(e, c, 1).wait_recv()
        side = r_side(e)
        total = r.opart[c] + r.land[side, 2, c].astype(F32) + r.land[side, 1, c].astype(F32)
        for kind in range(3):
            rs_copy(e, c, kind).wait_send()
            ag_copy(e, full, c, kind).wait_send()
        return total

    def gather_loop(e, full, order, stage):
        def step(j):
            @pl.when(j < N)
            def _():
                ag_landing(e, full, order(j), 1).wait_recv()

            @pl.when((j >= N - 1) & (j < 2 * N - 1))
            def _():
                ag_take_x(e, full, order(j - N + 1))

            @pl.when(j >= N)
            def _():
                ag_landing(e, full, order(j - N), 2).wait_recv()

            stage(j)

        loop(2 * N, step)

    def chip_chunk(j, order, own_first):
        first = j < N
        chunk = order(jnp.where(first, j, j - N))
        if own_first:
            return jnp.where(first, xi, other), chunk
        return jnp.where(first, other, xi), chunk

    ascending = lambda j: j
    descending = lambda j: N - 1 - j

    def norm_rows(s):
        return lax.rsqrt(jnp.mean(s * s, axis=-1, keepdims=True) + EPS_NORM)

    def group_sum(v):
        high = v.astype(BF16)
        rest = (v - high.astype(F32)).astype(BF16)
        weight = r.gsum[...]
        return (mm(high, weight) + mm(rest, weight)) * (1.0 / (2 * GROUP_CH))

    def fold(v):
        return jnp.sum(v.reshape(v.shape[0] // SEGS, SEGS, v.shape[1]), axis=0)

    def flat(v):
        return v.reshape(-1, v.shape[-1])

    w_copies = [
        pltpu.make_async_copy(
            r.ffw.at[l, k], r.wffn.at[l, :, pl.ds(k * F, F)], r.wsem.at[l, k]
        )
        for l in range(L)
        for k in range(2)
    ]
    for copy in w_copies:
        copy.start()

    tokens = N * R
    width = tokens // SEGS
    row = iota((tokens, tokens), 0)
    col = iota((tokens, tokens), 1)
    place = lax.rem(row, SEGS) * width + row // SEGS
    perm = jnp.where(col == place, 1.0, 0.0).astype(BF16)
    r.st[0, 0] = mm(perm, r.x[...]).reshape(N, R, D)
    r.grad[...] = mm(perm, r.ct[...]).reshape(N, R, D)

    r.ngf[...] = r.ng[...].astype(F32)
    r.wmix[...] = jnp.zeros_like(r.wmix)
    r.wout[...] = jnp.zeros_like(r.wout)
    r.par[...] = jnp.zeros_like(r.par)
    r.gacc[...] = jnp.zeros_like(r.gacc)
    r.sacc[...] = jnp.zeros_like(r.sacc)
    for l in range(L):
        parts = (r.inw.at[l, 0], r.inw.at[l, 1], r.fw.at[l], r.gw.at[l, 0], r.gw.at[l, 1])
        for k, part in enumerate(parts):
            r.wmix[l, :, k * C : k * C + ch] = part[...]
        for k in range(2):
            r.wout[l, k * C : k * C + ch, :] = r.ow[l, k]
        angle = r.ph[l : l + 1, :]
        turn_cos, turn_sin = jnp.cos(angle), jnp.sin(angle)
        r.par[l, 0:1, 0:ch] = turn_cos
        r.par[l, 1:2, 0:ch] = turn_sin
        r.par[l, 2:3, 0:ch] = sigmoid(r.bl[l : l + 1, :])
        r.par[l, 3:4, 0:ch] = r.gg[l, 0:1, :].astype(F32)
        r.par[l, 4:5, 0:ch] = r.gg[l, 1:2, :].astype(F32)
        for _ in range(width.bit_length() - 1):
            turn_cos, turn_sin = (
                turn_cos * turn_cos - turn_sin * turn_sin,
                2.0 * turn_cos * turn_sin,
            )
        r.par[l, 5:6, 0:ch] = turn_cos
        r.par[l, 6:7, 0:ch] = turn_sin
    gi, gj = iota((C, C), 0), iota((C, C), 1)
    same = (gi // GROUP_CH == gj // GROUP_CH) & (gi < ch) & (gj < ch)
    r.gsum[...] = jnp.where(same, 1.0, 0.0).astype(BF16)

    def rows_of(q):
        return slice(q * SEGS, (q + 1) * SEGS)

    def scan_local(l, chip, c, turn_cos, turn_sin):
        for k in range(2):
            h_re, h_im, prod = r.seg[0, chip, k], r.seg[1, chip, k], r.seg[2, chip, k]
            for q in range(Q):
                rate = r.keep[chip, c, k, rows_of(q), :]
                h_re, h_im = (
                    rate * (turn_cos * h_re - turn_sin * h_im) + r.drive[0, chip, c, k, rows_of(q), :],
                    rate * (turn_cos * h_im + turn_sin * h_re) + r.drive[1, chip, c, k, rows_of(q), :],
                )
                prod = prod * rate
            r.seg[0, chip, k], r.seg[1, chip, k], r.seg[2, chip, k] = h_re, h_im, prod

    def scan_final(l, chip, c, turn_cos, turn_sin):
        base = SEGS + c * R
        for k in range(2):
            h_re, h_im = r.cur[0, chip, k], r.cur[1, chip, k]
            for q in range(Q):
                rate = r.keep[chip, c, k, rows_of(q), :]
                h_re, h_im = (
                    rate * (turn_cos * h_re - turn_sin * h_im) + r.drive[0, chip, c, k, rows_of(q), :],
                    rate * (turn_cos * h_im + turn_sin * h_re) + r.drive[1, chip, c, k, rows_of(q), :],
                )
                at = pl.ds(pl.multiple_of(base + q * SEGS, SEGS), SEGS)
                r.state[l, 0, chip, k, at, :] = h_re
                r.state[l, 1, chip, k, at, :] = h_im
            r.cur[0, chip, k], r.cur[1, chip, k] = h_re, h_im

    def scan_back_local(l, chip, c, turn_cos, turn_sin):
        for k in range(2):
            u_re, u_im = r.seg[0, chip, k], r.seg[1, chip, k]
            for q in reversed(range(Q)):
                rate = r.keep[chip, c, k, rows_of(q), :]
                t_re = r.drive[0, chip, c, k, rows_of(q), :] + u_re
                t_im = r.drive[1, chip, c, k, rows_of(q), :] + u_im
                u_re = rate * (turn_cos * t_re + turn_sin * t_im)
                u_im = rate * (turn_cos * t_im - turn_sin * t_re)
            r.seg[0, chip, k], r.seg[1, chip, k] = u_re, u_im

    def scan_back_final(l, chip, c, turn_cos, turn_sin):
        for k in range(2):
            u_re, u_im = r.cur[0, chip, k], r.cur[1, chip, k]
            for q in reversed(range(Q)):
                rate = r.keep[chip, c, k, rows_of(q), :]
                t_re = r.drive[0, chip, c, k, rows_of(q), :] + u_re
                t_im = r.drive[1, chip, c, k, rows_of(q), :] + u_im
                r.tot[0, k, rows_of(q), :] = t_re
                r.tot[1, k, rows_of(q), :] = t_im
                u_re = rate * (turn_cos * t_re + turn_sin * t_im)
                u_im = rate * (turn_cos * t_im - turn_sin * t_re)
            r.cur[0, chip, k], r.cur[1, chip, k] = u_re, u_im

    def carry_over(l, back):
        all_cos, all_sin = r.par[l, 5:6, :], r.par[l, 6:7, :]
        if back:
            all_sin = -all_sin
        c_re = jnp.zeros((1, C), F32)
        c_im = jnp.zeros((1, C), F32)
        order = [(chip, k, s) for chip in range(2) for k in range(2) for s in range(SEGS)]
        for chip, k, s in reversed(order) if back else order:
            one = slice(s, s + 1)
            r.cur[0, chip, k, one, :] = c_re
            r.cur[1, chip, k, one, :] = c_im
            prod = r.segk[l, chip, k, one, :]
            c_re, c_im = (
                prod * (all_cos * c_re - all_sin * c_im) + r.seg[0, chip, k, one, :],
                prod * (all_cos * c_im + all_sin * c_re) + r.seg[1, chip, k, one, :],
            )

    def forward_layer(l):
        turn_cos, turn_sin, lower = r.par[l, 0:1, :], r.par[l, 1:2, :], r.par[l, 2:3, :]
        gain_re, gain_im = r.par[l, 3:4, :], r.par[l, 4:5, :]
        e = 2 * l
        full = r.mixfull.at[l]

        def send_mix(c):
            @pl.when(l > 0)
            def _():
                r.st[l, 0, c] = r.st[l - 1, 1, c] + rs_final(e - 1, r.ffnfull.at[l - 1], c)

            s = r.st[l, 0, c]
            full[xi, c, core] = (s * norm_rows(s) * r.ngf[l, 0:1, :]).astype(BF16)
            ag_start(e, full, c)

        loop(N, send_mix)

        r.seg[0:2] = jnp.zeros((2, 2, 2, SEGS, C), F32)
        r.seg[2] = jnp.ones((2, 2, SEGS, C), F32)

        def project(j):
            chip, c = chip_chunk(j, ascending, True)
            proj = mm(flat(full[chip, c]), r.wmix[l])
            r.proj[l, chip, c] = proj.reshape(2, R, 5 * C)
            in_re, in_im, pre = proj[:, 0:C], proj[:, C : 2 * C], proj[:, 2 * C : 3 * C]
            rate = lower + (1.0 - lower) * sigmoid(pre)
            r.keep[chip, c] = rate.reshape(2, R, C)
            r.drive[0, chip, c] = ((1.0 - rate) * in_re * sigmoid(in_re)).reshape(2, R, C)
            r.drive[1, chip, c] = ((1.0 - rate) * in_im * sigmoid(in_im)).reshape(2, R, C)
            scan_local(l, chip, c, turn_cos, turn_sin)

        gather_loop(e, full, ascending, project)
        r.segk[l] = r.seg[2]
        carry_over(l, False)
        for part in range(2):
            r.state[l, part, :, :, 0:SEGS, :] = r.cur[part]

        def mix(j):
            chip, c = chip_chunk(j, ascending, False)
            scan_final(l, chip, c, turn_cos, turn_sin)
            at = pl.ds(pl.multiple_of(SEGS + c * R, SEGS), R)
            s_re = flat(r.state[l, 0, chip, :, at, :])
            s_im = flat(r.state[l, 1, chip, :, at, :])
            centre = group_sum(s_re + s_im)
            d_re, d_im = s_re - centre, s_im - centre
            scale = lax.rsqrt(group_sum(d_re * d_re + d_im * d_im) + EPS_GROUP)
            u_re, u_im = d_re * scale, d_im * scale
            r.unit[l, 0, chip, c] = u_re.reshape(2, R, C)
            r.unit[l, 1, chip, c] = u_im.reshape(2, R, C)
            r.inv[l, chip, c] = scale.reshape(2, R, C)
            gate_re = flat(r.proj[l, chip, c, :, :, 3 * C : 4 * C])
            gate_im = flat(r.proj[l, chip, c, :, :, 4 * C : 5 * C])
            m_re = (u_re * gain_re * sigmoid(gate_re)).astype(BF16)
            m_im = (u_im * gain_im * sigmoid(gate_im)).astype(BF16)
            r.mixed[l, chip, c, :, :, 0:C] = m_re.reshape(2, R, C)
            r.mixed[l, chip, c, :, :, C : 2 * C] = m_im.reshape(2, R, C)
            r.psc[...] = mm(flat(r.mixed[l, chip, c]), r.wout[l]).reshape(2, R, D)

            @pl.when(j < N)
            def _():
                rs_other(e, c)

            @pl.when((j >= 1) & (j <= N))
            def _():
                rs_pass(e, j - 1)

            @pl.when(j >= N)
            def _():
                rs_own(e, c)

        loop(2 * N, mix)

        e2 = e + 1
        full2 = r.ffnfull.at[l]

        def send_ffn(c):
            s = r.st[l, 0, c] + rs_final(e, full, c)
            r.st[l, 1, c] = s
            full2[xi, c, core] = (s * norm_rows(s) * r.ngf[l, 1:2, :]).astype(BF16)
            ag_start(e2, full2, c)

        loop(N, send_ffn)

        @pl.when(l == 0)
        def _():
            for copy in w_copies:
                copy.wait()

        def feed(j):
            chip, c = chip_chunk(j, ascending, True)
            both = mm(flat(full2[chip, c]), r.wffn[l])
            r.gup[l, chip, c] = both.astype(BF16).reshape(2, R, 2 * F)
            gate, up = both[:, 0:F], both[:, F : 2 * F]
            hidden = (gate * sigmoid(gate) * up).astype(BF16)
            r.hidden[l, chip, c] = hidden.reshape(2, R, F)
            r.psc[...] = mm(hidden, r.dw[l]).reshape(2, R, D)

            @pl.when(j < N)
            def _():
                rs_own(e2, c)

            @pl.when(j >= N)
            def _():
                rs_other(e2, c)

            @pl.when(j > N)
            def _():
                rs_pass(e2, j - N - 1)

        gather_loop(e2, full2, ascending, feed)
        rs_pass(e2, N - 1)

    loop(L, forward_layer)

    def last_sum(c):
        e = 2 * L - 1
        r.st[L, 0, c] = r.st[L - 1, 1, c] + rs_final(e, r.ffnfull.at[L - 1], c)

    loop(N, last_sum)
    unperm = perm
    r.out[...] = mm_tn(unperm, r.st[L, 0].reshape(tokens, D).astype(BF16)).astype(BF16)

    def norm_back(l, which, c, grad_out):
        s = r.st[l, which, c]
        scale = norm_rows(s)
        r.gacc[l, which] += fold(grad_out * s * scale)
        scaled = grad_out * r.ngf[l, which : which + 1, :]
        back = scale * scaled - s * (scale * scale * scale) * jnp.mean(
            scaled * s, axis=-1, keepdims=True
        )
        r.grad[c] = r.grad[c] + back

    def backward_layer(step):
        l = L - 1 - step
        e = 2 * L + 2 * step
        full = r.gfull.at[l, 0]

        def send_ffn(j):
            c = descending(j)

            @pl.when(step > 0)
            def _():
                norm_back(l + 1, 0, c, rs_final(e - 1, r.gfull.at[l + 1, 1], c))

            full[xi, c, core] = r.grad[c].astype(BF16)
            ag_start(e, full, c)

        loop(N, send_ffn)

        def feed_back(j):
            chip, c = chip_chunk(j, descending, True)
            g_hidden = mm_nt(flat(full[chip, c]), r.dw[l])
            both = flat(r.gup[l, chip, c]).astype(F32)
            gate, up = both[:, 0:F], both[:, F : 2 * F]
            s = sigmoid(gate)
            g_gate = (g_hidden * up * s * (1.0 + gate * (1.0 - s))).astype(BF16)
            g_up = (g_hidden * gate * s).astype(BF16)
            r.dgu[chip, c, :, :, 0:F] = g_gate.reshape(2, R, F)
            r.dgu[chip, c, :, :, F : 2 * F] = g_up.reshape(2, R, F)
            r.psc[...] = mm_nt(flat(r.dgu[chip, c]), r.wffn[l]).reshape(2, R, D)

            @pl.when(j < N)
            def _():
                rs_own(e, c)

            @pl.when(j >= N)
            def _():
                rs_other(e, c)

            @pl.when(j > N)
            def _():
                rs_pass(e, descending(j - N - 1))

        gather_loop(e, full, descending, feed_back)
        rs_pass(e, 0)

        def down_tile(i):
            cols = pl.ds(pl.multiple_of(i * LANES, LANES), LANES)
            r.gdown[l, cols, :] = mm_tn(flat(r.hidden[l, :, :, :, :, cols]), flat(full[...])).astype(BF16)

        loop(F // LANES, down_tile)

        def ffn_tile(i):
            cols = pl.ds(pl.multiple_of(i * LANES, LANES), LANES)
            r.gffn[l, cols, :] = mm_tn(flat(r.ffnfull[l, :, :, :, :, cols]), flat(r.dgu[...])).astype(BF16)

        loop(D // LANES, ffn_tile)

        turn_cos, turn_sin, lower = r.par[l, 0:1, :], r.par[l, 1:2, :], r.par[l, 2:3, :]
        gain_re, gain_im = r.par[l, 3:4, :], r.par[l, 4:5, :]
        e2 = e + 1
        full2 = r.gfull.at[l, 1]

        def send_mix(j):
            c = descending(j)
            norm_back(l, 1, c, rs_final(e, full, c))
            full2[xi, c, core] = r.grad[c].astype(BF16)
            ag_start(e2, full2, c)

        loop(N, send_mix)
        r.seg[0:2] = jnp.zeros((2, 2, 2, SEGS, C), F32)

        def mix_back(j):
            chip, c = chip_chunk(j, descending, True)
            g_both = mm_nt(flat(full2[chip, c]), r.wout[l])
            g_re, g_im = g_both[:, 0:C], g_both[:, C : 2 * C]
            s_re = sigmoid(flat(r.proj[l, chip, c, :, :, 3 * C : 4 * C]))
            s_im = sigmoid(flat(r.proj[l, chip, c, :, :, 4 * C : 5 * C]))
            u_re, u_im = flat(r.unit[l, 0, chip, c]), flat(r.unit[l, 1, chip, c])
            n_re, n_im = g_re * s_re, g_im * s_im
            r.sacc[l, 0] += fold(n_re * u_re)
            r.sacc[l, 1] += fold(n_im * u_im)
            x_re, x_im = n_re * gain_re, n_im * gain_im
            cross_re, cross_im = x_re * u_re, x_im * u_im
            r.dproj[chip, c, :, :, 3 * C : 4 * C] = (cross_re * (1.0 - s_re)).astype(BF16).reshape(2, R, C)
            r.dproj[chip, c, :, :, 4 * C : 5 * C] = (cross_im * (1.0 - s_im)).astype(BF16).reshape(2, R, C)
            mean_one = group_sum(x_re + x_im)
            mean_two = group_sum(cross_re + cross_im)
            scale = flat(r.inv[l, chip, c])
            r.drive[0, chip, c] = (scale * (x_re - mean_one - u_re * mean_two)).reshape(2, R, C)
            r.drive[1, chip, c] = (scale * (x_im - mean_one - u_im * mean_two)).reshape(2, R, C)
            pre = flat(r.proj[l, chip, c, :, :, 2 * C : 3 * C])
            r.keep[chip, c] = (lower + (1.0 - lower) * sigmoid(pre)).reshape(2, R, C)
            scan_back_local(l, chip, c, turn_cos, turn_sin)

        gather_loop(e2, full2, descending, mix_back)
        carry_over(l, True)

        def scan_back(j):
            chip, c = chip_chunk(j, descending, False)
            scan_back_final(l, chip, c, turn_cos, turn_sin)
            t_re, t_im = flat(r.tot[0]), flat(r.tot[1])
            at = pl.ds(pl.multiple_of(c * R, SEGS), R)
            p_re = flat(r.state[l, 0, chip, :, at, :])
            p_im = flat(r.state[l, 1, chip, :, at, :])
            in_re = flat(r.proj[l, chip, c, :, :, 0:C])
            in_im = flat(r.proj[l, chip, c, :, :, C : 2 * C])
            fs = sigmoid(flat(r.proj[l, chip, c, :, :, 2 * C : 3 * C]))
            rate = lower + (1.0 - lower) * fs
            s_re, s_im = sigmoid(in_re), sigmoid(in_im)
            gc_re = t_re * p_re + t_im * p_im
            gc_im = t_im * p_re - t_re * p_im
            g_keep = gc_re * turn_cos + gc_im * turn_sin - (t_re * in_re * s_re + t_im * in_im * s_im)
            r.sacc[l, 2] += fold(rate * (gc_im * turn_cos - gc_re * turn_sin))
            r.sacc[l, 3] += fold(g_keep * (1.0 - fs))
            d_re = t_re * (1.0 - rate) * s_re * (1.0 + in_re * (1.0 - s_re))
            d_im = t_im * (1.0 - rate) * s_im * (1.0 + in_im * (1.0 - s_im))
            d_f = g_keep * (1.0 - lower) * fs * (1.0 - fs)
            r.dproj[chip, c, :, :, 0:C] = d_re.astype(BF16).reshape(2, R, C)
            r.dproj[chip, c, :, :, C : 2 * C] = d_im.astype(BF16).reshape(2, R, C)
            r.dproj[chip, c, :, :, 2 * C : 3 * C] = d_f.astype(BF16).reshape(2, R, C)
            r.psc[...] = mm_nt(flat(r.dproj[chip, c]), r.wmix[l]).reshape(2, R, D)

            @pl.when(j < N)
            def _():
                rs_other(e2, c)

            @pl.when((j >= 1) & (j <= N))
            def _():
                rs_pass(e2, descending(j - 1))

            @pl.when(j >= N)
            def _():
                rs_own(e2, c)

        loop(2 * N, scan_back)

        def out_tile(i):
            cols = pl.ds(pl.multiple_of(i * LANES, LANES), LANES)
            r.gout[l, cols, :] = mm_tn(flat(r.mixed[l, :, :, :, :, cols]), flat(full2[...])).astype(BF16)

        loop(2 * C // LANES, out_tile)

        def mix_tile(i):
            cols = pl.ds(pl.multiple_of(i * LANES, LANES), LANES)
            r.gmix[l, cols, :] = mm_tn(flat(r.mixfull[l, :, :, :, :, cols]), flat(r.dproj[...])).astype(BF16)

        loop(D // LANES, mix_tile)

    loop(L, backward_layer)

    def last_grad(j):
        c = descending(j)
        norm_back(0, 0, c, rs_final(4 * L - 1, r.gfull.at[0, 1], c))

    loop(N, last_grad)
    r.ig[...] = mm_tn(perm, r.grad[...].reshape(tokens, D).astype(BF16)).astype(BF16)
    for l in range(L):
        for which in range(2):
            r.gains[2 * l + which : 2 * l + which + 1, :] = jnp.sum(r.gacc[l, which], axis=0, keepdims=True)
        for k in range(4):
            value = jnp.sum(r.sacc[l, k], axis=0, keepdims=True)
            if k == 3:
                lower = r.par[l, 2:3, :]
                value = value * lower * (1.0 - lower)
            r.small[4 * l + k : 4 * l + k + 1, :] = value


def local(*args):
    x, ct, ng, inw, fw, gw, ow, ph, bl, gg, ffw, dw = args
    L, D = ng.shape[0], ng.shape[2]
    ch = fw.shape[2]
    F = dw.shape[1]
    C = -(-ch // LANES) * LANES
    z = types.SimpleNamespace(L=L, D=D, C=C, F=F, ch=ch, R=x.shape[0] // CHUNKS, single_side=False)
    names, scratch = scratch_of(z)
    vmem = pl.BlockSpec(memory_space=pltpu.VMEM)
    in_specs = [vmem] * 12
    in_specs[10] = pl.BlockSpec(memory_space=pl.ANY)
    shape = jax.ShapeDtypeStruct
    out, ig, gffn, gdown, gmix, gout, small, gains = pl.pallas_call(
        functools.partial(mega, z, names),
        out_shape=(
            shape(x.shape, BF16),
            shape(x.shape, BF16),
            shape((L, D, 2 * F), BF16),
            shape((L, F, D), BF16),
            shape((L, D, 5 * C), BF16),
            shape((L, 2 * C, D), BF16),
            shape((4 * L, C), F32),
            shape((2 * L, D), F32),
        ),
        in_specs=in_specs,
        out_specs=[vmem] * 8,
        scratch_shapes=scratch,
        compiler_params=pltpu.CompilerParams(
            collective_id=0, has_side_effects=True, vmem_limit_bytes=VMEM_BYTES
        ),
        name="layers",
    )(x, ct, ng, inw, fw, gw, ow, ph, bl, gg, ffw, dw)

    gffn, gdown, gmix, gout, small = lax.psum((gffn, gdown, gmix, gout, small), "dp")
    gains = lax.psum(gains, ("dp", "tensor")).reshape(L, 2, D)
    piece = D // lax.axis_size("tensor")
    gains = lax.dynamic_slice_in_dim(gains, lax.axis_index("tensor") * piece, piece, 2)
    gmix = gmix.astype(F32).reshape(L, D, 5, C)[..., :ch]
    small = small.reshape(L, 4, C)[..., :ch]
    return (
        out,
        ig,
        gains,
        jnp.stack([gmix[:, :, 0], gmix[:, :, 1]], axis=1),
        gmix[:, :, 2],
        jnp.stack([gmix[:, :, 3], gmix[:, :, 4]], axis=1),
        gout.astype(F32).reshape(L, 2, C, D)[:, :, :ch],
        small[:, 2],
        small[:, 3],
        small[:, 0:2],
        jnp.stack([gffn[:, :, :F], gffn[:, :, F:]], axis=1).astype(F32),
        gdown.astype(F32),
    )


def solution(mesh):
    tokens = P(("dp", "tensor"), None)
    return jax.shard_map(
        local,
        mesh=mesh,
        in_specs=(
            tokens,
            tokens,
            P(),
            P(None, None, None, "tensor"),
            P(None, None, "tensor"),
            P(None, None, None, "tensor"),
            P(None, None, "tensor", None),
            P(None, "tensor"),
            P(None, "tensor"),
            P(None, None, "tensor"),
            P(None, None, None, "tensor"),
            P(None, "tensor", None),
        ),
        out_specs=(
            tokens,
            tokens,
            P(None, None, "tensor"),
            P(None, None, None, "tensor"),
            P(None, None, "tensor"),
            P(None, None, None, "tensor"),
            P(None, None, "tensor", None),
            P(None, "tensor"),
            P(None, "tensor"),
            P(None, None, "tensor"),
            P(None, None, None, "tensor"),
            P(None, "tensor", None),
        ),
        check_vma=False,
    )
```

```python
import functools
import types

import jax
import jax.numpy as jnp
from jax import lax
from jax.experimental import pallas as pl
from jax.experimental.pallas import tpu as pltpu
from jax.sharding import PartitionSpec as P

MESH = pl.DeviceIdType.MESH
F32 = jnp.float32
BF16 = jnp.bfloat16

GROUP_CH = 48
EPS_NORM = 1e-06
EPS_GROUP = 1e-05
LANES = 128
SEGS = 8
CHUNKS = 4
VMEM_BYTES = 63 * 1024 * 1024


def sigmoid(v):
    return 0.5 * jnp.tanh(0.5 * v) + 0.5


def mm(left, right):
    return jnp.dot(left, right, preferred_element_type=F32)


def mm_nt(left, right):
    return lax.dot_general(left, right, (((1,), (1,)), ((), ())), preferred_element_type=F32)


def mm_tn(left, right):
    return lax.dot_general(left, right, (((0,), (0,)), ((), ())), preferred_element_type=F32)


def loop(count, body):
    def step(index, carry):
        body(index)
        return carry

    lax.fori_loop(0, count, step, 0)


def iota(shape, dim):
    return lax.broadcasted_iota(jnp.int32, shape, dim)


def scratch_of(z):
    L, D, C, F, R, N = z.L, z.D, z.C, z.F, z.R, CHUNKS
    rows = (2, N, 2, R)
    own = (N, R)
    bufs = dict(
        wmix=((L, 5 * C, D), BF16),
        wout=((L, 2 * C, D), BF16),
        wffn=((L, D, 2 * F), BF16),
        par=((L, 8, C), F32),
        ngf=((L, 2, D), F32),
        gsum=((C, C), BF16),
        st=((2 * L + 1, *own, D), F32),
        mixfull=((L, *rows, D), BF16),
        ffnfull=((L, *rows, D), BF16),
        gfull=((2, *rows, D), BF16),
        proj=((L, *rows, 5 * C), F32),
        state=((L, 2, 2, 2, SEGS + N * R, C), F32),
        unit=((L, 2, *rows, C), F32),
        inv=((L, *rows, C), F32),
        mixed=((L, *rows, 2 * C), BF16),
        gup=((L, *rows, 2 * F), BF16),
        hidden=((L, *rows, F), BF16),
        keep=((*rows, C), F32),
        drive=((2, *rows, C), F32),
        seg=((3, 2, 2, SEGS, C), F32),
        segk=((L, 2, 2, SEGS, C), F32),
        cur=((2, 2, 2, SEGS, C), F32),
        tot=((2, 2, R, C), F32),
        dgu=((*rows, 2 * F), BF16),
        dproj=((*rows, 5 * C), BF16),
        psc=((2, R, D), F32),
        xpart=((*own, D), F32),
        opart=((*own, D), F32),
        grad=((*own, D), F32),
        stage=((3, *own, D), BF16),
        land=((2, 3, *own, D), BF16),
        gacc=((L, 2, SEGS, D), F32),
        sacc=((L, 4, SEGS, C), F32),
        wdown=((L, F, D), BF16),
        swork=((2 * SEGS, D), F32),
        sland=((5, 2 * SEGS, D), F32),
    )
    if z.reduce:
        unit = (z.units * L, z.blk, D)
        bufs.update(yland=(unit, BF16), zland=(unit, BF16), mland=(unit, BF16))
    sems = dict(
        ags=(4 * L, 3, N),
        agr=(4 * L, 3, N),
        rss=(4 * L, 3, N),
        rsr=(4 * L, 3, N),
        wsem=(L, 10),
        ss=(5,),
        sr=(5,),
    )
    if z.reduce:
        sems.update(us=(z.units * L, 5), ur=(z.units * L, 5))
    names = list(bufs) + list(sems)
    shapes = [pltpu.VMEM(s, d) for s, d in bufs.values()]
    shapes += [pltpu.SemaphoreType.DMA(s) for s in sems.values()]
    names.append("freed")
    shapes.append(pltpu.SemaphoreType.REGULAR)
    return names, shapes


IN_NAMES = ("x", "ct", "ng", "inw", "fw", "gw", "ow", "ph", "bl", "gg", "ffw", "dw")
OUT_NAMES = ("out", "ig", "wg", "sums")


def mega(z, names, *refs):
    r = types.SimpleNamespace(**dict(zip(IN_NAMES + OUT_NAMES + tuple(names), refs)))
    L, D, C, F, R, N = z.L, z.D, z.C, z.F, z.R, CHUNKS
    ch = z.ch
    Q = R // SEGS
    dp = lax.axis_index("dp")
    me = lax.axis_index("tensor")
    core = lax.rem(me, 2)
    xi = me // 2
    other = 1 - xi
    sib = xi * 2 + 1 - core
    xnb = other * 2 + core

    inner = lax.rem(dp, 8)
    base = dp - inner
    y = lax.rem(inner, 2)
    line = inner // 2
    middle = (line == 1) | (line == 2)

    def on_line(place, row):
        return (base + 2 * place + row, me)

    y_peer = on_line(line, 1 - y)
    pair_peer = on_line(line + 1 - 2 * lax.rem(line, 2), y)
    cross_peer = on_line(3 - line, y)

    peers = [(dp, sib), (dp, xnb)]
    if z.reduce:
        peers += [y_peer, pair_peer, cross_peer]
    barrier = pltpu.get_barrier_semaphore()
    for peer in peers:
        pl.semaphore_signal(barrier, inc=1, device_id=peer, device_id_type=MESH)
    pl.semaphore_wait(barrier, len(peers))

    def remote(src, dst, send, recv, peer):
        return pltpu.make_async_remote_copy(
            src_ref=src,
            dst_ref=dst,
            send_sem=send,
            recv_sem=recv,
            device_id=peer if isinstance(peer, tuple) else (dp, peer),
            device_id_type=MESH,
        )

    def unit_of(u):
        return L - 1 - u // z.units, lax.rem(u, z.units)

    def unit_copy(u, stage):
        l, k = unit_of(u)
        mine = r.wg.at[l, k, y]
        src, dst, peer = (
            (r.wg.at[l, k, 1 - y], r.yland.at[u], y_peer),
            (mine, r.zland.at[u], pair_peer),
            (mine, r.mland.at[u], cross_peer),
            (mine, r.zland.at[u], pair_peer),
            (mine, mine, y_peer),
        )[stage]
        return remote(src, dst, r.us.at[u, stage], r.ur.at[u, stage], peer)

    def unit_add(u, landed):
        l, k = unit_of(u)
        r.wg[l, k, y] = (r.wg[l, k, y].astype(F32) + landed[u].astype(F32)).astype(BF16)

    def unit_stage(u, stage):
        if stage == 0:
            unit_copy(u, 0).start()
        if stage == 1:
            unit_copy(u, 0).wait_send()
            pl.semaphore_signal(r.freed, inc=1, device_id=y_peer, device_id_type=MESH)
            unit_copy(u, 0).wait_recv()
            unit_add(u, r.yland)

            @pl.when(jnp.logical_not(middle))
            def _():
                unit_copy(u, 1).start()

        if stage == 2:

            @pl.when(middle)
            def _():
                unit_copy(u, 1).wait_recv()
                unit_add(u, r.zland)
                unit_copy(u, 2).start()

        if stage == 3:

            @pl.when(middle)
            def _():
                unit_copy(u, 2).wait_recv()
                unit_copy(u, 2).wait_send()
                unit_add(u, r.mland)
                unit_copy(u, 3).start()

        if stage == 4:

            @pl.when(jnp.logical_not(middle))
            def _():
                l, k = unit_of(u)
                unit_copy(u, 1).wait_send()
                unit_copy(u, 3).wait_recv()
                r.wg[l, k, y] = r.zland[u]

            pl.semaphore_wait(r.freed, 1)
            unit_copy(u, 4).start()
        if stage == 5:
            l, k = unit_of(u)
            theirs = r.wg.at[l, k, 1 - y]
            remote(theirs, theirs, r.us.at[u, 4], r.ur.at[u, 4], y_peer).wait_recv()
            unit_copy(u, 4).wait_send()

            @pl.when(middle)
            def _():
                unit_copy(u, 3).wait_send()

    def tick(m):
        if not z.reduce:
            return
        for stage in reversed(range(6)):
            u = m - stage

            @pl.when((u >= 0) & (u < z.units * L))
            def _():
                unit_stage(u, stage)

    def ag_copy(e, full, c, kind):
        chip = other if kind == 2 else xi
        peer = xnb if kind == 0 else sib
        ref = full.at[chip, c, core]
        return remote(ref, ref, r.ags.at[e, kind, c], r.agr.at[e, kind, c], peer)

    def ag_landing(e, full, c, kind):
        chip = xi if kind == 1 else other
        col = core if kind == 0 else 1 - core
        ref = full.at[chip, c, col]
        return remote(ref, ref, r.ags.at[e, kind, c], r.agr.at[e, kind, c], sib)

    def ag_start(e, full, c):
        ag_copy(e, full, c, 0).start()
        ag_copy(e, full, c, 1).start()

    def ag_take_x(e, full, c):
        ag_landing(e, full, c, 0).wait_recv()
        ag_copy(e, full, c, 2).start()

    def rs_copy(e, c, kind):
        return remote(
            r.stage.at[kind, c],
            r.land.at[r_side(e), kind, c],
            r.rss.at[e, kind, c],
            r.rsr.at[e, kind, c],
            xnb if kind == 1 else sib,
        )

    def r_side(e):
        return e // (2 * L)

    def rs_other(e, c):
        r.stage[0, c] = r.psc[1 - core].astype(BF16)
        rs_copy(e, c, 0).start()
        r.xpart[c] = r.psc[core]

    def rs_pass(e, c):
        rs_copy(e, c, 0).wait_recv()
        r.stage[1, c] = (r.xpart[c] + r.land[r_side(e), 0, c].astype(F32)).astype(BF16)
        rs_copy(e, c, 1).start()

    def rs_own(e, c):
        r.stage[2, c] = r.psc[1 - core].astype(BF16)
        rs_copy(e, c, 2).start()
        r.opart[c] = r.psc[core]

    def rs_final(e, full, c):
        rs_copy(e, c, 2).wait_recv()
        rs_copy(e, c, 1).wait_recv()
        side = r_side(e)
        total = r.opart[c] + r.land[side, 2, c].astype(F32) + r.land[side, 1, c].astype(F32)
        for kind in range(3):
            rs_copy(e, c, kind).wait_send()
            ag_copy(e, full, c, kind).wait_send()
        return total

    def gather_loop(e, full, order, stage):
        def step(j):
            @pl.when(j < N)
            def _():
                ag_landing(e, full, order(j), 1).wait_recv()

            @pl.when((j >= N - 1) & (j < 2 * N - 1))
            def _():
                ag_take_x(e, full, order(j - N + 1))

            @pl.when(j >= N)
            def _():
                ag_landing(e, full, order(j - N), 2).wait_recv()

            stage(j)

        loop(2 * N, step)

    def chip_chunk(j, order, own_first):
        first = j < N
        chunk = order(jnp.where(first, j, j - N))
        if own_first:
            return jnp.where(first, xi, other), chunk
        return jnp.where(first, other, xi), chunk

    ascending = lambda j: j
    descending = lambda j: N - 1 - j

    def norm_rows(s):
        return lax.rsqrt(jnp.mean(s * s, axis=-1, keepdims=True) + EPS_NORM)

    def group_sum(v):
        high = v.astype(BF16)
        rest = (v - high.astype(F32)).astype(BF16)
        weight = r.gsum[...]
        return (mm(high, weight) + mm(rest, weight)) * (1.0 / (2 * GROUP_CH))

    def fold(v):
        return jnp.sum(v.reshape(v.shape[0] // SEGS, SEGS, v.shape[1]), axis=0)

    def flat(v):
        return v.reshape(-1, v.shape[-1])

    r.wmix[...] = jnp.zeros_like(r.wmix)
    r.wout[...] = jnp.zeros_like(r.wout)
    w_copies = []
    for l in range(L):
        parts = (r.inw.at[l, 0], r.inw.at[l, 1], r.fw.at[l], r.gw.at[l, 0], r.gw.at[l, 1])
        pairs = [(part, r.wmix.at[l, pl.ds(k * C, ch), :]) for k, part in enumerate(parts)]
        pairs += [(r.ow.at[l, k], r.wout.at[l, pl.ds(k * C, ch), :]) for k in range(2)]
        pairs += [(r.ffw.at[l, k], r.wffn.at[l, :, pl.ds(k * F, F)]) for k in range(2)]
        pairs += [(r.dw.at[l], r.wdown.at[l])]
        w_copies += [
            pltpu.make_async_copy(src, dst, r.wsem.at[l, k]) for k, (src, dst) in enumerate(pairs)
        ]
    for copy in w_copies:
        copy.start()

    tokens = N * R
    width = tokens // SEGS
    row = iota((tokens, tokens), 0)
    col = iota((tokens, tokens), 1)
    place = lax.rem(row, SEGS) * width + row // SEGS
    perm = jnp.where(col == place, 1.0, 0.0).astype(BF16)
    r.st[0] = mm(perm, r.x[...]).reshape(N, R, D)
    r.grad[...] = mm(perm, r.ct[...]).reshape(N, R, D)

    r.ngf[...] = r.ng[...].astype(F32)
    r.par[...] = jnp.zeros_like(r.par)
    r.gacc[...] = jnp.zeros_like(r.gacc)
    r.wg[:, z.units - 1, 1] = jnp.zeros((L, z.blk, D), BF16)
    r.sacc[...] = jnp.zeros_like(r.sacc)
    for l in range(L):
        angle = r.ph[l : l + 1, :]
        turn_cos, turn_sin = jnp.cos(angle), jnp.sin(angle)
        r.par[l, 0:1, 0:ch] = turn_cos
        r.par[l, 1:2, 0:ch] = turn_sin
        r.par[l, 2:3, 0:ch] = sigmoid(r.bl[l : l + 1, :])
        r.par[l, 3:4, 0:ch] = r.gg[l, 0:1, :].astype(F32)
        r.par[l, 4:5, 0:ch] = r.gg[l, 1:2, :].astype(F32)
        for _ in range(width.bit_length() - 1):
            turn_cos, turn_sin = (
                turn_cos * turn_cos - turn_sin * turn_sin,
                2.0 * turn_cos * turn_sin,
            )
        r.par[l, 5:6, 0:ch] = turn_cos
        r.par[l, 6:7, 0:ch] = turn_sin
    gi, gj = iota((C, C), 0), iota((C, C), 1)
    same = (gi // GROUP_CH == gj // GROUP_CH) & (gi < ch) & (gj < ch)
    r.gsum[...] = jnp.where(same, 1.0, 0.0).astype(BF16)

    def rows_of(q):
        return slice(q * SEGS, (q + 1) * SEGS)

    def scan_local(l, chip, c, turn_cos, turn_sin):
        for k in range(2):
            h_re, h_im, prod = r.seg[0, chip, k], r.seg[1, chip, k], r.seg[2, chip, k]
            for q in range(Q):
                rate = r.keep[chip, c, k, rows_of(q), :]
                h_re, h_im = (
                    rate * (turn_cos * h_re - turn_sin * h_im) + r.drive[0, chip, c, k, rows_of(q), :],
                    rate * (turn_cos * h_im + turn_sin * h_re) + r.drive[1, chip, c, k, rows_of(q), :],
                )
                prod = prod * rate
            r.seg[0, chip, k], r.seg[1, chip, k], r.seg[2, chip, k] = h_re, h_im, prod

    def scan_final(l, chip, c, turn_cos, turn_sin):
        base = SEGS + c * R
        for k in range(2):
            h_re, h_im = r.cur[0, chip, k], r.cur[1, chip, k]
            for q in range(Q):
                rate = r.keep[chip, c, k, rows_of(q), :]
                h_re, h_im = (
                    rate * (turn_cos * h_re - turn_sin * h_im) + r.drive[0, chip, c, k, rows_of(q), :],
                    rate * (turn_cos * h_im + turn_sin * h_re) + r.drive[1, chip, c, k, rows_of(q), :],
                )
                at = pl.ds(pl.multiple_of(base + q * SEGS, SEGS), SEGS)
                r.state[l, 0, chip, k, at, :] = h_re
                r.state[l, 1, chip, k, at, :] = h_im
            r.cur[0, chip, k], r.cur[1, chip, k] = h_re, h_im

    def scan_back_local(l, chip, c, turn_cos, turn_sin):
        for k in range(2):
            u_re, u_im = r.seg[0, chip, k], r.seg[1, chip, k]
            for q in reversed(range(Q)):
                rate = r.keep[chip, c, k, rows_of(q), :]
                t_re = r.drive[0, chip, c, k, rows_of(q), :] + u_re
                t_im = r.drive[1, chip, c, k, rows_of(q), :] + u_im
                u_re = rate * (turn_cos * t_re + turn_sin * t_im)
                u_im = rate * (turn_cos * t_im - turn_sin * t_re)
            r.seg[0, chip, k], r.seg[1, chip, k] = u_re, u_im

    def scan_back_final(l, chip, c, turn_cos, turn_sin):
        for k in range(2):
            u_re, u_im = r.cur[0, chip, k], r.cur[1, chip, k]
            for q in reversed(range(Q)):
                rate = r.keep[chip, c, k, rows_of(q), :]
                t_re = r.drive[0, chip, c, k, rows_of(q), :] + u_re
                t_im = r.drive[1, chip, c, k, rows_of(q), :] + u_im
                r.tot[0, k, rows_of(q), :] = t_re
                r.tot[1, k, rows_of(q), :] = t_im
                u_re = rate * (turn_cos * t_re + turn_sin * t_im)
                u_im = rate * (turn_cos * t_im - turn_sin * t_re)
            r.cur[0, chip, k], r.cur[1, chip, k] = u_re, u_im

    def carry_over(l, back):
        all_cos, all_sin = r.par[l, 5:6, :], r.par[l, 6:7, :]
        if back:
            all_sin = -all_sin
        c_re = jnp.zeros((1, C), F32)
        c_im = jnp.zeros((1, C), F32)
        order = [(chip, k, s) for chip in range(2) for k in range(2) for s in range(SEGS)]
        for chip, k, s in reversed(order) if back else order:
            one = slice(s, s + 1)
            r.cur[0, chip, k, one, :] = c_re
            r.cur[1, chip, k, one, :] = c_im
            prod = r.segk[l, chip, k, one, :]
            c_re, c_im = (
                prod * (all_cos * c_re - all_sin * c_im) + r.seg[0, chip, k, one, :],
                prod * (all_cos * c_im + all_sin * c_re) + r.seg[1, chip, k, one, :],
            )

    def forward_layer(l):
        turn_cos, turn_sin, lower = r.par[l, 0:1, :], r.par[l, 1:2, :], r.par[l, 2:3, :]
        gain_re, gain_im = r.par[l, 3:4, :], r.par[l, 4:5, :]
        e = 2 * l
        full = r.mixfull.at[l]

        def send_mix(c):
            @pl.when(l > 0)
            def _():
                r.st[2 * l, c] = r.st[2 * l - 1, c] + rs_final(e - 1, r.ffnfull.at[l - 1], c)

            s = r.st[2 * l, c]
            full[xi, c, core] = (s * norm_rows(s) * r.ngf[l, 0:1, :]).astype(BF16)
            ag_start(e, full, c)

        loop(N, send_mix)

        @pl.when(l == 0)
        def _():
            for copy in w_copies:
                copy.wait()

        r.seg[0:2] = jnp.zeros((2, 2, 2, SEGS, C), F32)
        r.seg[2] = jnp.ones((2, 2, SEGS, C), F32)

        def project(j):
            chip, c = chip_chunk(j, ascending, True)
            proj = mm_nt(flat(full[chip, c]), r.wmix[l])
            r.proj[l, chip, c] = proj.reshape(2, R, 5 * C)
            in_re, in_im, pre = proj[:, 0:C], proj[:, C : 2 * C], proj[:, 2 * C : 3 * C]
            rate = lower + (1.0 - lower) * sigmoid(pre)
            r.keep[chip, c] = rate.reshape(2, R, C)
            r.drive[0, chip, c] = ((1.0 - rate) * in_re * sigmoid(in_re)).reshape(2, R, C)
            r.drive[1, chip, c] = ((1.0 - rate) * in_im * sigmoid(in_im)).reshape(2, R, C)
            scan_local(l, chip, c, turn_cos, turn_sin)

        gather_loop(e, full, ascending, project)
        r.segk[l] = r.seg[2]
        carry_over(l, False)
        for part in range(2):
            r.state[l, part, :, :, 0:SEGS, :] = r.cur[part]

        def mix(j):
            chip, c = chip_chunk(j, ascending, False)
            scan_final(l, chip, c, turn_cos, turn_sin)
            at = pl.ds(pl.multiple_of(SEGS + c * R, SEGS), R)
            s_re = flat(r.state[l, 0, chip, :, at, :])
            s_im = flat(r.state[l, 1, chip, :, at, :])
            centre = group_sum(s_re + s_im)
            d_re, d_im = s_re - centre, s_im - centre
            scale = lax.rsqrt(group_sum(d_re * d_re + d_im * d_im) + EPS_GROUP)
            u_re, u_im = d_re * scale, d_im * scale
            r.unit[l, 0, chip, c] = u_re.reshape(2, R, C)
            r.unit[l, 1, chip, c] = u_im.reshape(2, R, C)
            r.inv[l, chip, c] = scale.reshape(2, R, C)
            gate_re = flat(r.proj[l, chip, c, :, :, 3 * C : 4 * C])
            gate_im = flat(r.proj[l, chip, c, :, :, 4 * C : 5 * C])
            m_re = (u_re * gain_re * sigmoid(gate_re)).astype(BF16)
            m_im = (u_im * gain_im * sigmoid(gate_im)).astype(BF16)
            r.mixed[l, chip, c, :, :, 0:C] = m_re.reshape(2, R, C)
            r.mixed[l, chip, c, :, :, C : 2 * C] = m_im.reshape(2, R, C)
            r.psc[...] = mm(flat(r.mixed[l, chip, c]), r.wout[l]).reshape(2, R, D)

            @pl.when(j < N)
            def _():
                rs_other(e, c)

            @pl.when((j >= 1) & (j <= N))
            def _():
                rs_pass(e, j - 1)

            @pl.when(j >= N)
            def _():
                rs_own(e, c)

        loop(2 * N, mix)

        e2 = e + 1
        full2 = r.ffnfull.at[l]

        def send_ffn(c):
            s = r.st[2 * l, c] + rs_final(e, full, c)
            r.st[2 * l + 1, c] = s
            full2[xi, c, core] = (s * norm_rows(s) * r.ngf[l, 1:2, :]).astype(BF16)
            ag_start(e2, full2, c)

        loop(N, send_ffn)

        def feed(j):
            chip, c = chip_chunk(j, ascending, True)
            both = mm(flat(full2[chip, c]), r.wffn[l])
            r.gup[l, chip, c] = both.astype(BF16).reshape(2, R, 2 * F)
            gate, up = both[:, 0:F], both[:, F : 2 * F]
            hidden = (gate * sigmoid(gate) * up).astype(BF16)
            r.hidden[l, chip, c] = hidden.reshape(2, R, F)
            r.psc[...] = mm(hidden, r.wdown[l]).reshape(2, R, D)

            @pl.when(j < N)
            def _():
                rs_own(e2, c)

            @pl.when(j >= N)
            def _():
                rs_other(e2, c)

            @pl.when(j > N)
            def _():
                rs_pass(e2, j - N - 1)

        gather_loop(e2, full2, ascending, feed)
        rs_pass(e2, N - 1)

    loop(L, forward_layer)

    def last_sum(c):
        e = 2 * L - 1
        r.st[2 * L, c] = r.st[2 * L - 1, c] + rs_final(e, r.ffnfull.at[L - 1], c)

    loop(N, last_sum)
    unperm = perm
    r.out[...] = mm_tn(unperm, r.st[2 * L].reshape(tokens, D).astype(BF16)).astype(BF16)

    def norm_back(l, which, c, grad_out):
        s = r.st[2 * l + which, c]
        scale = norm_rows(s)
        r.gacc[l, which] += fold(grad_out * s * scale)
        scaled = grad_out * r.ngf[l, which : which + 1, :]
        back = scale * scaled - s * (scale * scale * scale) * jnp.mean(
            scaled * s, axis=-1, keepdims=True
        )
        r.grad[c] = r.grad[c] + back

    def backward_layer(step):
        l = L - 1 - step
        e = 2 * L + 2 * step
        full = r.gfull.at[0]

        def send_ffn(j):
            c = descending(j)

            @pl.when(step > 0)
            def _():
                norm_back(l + 1, 0, c, rs_final(e - 1, r.gfull.at[1], c))

            full[xi, c, core] = r.grad[c].astype(BF16)
            ag_start(e, full, c)

        loop(N, send_ffn)

        @pl.when(step > 0)
        def _():
            tick((step - 1) * z.units + 7)

        def feed_back(j):
            chip, c = chip_chunk(j, descending, True)
            g_hidden = mm_nt(flat(full[chip, c]), r.wdown[l])
            both = flat(r.gup[l, chip, c]).astype(F32)
            gate, up = both[:, 0:F], both[:, F : 2 * F]
            s = sigmoid(gate)
            g_gate = (g_hidden * up * s * (1.0 + gate * (1.0 - s))).astype(BF16)
            g_up = (g_hidden * gate * s).astype(BF16)
            r.dgu[chip, c, :, :, 0:F] = g_gate.reshape(2, R, F)
            r.dgu[chip, c, :, :, F : 2 * F] = g_up.reshape(2, R, F)
            r.psc[...] = mm_nt(flat(r.dgu[chip, c]), r.wffn[l]).reshape(2, R, D)

            @pl.when(j < N)
            def _():
                rs_own(e, c)

            @pl.when(j >= N)
            def _():
                rs_other(e, c)

            @pl.when(j > N)
            def _():
                rs_pass(e, descending(j - N - 1))

            @pl.when((step > 0) & (lax.rem(j, N) == N // 2))
            def _():
                tick((step - 1) * z.units + 8 + j // N)

        gather_loop(e, full, descending, feed_back)
        rs_pass(e, 0)

        def ffn_tile(i):
            cols = pl.ds(pl.multiple_of(i * F, LANES), F)

            @pl.when(i == 0)
            def _():
                part = mm_tn(flat(r.hidden[l]), flat(full[...])).astype(BF16)
                r.wg[l, 0 : z.fu] = part.reshape(z.fu, 2, z.blk, D)

            @pl.when(i > 0)
            def _():
                cols = pl.ds(pl.multiple_of((i - 1) * F, LANES), F)
                part = mm_tn(flat(r.ffnfull[l, :, :, :, :, cols]), flat(r.dgu[...])).astype(BF16)
                r.wg[l, pl.ds(i * z.fu, z.fu)] = part.reshape(z.fu, 2, z.blk, D)

        loop(1 + D // F, ffn_tile)
        first_tick = step * z.units
        tick(first_tick)

        turn_cos, turn_sin, lower = r.par[l, 0:1, :], r.par[l, 1:2, :], r.par[l, 2:3, :]
        gain_re, gain_im = r.par[l, 3:4, :], r.par[l, 4:5, :]
        e2 = e + 1
        full2 = r.gfull.at[1]

        def send_mix(j):
            c = descending(j)
            norm_back(l, 1, c, rs_final(e, full, c))
            full2[xi, c, core] = r.grad[c].astype(BF16)
            ag_start(e2, full2, c)

        loop(N, send_mix)
        tick(first_tick + 1)
        r.seg[0:2] = jnp.zeros((2, 2, 2, SEGS, C), F32)

        def mix_back(j):
            chip, c = chip_chunk(j, descending, True)
            g_both = mm_nt(flat(full2[chip, c]), r.wout[l])
            g_re, g_im = g_both[:, 0:C], g_both[:, C : 2 * C]
            s_re = sigmoid(flat(r.proj[l, chip, c, :, :, 3 * C : 4 * C]))
            s_im = sigmoid(flat(r.proj[l, chip, c, :, :, 4 * C : 5 * C]))
            u_re, u_im = flat(r.unit[l, 0, chip, c]), flat(r.unit[l, 1, chip, c])
            n_re, n_im = g_re * s_re, g_im * s_im
            r.sacc[l, 0] += fold(n_re * u_re)
            r.sacc[l, 1] += fold(n_im * u_im)
            x_re, x_im = n_re * gain_re, n_im * gain_im
            cross_re, cross_im = x_re * u_re, x_im * u_im
            r.dproj[chip, c, :, :, 3 * C : 4 * C] = (cross_re * (1.0 - s_re)).astype(BF16).reshape(2, R, C)
            r.dproj[chip, c, :, :, 4 * C : 5 * C] = (cross_im * (1.0 - s_im)).astype(BF16).reshape(2, R, C)
            mean_one = group_sum(x_re + x_im)
            mean_two = group_sum(cross_re + cross_im)
            scale = flat(r.inv[l, chip, c])
            r.drive[0, chip, c] = (scale * (x_re - mean_one - u_re * mean_two)).reshape(2, R, C)
            r.drive[1, chip, c] = (scale * (x_im - mean_one - u_im * mean_two)).reshape(2, R, C)
            pre = flat(r.proj[l, chip, c, :, :, 2 * C : 3 * C])
            r.keep[chip, c] = (lower + (1.0 - lower) * sigmoid(pre)).reshape(2, R, C)
            scan_back_local(l, chip, c, turn_cos, turn_sin)

            @pl.when(lax.rem(j, N) == N // 2)
            def _():
                tick(first_tick + 2 + j // N)

        gather_loop(e2, full2, descending, mix_back)
        carry_over(l, True)

        def scan_back(j):
            chip, c = chip_chunk(j, descending, False)
            scan_back_final(l, chip, c, turn_cos, turn_sin)
            t_re, t_im = flat(r.tot[0]), flat(r.tot[1])
            at = pl.ds(pl.multiple_of(c * R, SEGS), R)
            p_re = flat(r.state[l, 0, chip, :, at, :])
            p_im = flat(r.state[l, 1, chip, :, at, :])
            in_re = flat(r.proj[l, chip, c, :, :, 0:C])
            in_im = flat(r.proj[l, chip, c, :, :, C : 2 * C])
            fs = sigmoid(flat(r.proj[l, chip, c, :, :, 2 * C : 3 * C]))
            rate = lower + (1.0 - lower) * fs
            s_re, s_im = sigmoid(in_re), sigmoid(in_im)
            gc_re = t_re * p_re + t_im * p_im
            gc_im = t_im * p_re - t_re * p_im
            g_keep = gc_re * turn_cos + gc_im * turn_sin - (t_re * in_re * s_re + t_im * in_im * s_im)
            r.sacc[l, 2] += fold(rate * (gc_im * turn_cos - gc_re * turn_sin))
            r.sacc[l, 3] += fold(g_keep * (1.0 - fs))
            d_re = t_re * (1.0 - rate) * s_re * (1.0 + in_re * (1.0 - s_re))
            d_im = t_im * (1.0 - rate) * s_im * (1.0 + in_im * (1.0 - s_im))
            d_f = g_keep * (1.0 - lower) * fs * (1.0 - fs)
            r.dproj[chip, c, :, :, 0:C] = d_re.astype(BF16).reshape(2, R, C)
            r.dproj[chip, c, :, :, C : 2 * C] = d_im.astype(BF16).reshape(2, R, C)
            r.dproj[chip, c, :, :, 2 * C : 3 * C] = d_f.astype(BF16).reshape(2, R, C)
            r.psc[...] = mm(flat(r.dproj[chip, c]), r.wmix[l]).reshape(2, R, D)

            @pl.when(j < N)
            def _():
                rs_other(e2, c)

            @pl.when((j >= 1) & (j <= N))
            def _():
                rs_pass(e2, descending(j - 1))

            @pl.when(j >= N)
            def _():
                rs_own(e2, c)

            @pl.when(lax.rem(j, N) == N // 2)
            def _():
                tick(first_tick + 4 + j // N)

        loop(2 * N, scan_back)

        base_unit = z.units - 4

        def out_tile(i):
            cols = pl.ds(pl.multiple_of(i * C, LANES), C)
            part = mm_tn(flat(r.mixed[l, :, :, :, :, cols]), flat(full2[...])).astype(BF16)
            r.wg[l, base_unit, i] = part[0:ch]

        loop(2, out_tile)

        def mix_tile(i):
            k = lax.rem(i + 3, 5)
            cols = pl.ds(pl.multiple_of(k * C, LANES), C)
            part = mm_tn(flat(r.dproj[:, :, :, :, cols]), flat(r.mixfull[l])).astype(BF16)
            r.wg[l, base_unit + 1 + i // 2, lax.rem(i, 2)] = part[0:ch]

        loop(5, mix_tile)
        tick(first_tick + 6)

    loop(L, backward_layer)

    def last_grad(j):
        c = descending(j)
        norm_back(0, 0, c, rs_final(4 * L - 1, r.gfull.at[1], c))

    loop(N, last_grad)
    r.ig[...] = mm_tn(perm, r.grad[...].reshape(tokens, D).astype(BF16)).astype(BF16)

    r.swork[...] = jnp.zeros_like(r.swork)
    for l in range(L):
        for which in range(2):
            at = 2 * l + which
            r.swork[at : at + 1, :] = jnp.sum(r.gacc[l, which], axis=0, keepdims=True)

    def swap_sum(k, peer, first):
        copy = remote(r.swork, r.sland.at[k], r.ss.at[k], r.sr.at[k], peer)
        copy.start()
        copy.wait()
        r.swork[...] = r.swork[...] + r.sland[k]

    swap_sum(0, sib, True)
    swap_sum(1, xnb, True)
    for l in range(L):
        for k in range(4):
            value = jnp.sum(r.sacc[l, k], axis=0, keepdims=True)
            if k == 3:
                lower = r.par[l, 2:3, :]
                value = value * lower * (1.0 - lower)
            at = 2 * L + 4 * l + k
            r.swork[at : at + 1, 0:C] = value
    if z.reduce:
        swap_sum(2, y_peer, False)
        swap_sum(3, pair_peer, False)
        swap_sum(4, cross_peer, False)
        start = (L - 1) * z.units + 7

        def drain(i):
            tick(start + i)

        loop(z.units + 5 - 7, drain)
    r.sums[...] = r.swork[...]


def local(*args):
    x, ct, ng, inw, fw, gw, ow, ph, bl, gg, ffw, dw = args
    L, D = ng.shape[0], ng.shape[2]
    ch = fw.shape[2]
    F = dw.shape[1]
    C = -(-ch // LANES) * LANES
    n_dp = lax.axis_size("dp")
    reduce = n_dp % 8 == 0
    fu = F // (2 * ch)
    units = fu * (1 + D // F) + 4
    z = types.SimpleNamespace(
        L=L, D=D, C=C, F=F, ch=ch, R=x.shape[0] // CHUNKS, reduce=reduce, blk=ch, fu=fu, units=units
    )
    names, scratch = scratch_of(z)
    vmem = pl.BlockSpec(memory_space=pltpu.VMEM)
    in_specs = [vmem] * 12
    for k in (3, 4, 5, 6, 10, 11):
        in_specs[k] = pl.BlockSpec(memory_space=pl.ANY)
    shape = jax.ShapeDtypeStruct
    out, ig, wg, sums = pl.pallas_call(
        functools.partial(mega, z, names),
        out_shape=(
            shape(x.shape, BF16),
            shape(x.shape, BF16),
            shape((L, units, 2, ch, D), BF16),
            shape((2 * SEGS, D), F32),
        ),
        in_specs=in_specs,
        out_specs=[vmem] * 4,
        scratch_shapes=scratch,
        compiler_params=pltpu.CompilerParams(
            collective_id=0, has_side_effects=True, vmem_limit_bytes=VMEM_BYTES
        ),
        name="layers",
    )(x, ct, ng, jnp.swapaxes(inw, 2, 3), jnp.swapaxes(fw, 1, 2), jnp.swapaxes(gw, 2, 3), ow, ph, bl, gg, ffw, dw)

    if not reduce:
        wg, sums = lax.psum((wg, sums), "dp")
    elif n_dp > 8:
        groups = [list(range(k, n_dp, 8)) for k in range(8)]
        wg, sums = lax.psum((wg, sums), "dp", axis_index_groups=groups)
    wg = wg.astype(F32)
    gains = sums[: 2 * L].reshape(L, 2, D)
    piece = D // lax.axis_size("tensor")
    gains = lax.dynamic_slice_in_dim(gains, lax.axis_index("tensor") * piece, piece, 2)
    small = sums[2 * L : 6 * L, :ch].reshape(L, 4, ch)
    g_down = wg[:, :fu].reshape(L, F, D)
    g_ffn = wg[:, fu : units - 4].reshape(L, D, 2 * F)
    return (
        out,
        ig,
        gains,
        jnp.swapaxes(wg[:, units - 2], 2, 3),
        jnp.swapaxes(wg[:, units - 1, 0], 1, 2),
        jnp.swapaxes(wg[:, units - 3], 2, 3),
        wg[:, units - 4],
        small[:, 2],
        small[:, 3],
        small[:, 0:2],
        jnp.stack([g_ffn[:, :, :F], g_ffn[:, :, F:]], axis=1),
        g_down,
    )


def solution(mesh):
    tokens = P(("dp", "tensor"), None)
    return jax.shard_map(
        local,
        mesh=mesh,
        in_specs=(
            tokens,
            tokens,
            P(),
            P(None, None, None, "tensor"),
            P(None, None, "tensor"),
            P(None, None, None, "tensor"),
            P(None, None, "tensor", None),
            P(None, "tensor"),
            P(None, "tensor"),
            P(None, None, "tensor"),
            P(None, None, None, "tensor"),
            P(None, "tensor", None),
        ),
        out_specs=(
            tokens,
            tokens,
            P(None, None, "tensor"),
            P(None, None, None, "tensor"),
            P(None, None, "tensor"),
            P(None, None, None, "tensor"),
            P(None, None, "tensor", None),
            P(None, "tensor"),
            P(None, "tensor"),
            P(None, None, "tensor"),
            P(None, None, None, "tensor"),
            P(None, "tensor", None),
        ),
        check_vma=False,
    )
```

```python
import functools
import types

import jax
import jax.numpy as jnp
from jax import lax
from jax.experimental import pallas as pl
from jax.experimental.pallas import tpu as pltpu
from jax.sharding import PartitionSpec as P

MESH = pl.DeviceIdType.MESH
F32 = jnp.float32
BF16 = jnp.bfloat16

GROUP_CH = 48
EPS_NORM = 1e-06
EPS_GROUP = 1e-05
LANES = 128
SEGS = 8
CHUNKS = 4
LAG = 2
UNIT_PIECES = 3
PIECES = 2
SLOTS = 10
VMEM_BYTES = 63 * 1024 * 1024


def sigmoid(v):
    return 0.5 * jnp.tanh(0.5 * v) + 0.5


def mm(left, right):
    return jnp.dot(left, right, preferred_element_type=F32)


def mm_nt(left, right):
    return lax.dot_general(left, right, (((1,), (1,)), ((), ())), preferred_element_type=F32)


def mm_tn(left, right):
    return lax.dot_general(left, right, (((0,), (0,)), ((), ())), preferred_element_type=F32)


def loop(count, body):
    def step(index, carry):
        body(index)
        return carry

    lax.fori_loop(0, count, step, 0)


def iota(shape, dim):
    return lax.broadcasted_iota(jnp.int32, shape, dim)


def permutation(tokens):
    width = tokens // SEGS
    row = iota((tokens, tokens), 0)
    place = lax.rem(row, SEGS) * width + row // SEGS
    return jnp.where(iota((tokens, tokens), 1) == place, 1.0, 0.0).astype(BF16)


def scratch_of(z):
    L, D, C, F, R, N = z.L, z.D, z.C, z.F, z.R, CHUNKS
    rows = (2, N, 2, R)
    own = (N, R)
    bufs = dict(
        wmix=((L, 5 * C, D), BF16),
        wout=((L, 2 * C, D), BF16),
        wffn=((L, D, 2 * F), BF16),
        par=((L, 8, C), F32),
        ngf=((L, 2, D), F32),
        gsum=((C, C), BF16),
        st=((2 * L, *own, D), F32),
        mixfull=((L, *rows, D), BF16),
        ffnfull=((L, *rows, D), BF16),
        gfull=((2, *rows, D), BF16),
        proj=((L, *rows, 5 * C), F32),
        state=((L, 2, 2, 2, SEGS + N * R, C), F32),
        unit=((L, 2, *rows, C), F32),
        inv=((L, *rows, C), F32),
        mixed=((L, *rows, 2 * C), BF16),
        gup=((L, *rows, 2 * F), BF16),
        hidden=((L, *rows, F), BF16),
        keep=((*rows, C), F32),
        drive=((2, *rows, C), F32),
        seg=((3, 2, 2, SEGS, C), F32),
        segk=((L, 2, 2, SEGS, C), F32),
        cur=((2, 2, 2, SEGS, C), F32),
        tot=((2, 2, R, C), F32),
        dgu=((*rows, 2 * F), BF16),
        dproj=((*rows, 5 * C), BF16),
        psc=((2, R, D), F32),
        xpart=((*own, D), F32),
        opart=((2, *own, D), F32),
        grad=((*own, D), F32),
        stage=((2, 3, *own, D), BF16),
        land=((2, 3, *own, D), BF16),
        gacc=((L, 2, SEGS, D), F32),
        sacc=((L, 4, SEGS, C), F32),
        wdown=((L, F, D), BF16),
        wg=((L, z.units, 2, z.blk, D), BF16),
        swork=((2 * SEGS, D), F32),
        sland=((5, 2 * SEGS, D), F32),
    )
    if z.reduce:
        unit = (SLOTS, z.blk, D)
        bufs.update(yland=(unit, BF16), mland=(unit, BF16))
        bufs.update(zland=((SLOTS // 2, z.blk, D), BF16), zfold=((SLOTS // 2, 2, z.blk, D), BF16))
    sems = dict(
        ags=(4 * L, 3, N),
        agr=(4 * L, 3, N),
        rss=(4 * L, 3, N),
        rsr=(4 * L, 3, N),
        wsem=(L, 10),
        ss=(5,),
        sr=(5,),
        outs=(z.units * L,),
    )
    if z.reduce:
        sems.update(us=(z.units * L, 5), ur=(z.units * L, 5))
    names = list(bufs) + list(sems)
    shapes = [pltpu.VMEM(s, d) for s, d in bufs.values()]
    shapes += [pltpu.SemaphoreType.DMA(s) for s in sems.values()]
    names.append("freed")
    shapes.append(pltpu.SemaphoreType.REGULAR((3,)))
    return names, shapes


IN_NAMES = ("x", "ct", "ng", "inw", "fw", "gw", "ow", "ph", "bl", "gg", "ffw", "dw")
OUT_NAMES = ("out", "ig", "wgout", "sums")


def mega(z, names, *refs):
    r = types.SimpleNamespace(**dict(zip(IN_NAMES + OUT_NAMES + tuple(names), refs)))
    L, D, C, F, R, N = z.L, z.D, z.C, z.F, z.R, CHUNKS
    ch = z.ch
    Q = R // SEGS
    dp = lax.axis_index("dp")
    me = lax.axis_index("tensor")
    core = lax.rem(me, 2)
    xi = me // 2
    other = 1 - xi
    sib = xi * 2 + 1 - core
    xnb = other * 2 + core

    inner = lax.rem(dp, 8)
    base = dp - inner
    y = lax.rem(inner, 2)
    line = inner // 2
    middle = (line == 1) | (line == 2)

    def on_line(place, row):
        return (base + 2 * place + row, me)

    y_peer = on_line(line, 1 - y)
    pair_peer = on_line(line + 1 - 2 * lax.rem(line, 2), y)
    cross_peer = on_line(3 - line, y)

    peers = [(dp, sib), (dp, xnb)]
    if z.reduce:
        peers += [y_peer, pair_peer, cross_peer]
    barrier = pltpu.get_barrier_semaphore()
    for peer in peers:
        pl.semaphore_signal(barrier, inc=1, device_id=peer, device_id_type=MESH)
    pl.semaphore_wait(barrier, len(peers))

    def remote(src, dst, send, recv, peer, pieces=1):
        def copy(source, target):
            return pltpu.make_async_remote_copy(
                src_ref=source,
                dst_ref=target,
                send_sem=send,
                recv_sem=recv,
                device_id=peer if isinstance(peer, tuple) else (dp, peer),
                device_id_type=MESH,
            )

        def start():
            lead = src.shape[0] if len(src.shape) == 3 else 1
            size = src.shape[-2] // pieces
            for first in range(lead):
                for k in range(pieces):
                    at = pl.ds(k * size, size)
                    if len(src.shape) == 3:
                        copy(src.at[first, at], dst.at[first, at]).start()
                    else:
                        copy(src.at[at], dst.at[at]).start()

        whole = copy(src, dst)
        return types.SimpleNamespace(
            start=start, wait_recv=whole.wait_recv, wait_send=whole.wait_send, wait=whole.wait
        )

    def unit_of(u):
        return L - 1 - u // z.units, lax.rem(u, z.units)

    half = line // 2

    def unit_copy(u, stage, even):
        l, k = unit_of(u)
        slot = lax.rem(u, SLOTS)
        mine = r.wg.at[l, k, y]
        if even:
            part = r.wg.at[l, k, half]
            src, dst, peer = (
                (r.wg.at[l, k], r.zfold.at[slot // 2], pair_peer),
                (r.wg.at[l, k, 1 - half], r.mland.at[slot], cross_peer),
                (part, r.yland.at[slot], y_peer),
                (part, part, cross_peer),
                (r.wg.at[l, k], r.wg.at[l, k], pair_peer),
            )[stage]
        else:
            src, dst, peer = (
                (r.wg.at[l, k, 1 - y], r.yland.at[slot], y_peer),
                (mine, r.zland.at[slot // 2], pair_peer),
                (mine, r.mland.at[slot], cross_peer),
                (mine, r.zland.at[slot // 2], pair_peer),
                (mine, mine, y_peer),
            )[stage]
        return remote(src, dst, r.us.at[u, stage], r.ur.at[u, stage], peer, UNIT_PIECES)

    def unit_land(u, stage, ref, peer):
        return remote(ref, ref, r.us.at[u, stage], r.ur.at[u, stage], peer)

    def unit_add(u, part, landed):
        l, k = unit_of(u)
        r.wg[l, k, part] = (r.wg[l, k, part].astype(F32) + landed.astype(F32)).astype(BF16)

    def tell(sem, peer):
        pl.semaphore_signal(sem, inc=1, device_id=peer, device_id_type=MESH)

    def on_middle(body):
        pl.when(middle)(body)

    def on_end(body):
        pl.when(jnp.logical_not(middle))(body)

    def odd_stage(u, stage):
        copy = lambda n: unit_copy(u, n, False)
        slot = lax.rem(u, SLOTS)
        l, k = unit_of(u)
        if stage == 0:
            copy(0).start()
        if stage == 1:
            copy(0).wait_send()
            tell(r.freed.at[0], y_peer)
            copy(0).wait_recv()
            unit_add(u, y, r.yland[slot])
            on_end(lambda: copy(1).start())
        if stage == 2:

            @on_middle
            def _():
                copy(1).wait_recv()
                unit_add(u, y, r.zland[slot // 2])
                copy(2).start()

        if stage == 3:

            @on_middle
            def _():
                copy(2).wait_recv()
                copy(2).wait_send()
                unit_add(u, y, r.mland[slot])
                copy(3).start()

        if stage == 4:

            @on_end
            def _():
                copy(1).wait_send()
                copy(3).wait_recv()
                r.wg[l, k, y] = r.zland[slot // 2]

            pl.semaphore_wait(r.freed.at[0], 1)
            copy(4).start()
        if stage == 5:
            unit_land(u, 4, r.wg.at[l, k, 1 - y], y_peer).wait_recv()
            copy(4).wait_send()
            on_middle(lambda: copy(3).wait_send())
            unit_out(u).start()

    def even_stage(u, stage):
        copy = lambda n: unit_copy(u, n, True)
        slot = lax.rem(u, SLOTS)
        l, k = unit_of(u)
        if stage == 0:
            on_end(lambda: copy(0).start())
        if stage == 1:

            @on_end
            def _():
                copy(0).wait_send()
                tell(r.freed.at[1], pair_peer)

            @on_middle
            def _():
                copy(0).wait_recv()
                for part in range(2):
                    unit_add(u, part, r.zfold[slot // 2, part])
                copy(1).start()

        if stage == 2:

            @on_middle
            def _():
                copy(1).wait_send()
                tell(r.freed.at[2], cross_peer)
                copy(1).wait_recv()
                unit_add(u, half, r.mland[slot])
                copy(2).start()

        if stage == 3:

            @on_middle
            def _():
                copy(2).wait_send()
                copy(2).wait_recv()
                unit_add(u, half, r.yland[slot])
                pl.semaphore_wait(r.freed.at[2], 1)
                copy(3).start()

        if stage == 4:

            @on_middle
            def _():
                unit_land(u, 3, r.wg.at[l, k, 1 - half], cross_peer).wait_recv()
                pl.semaphore_wait(r.freed.at[1], 1)
                copy(4).start()

        if stage == 5:
            on_end(lambda: copy(4).wait_recv())

            @on_middle
            def _():
                copy(3).wait_send()
                copy(4).wait_send()

            unit_out(u).start()

    def unit_out(u):
        l, k = unit_of(u)
        return pltpu.make_async_copy(r.wg.at[l, k], r.wgout.at[l, k], r.outs.at[u])

    def tick(m):
        if not z.reduce:
            return
        for stage in reversed(range(6)):
            u = m - LAG * stage

            there = (u >= 0) & (u < z.units * L)

            @pl.when(there & (lax.rem(u, 2) == 1))
            def _():
                odd_stage(u, stage)

            @pl.when(there & (lax.rem(u, 2) == 0))
            def _():
                even_stage(u, stage)

    def ag_copy(e, full, c, kind):
        chip = other if kind == 2 else xi
        peer = xnb if kind == 0 else sib
        ref = full.at[chip, c, core]
        return remote(ref, ref, r.ags.at[e, kind, c], r.agr.at[e, kind, c], peer, PIECES if kind == 0 else 1)

    def ag_landing(e, full, c, kind):
        chip = xi if kind == 1 else other
        col = core if kind == 0 else 1 - core
        ref = full.at[chip, c, col]
        return remote(ref, ref, r.ags.at[e, kind, c], r.agr.at[e, kind, c], sib)

    def ag_start(e, full, c):
        ag_copy(e, full, c, 0).start()
        ag_copy(e, full, c, 1).start()

    def ag_take_x(e, full, c):
        ag_landing(e, full, c, 0).wait_recv()
        ag_copy(e, full, c, 2).start()

    def rs_copy(e, c, kind):
        return remote(
            r.stage.at[r_side(e), kind, c],
            r.land.at[r_side(e), kind, c],
            r.rss.at[e, kind, c],
            r.rsr.at[e, kind, c],
            xnb if kind == 1 else sib,
            PIECES if kind == 1 else 1,
        )

    def r_side(e):
        return e // (2 * L)

    def rs_other(e, c):
        r.stage[r_side(e), 0, c] = r.psc[1 - core].astype(BF16)
        rs_copy(e, c, 0).start()
        r.xpart[c] = r.psc[core]

    def rs_pass(e, c):
        rs_copy(e, c, 0).wait_recv()
        r.stage[r_side(e), 1, c] = (r.xpart[c] + r.land[r_side(e), 0, c].astype(F32)).astype(BF16)
        rs_copy(e, c, 1).start()

    def rs_own(e, c):
        r.stage[r_side(e), 2, c] = r.psc[1 - core].astype(BF16)
        rs_copy(e, c, 2).start()
        r.opart[r_side(e), c] = r.psc[core]

    def rs_final(e, full, c):
        rs_copy(e, c, 2).wait_recv()
        rs_copy(e, c, 1).wait_recv()
        side = r_side(e)
        total = r.opart[side, c] + r.land[side, 2, c].astype(F32) + r.land[side, 1, c].astype(F32)
        for kind in range(3):
            rs_copy(e, c, kind).wait_send()
            ag_copy(e, full, c, kind).wait_send()
        return total

    def exchange_loop(e, full, order, send, stage, early=None):
        def when_late(cond, body):
            pl.when(cond if early is None else cond & jnp.logical_not(early))(body)

        send(order(0))
        if early is not None:

            @pl.when(early)
            def _():
                def take(c):
                    ag_landing(e, full, c, 1).wait_recv()
                    ag_landing(e, full, c, 2).wait_recv()

                loop(N, take)

        def step(i):
            @pl.when(i + 1 < N)
            def _():
                send(order(i + 1))

            def take_sib():
                ag_landing(e, full, order(i), 1).wait_recv()

            def take_x():
                ag_take_x(e, full, order(i - N + 1))

            def take_far():
                ag_landing(e, full, order(i - N), 2).wait_recv()

            when_late(i < N, take_sib)
            when_late((i >= N - 1) & (i < 2 * N - 1), take_x)
            when_late(i >= N, take_far)
            stage(i)

        loop(2 * N, step)

    def chip_chunk(i, order, own_first):
        first = i < N
        chunk = order(jnp.where(first, i, i - N))
        return jnp.where(first == own_first, xi, other), chunk

    def rs_step(e, i, order, own_first):
        first = i < N
        chunk = order(jnp.where(first, i, i - N))

        @pl.when(first == own_first)
        def _():
            rs_own(e, chunk)

        @pl.when(first != own_first)
        def _():
            rs_other(e, chunk)

        behind = jnp.where(own_first, i - N, i) - 1

        @pl.when((behind >= 0) & (behind < N))
        def _():
            rs_pass(e, order(behind))

    ascending = lambda j: j
    descending = lambda j: N - 1 - j

    def norm_rows(s):
        return lax.rsqrt(jnp.mean(s * s, axis=-1, keepdims=True) + EPS_NORM)

    def group_sum(v):
        high = v.astype(BF16)
        rest = (v - high.astype(F32)).astype(BF16)
        weight = r.gsum[...]
        return (mm(high, weight) + mm(rest, weight)) * (1.0 / (2 * GROUP_CH))

    def fold(v):
        return jnp.sum(v.reshape(v.shape[0] // SEGS, SEGS, v.shape[1]), axis=0)

    def flat(v):
        return v.reshape(-1, v.shape[-1])

    w_copies = []
    for l in range(L):
        parts = (r.inw.at[l, 0], r.inw.at[l, 1], r.fw.at[l], r.gw.at[l, 0], r.gw.at[l, 1])
        pairs = [(part, r.wmix.at[l, pl.ds(k * C, ch), :]) for k, part in enumerate(parts)]
        pairs += [(r.ow.at[l, k], r.wout.at[l, pl.ds(k * C, ch), :]) for k in range(2)]
        pairs += [(r.ffw.at[l, k], r.wffn.at[l, :, pl.ds(k * F, F)]) for k in range(2)]
        pairs += [(r.dw.at[l], r.wdown.at[l])]
        w_copies += [
            pltpu.make_async_copy(src, dst, r.wsem.at[l, k]) for k, (src, dst) in enumerate(pairs)
        ]
    for copy in w_copies:
        copy.start()

    tokens = N * R
    r.st[0] = mm(permutation(tokens), r.x[...]).reshape(N, R, D)
    r.ngf[...] = r.ng[...].astype(F32)

    def send_first(c):
        s = r.st[0, c]
        r.mixfull[0, xi, c, core] = (s * norm_rows(s) * r.ngf[0, 0:1, :]).astype(BF16)
        ag_start(0, r.mixfull.at[0], c)

    loop(N, send_first)

    r.grad[...] = mm(permutation(tokens), r.ct[...]).reshape(N, R, D)
    first_grad = r.gfull.at[0]

    def keep_cotangent(c):
        first_grad[xi, c, core] = r.grad[c].astype(BF16)

    loop(N, keep_cotangent)
    width = tokens // SEGS
    for k in range(5):
        r.wmix[:, k * C + ch : (k + 1) * C, :] = jnp.zeros((L, C - ch, D), BF16)
    for k in range(2):
        r.wout[:, k * C + ch : (k + 1) * C, :] = jnp.zeros((L, C - ch, D), BF16)
    r.par[...] = jnp.zeros_like(r.par)
    r.gacc[...] = jnp.zeros_like(r.gacc)
    r.wg[:, z.units - 1, 1] = jnp.zeros((L, z.blk, D), BF16)
    r.sacc[...] = jnp.zeros_like(r.sacc)
    for l in range(L):
        angle = r.ph[l : l + 1, :]
        turn_cos, turn_sin = jnp.cos(angle), jnp.sin(angle)
        r.par[l, 0:1, 0:ch] = turn_cos
        r.par[l, 1:2, 0:ch] = turn_sin
        r.par[l, 2:3, 0:ch] = sigmoid(r.bl[l : l + 1, :])
        r.par[l, 3:4, 0:ch] = r.gg[l, 0:1, :].astype(F32)
        r.par[l, 4:5, 0:ch] = r.gg[l, 1:2, :].astype(F32)
        for _ in range(width.bit_length() - 1):
            turn_cos, turn_sin = (
                turn_cos * turn_cos - turn_sin * turn_sin,
                2.0 * turn_cos * turn_sin,
            )
        r.par[l, 5:6, 0:ch] = turn_cos
        r.par[l, 6:7, 0:ch] = turn_sin
    gi, gj = iota((C, C), 0), iota((C, C), 1)
    same = (gi // GROUP_CH == gj // GROUP_CH) & (gi < ch) & (gj < ch)
    r.gsum[...] = jnp.where(same, 1.0, 0.0).astype(BF16)

    def rows_of(q):
        return slice(q * SEGS, (q + 1) * SEGS)

    def scan_local(l, chip, c, turn_cos, turn_sin):
        for k in range(2):
            h_re, h_im, prod = r.seg[0, chip, k], r.seg[1, chip, k], r.seg[2, chip, k]
            for q in range(Q):
                rate = r.keep[chip, c, k, rows_of(q), :]
                h_re, h_im = (
                    rate * (turn_cos * h_re - turn_sin * h_im) + r.drive[0, chip, c, k, rows_of(q), :],
                    rate * (turn_cos * h_im + turn_sin * h_re) + r.drive[1, chip, c, k, rows_of(q), :],
                )
                prod = prod * rate
            r.seg[0, chip, k], r.seg[1, chip, k], r.seg[2, chip, k] = h_re, h_im, prod

    def scan_final(l, chip, c, turn_cos, turn_sin):
        base = SEGS + c * R
        for k in range(2):
            h_re, h_im = r.cur[0, chip, k], r.cur[1, chip, k]
            for q in range(Q):
                rate = r.keep[chip, c, k, rows_of(q), :]
                h_re, h_im = (
                    rate * (turn_cos * h_re - turn_sin * h_im) + r.drive[0, chip, c, k, rows_of(q), :],
                    rate * (turn_cos * h_im + turn_sin * h_re) + r.drive[1, chip, c, k, rows_of(q), :],
                )
                at = pl.ds(pl.multiple_of(base + q * SEGS, SEGS), SEGS)
                r.state[l, 0, chip, k, at, :] = h_re
                r.state[l, 1, chip, k, at, :] = h_im
            r.cur[0, chip, k], r.cur[1, chip, k] = h_re, h_im

    def scan_back_local(l, chip, c, turn_cos, turn_sin):
        for k in range(2):
            u_re, u_im = r.seg[0, chip, k], r.seg[1, chip, k]
            for q in reversed(range(Q)):
                rate = r.keep[chip, c, k, rows_of(q), :]
                t_re = r.drive[0, chip, c, k, rows_of(q), :] + u_re
                t_im = r.drive[1, chip, c, k, rows_of(q), :] + u_im
                u_re = rate * (turn_cos * t_re + turn_sin * t_im)
                u_im = rate * (turn_cos * t_im - turn_sin * t_re)
            r.seg[0, chip, k], r.seg[1, chip, k] = u_re, u_im

    def scan_back_final(l, chip, c, turn_cos, turn_sin):
        for k in range(2):
            u_re, u_im = r.cur[0, chip, k], r.cur[1, chip, k]
            for q in reversed(range(Q)):
                rate = r.keep[chip, c, k, rows_of(q), :]
                t_re = r.drive[0, chip, c, k, rows_of(q), :] + u_re
                t_im = r.drive[1, chip, c, k, rows_of(q), :] + u_im
                r.tot[0, k, rows_of(q), :] = t_re
                r.tot[1, k, rows_of(q), :] = t_im
                u_re = rate * (turn_cos * t_re + turn_sin * t_im)
                u_im = rate * (turn_cos * t_im - turn_sin * t_re)
            r.cur[0, chip, k], r.cur[1, chip, k] = u_re, u_im

    def carry_over(l, back):
        all_cos, all_sin = r.par[l, 5:6, :], r.par[l, 6:7, :]
        if back:
            all_sin = -all_sin
        c_re = jnp.zeros((1, C), F32)
        c_im = jnp.zeros((1, C), F32)
        order = [(chip, k, s) for chip in range(2) for k in range(2) for s in range(SEGS)]
        for chip, k, s in reversed(order) if back else order:
            one = slice(s, s + 1)
            r.cur[0, chip, k, one, :] = c_re
            r.cur[1, chip, k, one, :] = c_im
            prod = r.segk[l, chip, k, one, :]
            c_re, c_im = (
                prod * (all_cos * c_re - all_sin * c_im) + r.seg[0, chip, k, one, :],
                prod * (all_cos * c_im + all_sin * c_re) + r.seg[1, chip, k, one, :],
            )

    def forward_layer(l):
        turn_cos, turn_sin, lower = r.par[l, 0:1, :], r.par[l, 1:2, :], r.par[l, 2:3, :]
        gain_re, gain_im = r.par[l, 3:4, :], r.par[l, 4:5, :]
        e = 2 * l
        full = r.mixfull.at[l]

        def send_mix(c):
            @pl.when(l > 0)
            def _():
                s = r.st[2 * l - 1, c] + rs_final(e - 1, r.ffnfull.at[l - 1], c)
                r.st[2 * l, c] = s
                full[xi, c, core] = (s * norm_rows(s) * r.ngf[l, 0:1, :]).astype(BF16)
                ag_start(e, full, c)

        @pl.when(l == 0)
        def _():
            for copy in w_copies:
                copy.wait()

        r.seg[0:2] = jnp.zeros((2, 2, 2, SEGS, C), F32)
        r.seg[2] = jnp.ones((2, 2, SEGS, C), F32)

        def project(j):
            chip, c = chip_chunk(j, ascending, True)
            proj = mm_nt(flat(full[chip, c]), r.wmix[l])
            r.proj[l, chip, c] = proj.reshape(2, R, 5 * C)
            in_re, in_im, pre = proj[:, 0:C], proj[:, C : 2 * C], proj[:, 2 * C : 3 * C]
            rate = lower + (1.0 - lower) * sigmoid(pre)
            r.keep[chip, c] = rate.reshape(2, R, C)
            r.drive[0, chip, c] = ((1.0 - rate) * in_re * sigmoid(in_re)).reshape(2, R, C)
            r.drive[1, chip, c] = ((1.0 - rate) * in_im * sigmoid(in_im)).reshape(2, R, C)
            scan_local(l, chip, c, turn_cos, turn_sin)

        exchange_loop(e, full, ascending, send_mix, project)

        def send_cotangent(i):
            ag_start(2 * L, first_grad, l * z.early + i)

        loop(z.early, send_cotangent)
        r.segk[l] = r.seg[2]
        carry_over(l, False)
        for part in range(2):
            r.state[l, part, :, :, 0:SEGS, :] = r.cur[part]

        def mix(j):
            chip, c = chip_chunk(j, ascending, False)
            scan_final(l, chip, c, turn_cos, turn_sin)
            at = pl.ds(pl.multiple_of(SEGS + c * R, SEGS), R)
            s_re = flat(r.state[l, 0, chip, :, at, :])
            s_im = flat(r.state[l, 1, chip, :, at, :])
            centre = group_sum(s_re + s_im)
            d_re, d_im = s_re - centre, s_im - centre
            scale = lax.rsqrt(group_sum(d_re * d_re + d_im * d_im) + EPS_GROUP)
            u_re, u_im = d_re * scale, d_im * scale
            r.unit[l, 0, chip, c] = u_re.reshape(2, R, C)
            r.unit[l, 1, chip, c] = u_im.reshape(2, R, C)
            r.inv[l, chip, c] = scale.reshape(2, R, C)
            gate_re = flat(r.proj[l, chip, c, :, :, 3 * C : 4 * C])
            gate_im = flat(r.proj[l, chip, c, :, :, 4 * C : 5 * C])
            m_re = (u_re * gain_re * sigmoid(gate_re)).astype(BF16)
            m_im = (u_im * gain_im * sigmoid(gate_im)).astype(BF16)
            r.mixed[l, chip, c, :, :, 0:C] = m_re.reshape(2, R, C)
            r.mixed[l, chip, c, :, :, C : 2 * C] = m_im.reshape(2, R, C)
            r.psc[...] = mm(flat(r.mixed[l, chip, c]), r.wout[l]).reshape(2, R, D)

            rs_step(e, j, ascending, False)

        loop(2 * N, mix)

        def take_cotangent(i):
            ag_take_x(2 * L, first_grad, l * z.early + i)

        loop(z.early, take_cotangent)
        e2 = e + 1
        full2 = r.ffnfull.at[l]

        def send_ffn(c):
            s = r.st[2 * l, c] + rs_final(e, full, c)
            r.st[2 * l + 1, c] = s
            full2[xi, c, core] = (s * norm_rows(s) * r.ngf[l, 1:2, :]).astype(BF16)
            ag_start(e2, full2, c)

        def feed(j):
            chip, c = chip_chunk(j, ascending, True)
            both = mm(flat(full2[chip, c]), r.wffn[l])
            r.gup[l, chip, c] = both.astype(BF16).reshape(2, R, 2 * F)
            gate, up = both[:, 0:F], both[:, F : 2 * F]
            hidden = (gate * sigmoid(gate) * up).astype(BF16)
            r.hidden[l, chip, c] = hidden.reshape(2, R, F)
            r.psc[...] = mm(hidden, r.wdown[l]).reshape(2, R, D)

            rs_step(e2, j, ascending, True)

        exchange_loop(e2, full2, ascending, send_ffn, feed)
        rs_pass(e2, N - 1)

    loop(L, forward_layer)

    def last_sum(c):
        e = 2 * L - 1
        s = r.st[2 * L - 1, c] + rs_final(e, r.ffnfull.at[L - 1], c)
        r.out[pl.ds(pl.multiple_of(c * R, R), R), :] = s.astype(BF16)

    def norm_back(l, which, c, grad_out):
        s = r.st[2 * l + which, c]
        scale = norm_rows(s)
        r.gacc[l, which] += fold(grad_out * s * scale)
        scaled = grad_out * r.ngf[l, which : which + 1, :]
        back = scale * scaled - s * (scale * scale * scale) * jnp.mean(
            scaled * s, axis=-1, keepdims=True
        )
        r.grad[c] = r.grad[c] + back

    def backward_layer(step):
        l = L - 1 - step
        e = 2 * L + 2 * step
        full = r.gfull.at[0]

        early = step == 0

        def send_ffn(c):
            @pl.when(step > 0)
            def _():
                norm_back(l + 1, 0, c, rs_final(e - 1, r.gfull.at[1], c))
                full[xi, c, core] = r.grad[c].astype(BF16)
                ag_start(e, full, c)

        def feed_back(j):
            chip, c = chip_chunk(j, descending, step > 0)
            g_hidden = mm_nt(flat(full[chip, c]), r.wdown[l])
            both = flat(r.gup[l, chip, c]).astype(F32)
            gate, up = both[:, 0:F], both[:, F : 2 * F]
            s = sigmoid(gate)
            g_gate = (g_hidden * up * s * (1.0 + gate * (1.0 - s))).astype(BF16)
            g_up = (g_hidden * gate * s).astype(BF16)
            r.dgu[chip, c, :, :, 0:F] = g_gate.reshape(2, R, F)
            r.dgu[chip, c, :, :, F : 2 * F] = g_up.reshape(2, R, F)
            r.psc[...] = mm_nt(flat(r.dgu[chip, c]), r.wffn[l]).reshape(2, R, D)

            rs_step(e, j, descending, step > 0)

            @pl.when((step > 0) & (j == 2))
            def _():
                tick(step * z.units - 1)

        exchange_loop(e, full, descending, send_ffn, feed_back, early)

        @pl.when(step > 0)
        def _():
            rs_pass(e, 0)

        @pl.when(step == 0)
        def _():
            loop(N, last_sum)

        def ffn_tile(i):
            cols = pl.ds(pl.multiple_of(i * F, LANES), F)
            part = mm_tn(flat(r.ffnfull[l, :, :, :, :, cols]), flat(r.dgu[...])).astype(BF16)
            r.wg[l, pl.ds(i * z.fu, z.fu)] = part.reshape(z.fu, 2, z.blk, D)

        loop(D // F, ffn_tile)
        part = mm_tn(flat(r.hidden[l]), flat(full[...])).astype(BF16)
        r.wg[l, z.units - 4 - z.fu : z.units - 4] = part.reshape(z.fu, 2, z.blk, D)
        first_tick = step * z.units
        tick(first_tick)

        turn_cos, turn_sin, lower = r.par[l, 0:1, :], r.par[l, 1:2, :], r.par[l, 2:3, :]
        gain_re, gain_im = r.par[l, 3:4, :], r.par[l, 4:5, :]
        e2 = e + 1
        full2 = r.gfull.at[1]

        def send_mix(c):
            norm_back(l, 1, c, rs_final(e, full, c))
            full2[xi, c, core] = r.grad[c].astype(BF16)
            ag_start(e2, full2, c)

        r.seg[0:2] = jnp.zeros((2, 2, 2, SEGS, C), F32)

        def mix_back(j):
            chip, c = chip_chunk(j, descending, True)
            g_both = mm_nt(flat(full2[chip, c]), r.wout[l])
            g_re, g_im = g_both[:, 0:C], g_both[:, C : 2 * C]
            s_re = sigmoid(flat(r.proj[l, chip, c, :, :, 3 * C : 4 * C]))
            s_im = sigmoid(flat(r.proj[l, chip, c, :, :, 4 * C : 5 * C]))
            u_re, u_im = flat(r.unit[l, 0, chip, c]), flat(r.unit[l, 1, chip, c])
            n_re, n_im = g_re * s_re, g_im * s_im
            r.sacc[l, 0] += fold(n_re * u_re)
            r.sacc[l, 1] += fold(n_im * u_im)
            x_re, x_im = n_re * gain_re, n_im * gain_im
            cross_re, cross_im = x_re * u_re, x_im * u_im
            r.dproj[chip, c, :, :, 3 * C : 4 * C] = (cross_re * (1.0 - s_re)).astype(BF16).reshape(2, R, C)
            r.dproj[chip, c, :, :, 4 * C : 5 * C] = (cross_im * (1.0 - s_im)).astype(BF16).reshape(2, R, C)
            mean_one = group_sum(x_re + x_im)
            mean_two = group_sum(cross_re + cross_im)
            scale = flat(r.inv[l, chip, c])
            r.drive[0, chip, c] = (scale * (x_re - mean_one - u_re * mean_two)).reshape(2, R, C)
            r.drive[1, chip, c] = (scale * (x_im - mean_one - u_im * mean_two)).reshape(2, R, C)
            pre = flat(r.proj[l, chip, c, :, :, 2 * C : 3 * C])
            r.keep[chip, c] = (lower + (1.0 - lower) * sigmoid(pre)).reshape(2, R, C)
            scan_back_local(l, chip, c, turn_cos, turn_sin)

            @pl.when(lax.rem(j, 3) == 1)
            def _():
                tick(first_tick + 1 + j // 3)

        exchange_loop(e2, full2, descending, send_mix, mix_back)
        carry_over(l, True)

        def scan_back(j):
            chip, c = chip_chunk(j, descending, False)
            scan_back_final(l, chip, c, turn_cos, turn_sin)
            t_re, t_im = flat(r.tot[0]), flat(r.tot[1])
            at = pl.ds(pl.multiple_of(c * R, SEGS), R)
            p_re = flat(r.state[l, 0, chip, :, at, :])
            p_im = flat(r.state[l, 1, chip, :, at, :])
            in_re = flat(r.proj[l, chip, c, :, :, 0:C])
            in_im = flat(r.proj[l, chip, c, :, :, C : 2 * C])
            fs = sigmoid(flat(r.proj[l, chip, c, :, :, 2 * C : 3 * C]))
            rate = lower + (1.0 - lower) * fs
            s_re, s_im = sigmoid(in_re), sigmoid(in_im)
            gc_re = t_re * p_re + t_im * p_im
            gc_im = t_im * p_re - t_re * p_im
            g_keep = gc_re * turn_cos + gc_im * turn_sin - (t_re * in_re * s_re + t_im * in_im * s_im)
            r.sacc[l, 2] += fold(rate * (gc_im * turn_cos - gc_re * turn_sin))
            r.sacc[l, 3] += fold(g_keep * (1.0 - fs))
            d_re = t_re * (1.0 - rate) * s_re * (1.0 + in_re * (1.0 - s_re))
            d_im = t_im * (1.0 - rate) * s_im * (1.0 + in_im * (1.0 - s_im))
            d_f = g_keep * (1.0 - lower) * fs * (1.0 - fs)
            r.dproj[chip, c, :, :, 0:C] = d_re.astype(BF16).reshape(2, R, C)
            r.dproj[chip, c, :, :, C : 2 * C] = d_im.astype(BF16).reshape(2, R, C)
            r.dproj[chip, c, :, :, 2 * C : 3 * C] = d_f.astype(BF16).reshape(2, R, C)
            r.psc[...] = mm(flat(r.dproj[chip, c]), r.wmix[l]).reshape(2, R, D)

            rs_step(e2, j, descending, False)

            @pl.when(j == N)
            def _():
                loop(2, out_tile)
                loop(2, gate_tile)

            @pl.when((j == 2) | (j == 3) | (j == N) | (j == 2 * N - 1))
            def _():
                tick(first_tick + jnp.where(j == 2 * N - 1, 7, 2 + j))

        base_unit = z.units - 4

        def out_tile(i):
            cols = pl.ds(pl.multiple_of(i * C, LANES), C)
            part = mm_tn(flat(r.mixed[l, :, :, :, :, cols]), flat(full2[...])).astype(BF16)
            r.wg[l, base_unit, i] = part[0:ch]

        def proj_tile(k, unit, block):
            cols = pl.ds(pl.multiple_of(k * C, LANES), C)
            part = mm_tn(flat(r.dproj[:, :, :, :, cols]), flat(r.mixfull[l])).astype(BF16)
            r.wg[l, unit, block] = part[0:ch]

        def gate_tile(i):
            proj_tile(3 + i, base_unit + 1, i)

        def in_tile(i):
            proj_tile(i, base_unit + 2 + i // 2, lax.rem(i, 2))

        loop(2 * N, scan_back)
        loop(3, in_tile)
        tick(first_tick + 8)

    loop(L, backward_layer)

    def last_grad(j):
        c = descending(j)
        norm_back(0, 0, c, rs_final(4 * L - 1, r.gfull.at[1], c))

    loop(N, last_grad)
    r.ig[...] = r.grad[...].reshape(tokens, D).astype(BF16)

    r.swork[...] = jnp.zeros_like(r.swork)
    for l in range(L):
        for which in range(2):
            at = 2 * l + which
            r.swork[at : at + 1, :] = jnp.sum(r.gacc[l, which], axis=0, keepdims=True)

    for l in range(L):
        for k in range(4):
            value = jnp.sum(r.sacc[l, k], axis=0, keepdims=True)
            if k == 3:
                lower = r.par[l, 2:3, :]
                value = value * lower * (1.0 - lower)
            at = 2 * L + 4 * l + k
            r.swork[at : at + 1, 0:C] = value

    swap_peers = [sib, xnb] + ([y_peer, pair_peer, cross_peer] if z.reduce else [])
    n_swaps = len(swap_peers)

    def swap(k):
        return remote(r.swork, r.sland.at[k], r.ss.at[k], r.sr.at[k], swap_peers[k])

    def swap_step(i):
        for k in range(n_swaps):

            @pl.when(i == k + 1)
            def _():
                swap(k).wait()
                rows = 2 * L if k < 2 else 2 * SEGS
                r.swork[0:rows, :] = r.swork[0:rows, :] + r.sland[k, 0:rows, :]

            @pl.when(i == k)
            def _():
                swap(k).start()

    start = L * z.units - 1
    ticks = 1 + 5 * LAG

    def drain(i):
        swap_step(i)
        tick(start + i)

    loop(ticks if z.reduce else n_swaps + 1, drain)
    r.sums[...] = r.swork[...]

    def write_out(u):
        if not z.reduce:
            unit_out(u).start()
        unit_out(u).wait()

    loop(z.units * L, write_out)


def finish(z, n_tensor, out, ig, sums, w_in, w_forget, w_gate, w_out, w_ffn, w_down, *o):
    L, ch, F = z.L, z.ch, z.F
    l, i = pl.program_id(0), pl.program_id(1)
    tokens = out.shape[0]

    @pl.when((l == 0) & (i == 0))
    def _():
        o[0][...] = mm_tn(permutation(tokens), out[...]).astype(BF16)
        me = lax.axis_index("tensor")
        piece = z.D // n_tensor
        for t in range(n_tensor):

            @pl.when(me == t)
            def _():
                for k in range(L):
                    o[2][k] = sums[2 * k : 2 * k + 2, t * piece : (t + 1) * piece]

        for k in range(L):
            at = 2 * L + 4 * k
            o[7][k : k + 1, :] = sums[at + 2 : at + 3, 0:ch]
            o[8][k : k + 1, :] = sums[at + 3 : at + 4, 0:ch]
            o[9][k] = sums[at : at + 2, 0:ch]

    @pl.when((l == 0) & (i == 1))
    def _():
        o[1][...] = mm_tn(permutation(tokens), ig[...]).astype(BF16)

    o[3][...] = w_in[...].astype(F32)
    o[4][...] = w_forget[...].astype(F32)
    o[5][...] = w_gate[...].astype(F32)
    o[6][...] = w_out[...].astype(F32)
    o[10][0, 0] = w_ffn[0, :, 0:F].astype(F32)
    o[10][0, 1] = w_ffn[0, :, F : 2 * F].astype(F32)
    o[11][...] = w_down[...].astype(F32)


def local(*args):
    x, ct, ng, inw, fw, gw, ow, ph, bl, gg, ffw, dw = args
    L, D = ng.shape[0], ng.shape[2]
    ch = fw.shape[2]
    F = dw.shape[1]
    C = -(-ch // LANES) * LANES
    n_dp = lax.axis_size("dp")
    reduce = n_dp % 8 == 0
    fu = F // (2 * ch)
    units = fu * (1 + D // F) + 4
    z = types.SimpleNamespace(
        L=L, D=D, C=C, F=F, ch=ch, R=x.shape[0] // CHUNKS, reduce=reduce, blk=ch, fu=fu, units=units
    )
    z.early = CHUNKS // L
    names, scratch = scratch_of(z)
    vmem = pl.BlockSpec(memory_space=pltpu.VMEM)
    anywhere = pl.BlockSpec(memory_space=pl.ANY)
    in_specs = [vmem] * 12
    for k in (3, 4, 5, 6, 10, 11):
        in_specs[k] = anywhere
    shape = jax.ShapeDtypeStruct
    out, ig, wg, sums = pl.pallas_call(
        functools.partial(mega, z, names),
        out_shape=(
            shape(x.shape, BF16),
            shape(x.shape, BF16),
            shape((L, units, 2, ch, D), BF16),
            shape((2 * SEGS, D), F32),
        ),
        in_specs=in_specs,
        out_specs=[vmem, vmem, anywhere, vmem],
        scratch_shapes=scratch,
        compiler_params=pltpu.CompilerParams(
            collective_id=0, has_side_effects=True, vmem_limit_bytes=VMEM_BYTES
        ),
        name="layers",
    )(x, ct, ng, jnp.swapaxes(inw, 2, 3), jnp.swapaxes(fw, 1, 2), jnp.swapaxes(gw, 2, 3), ow, ph, bl, gg, ffw, dw)

    if not reduce:
        wg, sums = lax.psum((wg, sums), "dp")
    elif n_dp > 8:
        groups = [list(range(k, n_dp, 8)) for k in range(8)]
        wg, sums = lax.psum((wg, sums), "dp", axis_index_groups=groups)
    n_tensor = lax.axis_size("tensor")
    blocks = wg.reshape(L, 2 * units, ch, D)
    rows = wg.reshape(L, 2 * units * ch, D)
    G = 3
    piece = ch // G

    def block_spec(count, index):
        return pl.BlockSpec((1, count, piece, D), lambda l, i: (l, index, i, 0))

    def row_spec(size, index):
        return pl.BlockSpec((1, size, D), lambda l, i: (l, index + i, 0))

    def whole(*dims):
        return pl.BlockSpec(dims, lambda l, i: (0,) * len(dims))

    first = 2 * (units - 4)
    res = pl.pallas_call(
        functools.partial(finish, z, n_tensor),
        grid=(L, G),
        out_shape=(
            shape(x.shape, BF16),
            shape(x.shape, BF16),
            shape((L, 2, D // n_tensor), F32),
            shape((L, 2, ch, D), F32),
            shape((L, 1, ch, D), F32),
            shape((L, 2, ch, D), F32),
            shape((L, 2, ch, D), F32),
            shape((L, ch), F32),
            shape((L, ch), F32),
            shape((L, 2, ch), F32),
            shape((L, 2, D, F), F32),
            shape((L, F, D), F32),
        ),
        in_specs=[
            whole(*x.shape),
            whole(*x.shape),
            whole(2 * SEGS, D),
            block_spec(2, first // 2 + 2),
            block_spec(1, first + 6),
            block_spec(2, first // 2 + 1),
            block_spec(2, first // 2),
            row_spec(D // G, 0),
            row_spec(F // G, D // (F // G)),
        ],
        out_specs=[
            whole(*x.shape),
            whole(*x.shape),
            whole(L, 2, D // n_tensor),
            block_spec(2, 0),
            block_spec(1, 0),
            block_spec(2, 0),
            block_spec(2, 0),
            whole(L, ch),
            whole(L, ch),
            whole(L, 2, ch),
            pl.BlockSpec((1, 2, D // G, F), lambda l, i: (l, 0, i, 0)),
            row_spec(F // G, 0),
        ],
        compiler_params=pltpu.CompilerParams(vmem_limit_bytes=VMEM_BYTES),
        name="finish",
    )(out, ig, sums, blocks, blocks, blocks, blocks, rows, rows)
    res = list(res)
    res[3] = jnp.swapaxes(res[3], 2, 3)
    res[4] = jnp.swapaxes(res[4][:, 0], 1, 2)
    res[5] = jnp.swapaxes(res[5], 2, 3)
    return tuple(res)


def solution(mesh):
    tokens = P(("dp", "tensor"), None)
    return jax.shard_map(
        local,
        mesh=mesh,
        in_specs=(
            tokens,
            tokens,
            P(),
            P(None, None, None, "tensor"),
            P(None, None, "tensor"),
            P(None, None, None, "tensor"),
            P(None, None, "tensor", None),
            P(None, "tensor"),
            P(None, "tensor"),
            P(None, None, "tensor"),
            P(None, None, None, "tensor"),
            P(None, "tensor", None),
        ),
        out_specs=(
            tokens,
            tokens,
            P(None, None, "tensor"),
            P(None, None, None, "tensor"),
            P(None, None, "tensor"),
            P(None, None, None, "tensor"),
            P(None, None, "tensor", None),
            P(None, "tensor"),
            P(None, "tensor"),
            P(None, None, "tensor"),
            P(None, None, None, "tensor"),
            P(None, "tensor", None),
        ),
        check_vma=False,
    )
```

```python
import functools
import types

import jax
import jax.numpy as jnp
from jax import lax
from jax.experimental import pallas as pl
from jax.experimental.pallas import tpu as pltpu
from jax.sharding import PartitionSpec as P

MESH = pl.DeviceIdType.MESH
F32 = jnp.float32
BF16 = jnp.bfloat16

GROUP_CH = 48
EPS_NORM = 1e-06
EPS_GROUP = 1e-05
LANES = 128
SEGS = 8
CHUNKS = 4
LAG = 2
PACE = (
    dict(feed=(1, 0, 0, 1, 0, 0, 1, 0), feed_end=0, ffn_end=2, mix=(1, 0, 1, 0, 1, 1, 1, 1), scan=(0, 1, 0, 1, 1, 0, 1, 0), end=2),
    dict(feed=(1, 0, 1, 0, 1, 0, 0, 1), feed_end=1, ffn_end=2, mix=(1, 0, 1, 0, 1, 1, 1, 1), scan=(0, 1, 0, 1, 1, 0, 1, 0), end=2),
)
AHEAD = 1
PIECES = 2
SLOTS = 10
VMEM_BYTES = 63 * 1024 * 1024


def sigmoid(v):
    return 0.5 * jnp.tanh(0.5 * v) + 0.5


def mm(left, right):
    return jnp.dot(left, right, preferred_element_type=F32)


def mm_nt(left, right):
    return lax.dot_general(left, right, (((1,), (1,)), ((), ())), preferred_element_type=F32)


def mm_tn(left, right):
    return lax.dot_general(left, right, (((0,), (0,)), ((), ())), preferred_element_type=F32)


def loop(count, body):
    def step(index, carry):
        body(index)
        return carry

    lax.fori_loop(0, count, step, 0)


def iota(shape, dim):
    return lax.broadcasted_iota(jnp.int32, shape, dim)


def permutation(tokens):
    width = tokens // SEGS
    row = iota((tokens, tokens), 0)
    place = lax.rem(row, SEGS) * width + row // SEGS
    return jnp.where(iota((tokens, tokens), 1) == place, 1.0, 0.0).astype(BF16)


def scratch_of(z):
    L, D, C, F, R, N = z.L, z.D, z.C, z.F, z.R, CHUNKS
    rows = (2, N, 2, R)
    own = (N, R)
    bufs = dict(
        wmix=((L, 5 * C, D), BF16),
        wout=((L, 2 * C, D), BF16),
        wffn=((L, D, 2 * F), BF16),
        par=((L, 8, C), F32),
        ngf=((L, 2, D), F32),
        gsum=((C, C), BF16),
        st=((2 * L, *own, D), F32),
        mixfull=((L, *rows, D), BF16),
        ffnfull=((L, *rows, D), BF16),
        gfull=((2, *rows, D), BF16),
        proj=((L, *rows, 5 * C), F32),
        state=((L, 2, 2, 2, SEGS + N * R, C), F32),
        unit=((L, 2, *rows, C), F32),
        inv=((L, *rows, C), F32),
        mixed=((L, *rows, 2 * C), BF16),
        gup=((L, *rows, 2 * F), BF16),
        hidden=((L, *rows, F), BF16),
        keep=((*rows, C), F32),
        drive=((2, *rows, C), F32),
        seg=((3, 2, 2, SEGS, C), F32),
        segk=((L, 2, 2, SEGS, C), F32),
        cur=((2, 2, 2, SEGS, C), F32),
        tot=((2, 2, R, C), F32),
        dgu=((*rows, 2 * F), BF16),
        dproj=((*rows, 5 * C), BF16),
        psc=((2, R, D), F32),
        xpart=((*own, D), F32),
        opart=((2, *own, D), F32),
        grad=((*own, D), F32),
        stage=((2, 3, *own, D), BF16),
        land=((2, 3, *own, D), BF16),
        gacc=((L, 2, SEGS, D), F32),
        sacc=((L, 4, SEGS, C), F32),
        wdown=((L, F, D), BF16),
        wg=((L, z.units, 2, z.blk, D), BF16),
        swork=((2 * SEGS, D), F32),
        sland=((5, 2 * SEGS, D), F32),
    )
    if z.reduce:
        unit = (SLOTS, z.sub, D)
        bufs.update(yland=(unit, BF16), mland=(unit, BF16))
        bufs.update(zland=(unit, BF16), zfold=((SLOTS, 2, z.sub, D), BF16))
    sems = dict(
        ags=(4 * L, 3, N),
        agr=(4 * L, 3, N),
        rss=(4 * L, 3, N),
        rsr=(4 * L, 3, N),
        wsem=(L, 10),
        ss=(5,),
        sr=(5,),
        outs=(z.period * L,),
    )
    if z.reduce:
        sems.update(us=(z.period * L, 5), ur=(z.period * L, 5))
    names = list(bufs) + list(sems)
    shapes = [pltpu.VMEM(s, d) for s, d in bufs.values()]
    shapes += [pltpu.SemaphoreType.DMA(s) for s in sems.values()]
    names.append("freed")
    shapes.append(pltpu.SemaphoreType.REGULAR((3,)))
    return names, shapes


IN_NAMES = ("x", "ct", "ng", "inw", "fw", "gw", "ow", "ph", "bl", "gg", "ffw", "dw")
OUT_NAMES = ("out", "ig", "wgout", "sums")


def mega(z, names, *refs):
    r = types.SimpleNamespace(**dict(zip(IN_NAMES + OUT_NAMES + tuple(names), refs)))
    L, D, C, F, R, N = z.L, z.D, z.C, z.F, z.R, CHUNKS
    ch = z.ch
    Q = R // SEGS
    dp = lax.axis_index("dp")
    me = lax.axis_index("tensor")
    core = lax.rem(me, 2)
    xi = me // 2
    other = 1 - xi
    sib = xi * 2 + 1 - core
    xnb = other * 2 + core

    inner = lax.rem(dp, 8)
    base = dp - inner
    y = lax.rem(inner, 2)
    line = inner // 2
    middle = (line == 1) | (line == 2)

    def on_line(place, row):
        return (base + 2 * place + row, me)

    y_peer = on_line(line, 1 - y)
    pair_peer = on_line(line + 1 - 2 * lax.rem(line, 2), y)
    cross_peer = on_line(3 - line, y)

    peers = [(dp, sib), (dp, xnb)]
    if z.reduce:
        peers += [y_peer, pair_peer, cross_peer]
    barrier = pltpu.get_barrier_semaphore()
    for peer in peers:
        pl.semaphore_signal(barrier, inc=1, device_id=peer, device_id_type=MESH)
    pl.semaphore_wait(barrier, len(peers))

    def remote(src, dst, send, recv, peer, pieces=1):
        def copy(source, target):
            return pltpu.make_async_remote_copy(
                src_ref=source,
                dst_ref=target,
                send_sem=send,
                recv_sem=recv,
                device_id=peer if isinstance(peer, tuple) else (dp, peer),
                device_id_type=MESH,
            )

        def start():
            lead = src.shape[0] if len(src.shape) == 3 else 1
            size = src.shape[-2] // pieces
            for first in range(lead):
                for k in range(pieces):
                    at = pl.ds(k * size, size)
                    if len(src.shape) == 3:
                        copy(src.at[first, at], dst.at[first, at]).start()
                    else:
                        copy(src.at[at], dst.at[at]).start()

        return types.SimpleNamespace(
            start=start,
            wait_recv=lambda: copy(src, dst).wait_recv(),
            wait_send=lambda: copy(src, dst).wait_send(),
            wait=lambda: copy(src, dst).wait(),
        )

    n_ffn = z.units - 4
    period = z.period

    def unit_of(u):
        s = u % period
        k = s // 2
        k = (k + n_ffn - z.fu) % n_ffn if k < n_ffn else k
        return L - 1 - u // period, k, slice((s % 2) * z.sub, (s % 2 + 1) * z.sub)

    half = line // 2

    def unit_copy(u, stage, even):
        l, k, rows = unit_of(u)
        slot = u % SLOTS
        both = r.wg.at[l, k, :, rows]
        if even:
            part = r.wg.at[l, k, half, rows]
            src, dst, peer = (
                (both, r.zfold.at[slot], pair_peer),
                (r.wg.at[l, k, 1 - half, rows], r.mland.at[slot], cross_peer),
                (part, r.yland.at[slot], y_peer),
                (part, part, cross_peer),
                (both, both, pair_peer),
            )[stage]
        else:
            mine = r.wg.at[l, k, y, rows]
            src, dst, peer = (
                (r.wg.at[l, k, 1 - y, rows], r.yland.at[slot], y_peer),
                (mine, r.zland.at[slot], pair_peer),
                (mine, r.mland.at[slot], cross_peer),
                (mine, r.zland.at[slot], pair_peer),
                (mine, mine, y_peer),
            )[stage]
        return remote(src, dst, r.us.at[u, stage], r.ur.at[u, stage], peer)

    def unit_land(u, stage, ref, peer):
        return remote(ref, ref, r.us.at[u, stage], r.ur.at[u, stage], peer)

    def unit_add(u, part, landed):
        l, k, rows = unit_of(u)
        r.wg[l, k, part, rows] = (r.wg[l, k, part, rows].astype(F32) + landed.astype(F32)).astype(BF16)

    def tell(sem, peer):
        pl.semaphore_signal(sem, inc=1, device_id=peer, device_id_type=MESH)

    def on_middle(body):
        pl.when(middle)(body)

    def on_end(body):
        pl.when(jnp.logical_not(middle))(body)

    def odd_stage(u, stage):
        copy = lambda n: unit_copy(u, n, False)
        slot = u % SLOTS
        l, k, rows = unit_of(u)
        if stage == 0:
            copy(0).start()
        if stage == 1:
            copy(0).wait_send()
            tell(r.freed.at[0], y_peer)
            copy(0).wait_recv()
            unit_add(u, y, r.yland[slot])
            on_end(lambda: copy(1).start())
        if stage == 2:

            @on_middle
            def _():
                copy(1).wait_recv()
                unit_add(u, y, r.zland[slot])
                copy(2).start()

        if stage == 3:

            @on_middle
            def _():
                copy(2).wait_recv()
                copy(2).wait_send()
                unit_add(u, y, r.mland[slot])
                copy(3).start()

        if stage == 4:

            @on_end
            def _():
                copy(1).wait_send()
                copy(3).wait_recv()
                r.wg[l, k, y, rows] = r.zland[slot]

            pl.semaphore_wait(r.freed.at[0], 1)
            copy(4).start()
        if stage == 5:
            unit_land(u, 4, r.wg.at[l, k, 1 - y, rows], y_peer).wait_recv()
            copy(4).wait_send()
            on_middle(lambda: copy(3).wait_send())
            unit_out(u).start()

    def even_stage(u, stage):
        copy = lambda n: unit_copy(u, n, True)
        slot = u % SLOTS
        l, k, rows = unit_of(u)
        if stage == 0:
            on_end(lambda: copy(0).start())
        if stage == 1:

            @on_end
            def _():
                copy(0).wait_send()
                tell(r.freed.at[1], pair_peer)

            @on_middle
            def _():
                copy(0).wait_recv()
                for part in range(2):
                    unit_add(u, part, r.zfold[slot, part])
                copy(1).start()

        if stage == 2:

            @on_middle
            def _():
                copy(1).wait_send()
                tell(r.freed.at[2], cross_peer)
                copy(1).wait_recv()
                unit_add(u, half, r.mland[slot])
                copy(2).start()

        if stage == 3:

            @on_middle
            def _():
                copy(2).wait_send()
                copy(2).wait_recv()
                unit_add(u, half, r.yland[slot])
                pl.semaphore_wait(r.freed.at[2], 1)
                copy(3).start()

        if stage == 4:

            @on_middle
            def _():
                unit_land(u, 3, r.wg.at[l, k, 1 - half, rows], cross_peer).wait_recv()
                pl.semaphore_wait(r.freed.at[1], 1)
                copy(4).start()

        if stage == 5:
            on_end(lambda: copy(4).wait_recv())

            @on_middle
            def _():
                copy(3).wait_send()
                copy(4).wait_send()

            unit_out(u).start()

    def unit_out(u):
        l, k, rows = unit_of(u)
        return pltpu.make_async_copy(r.wg.at[l, k, :, rows], r.wgout.at[l, k, :, rows], r.outs.at[u])

    clock = [0]
    last_tick = period * L + 5 * LAG

    def ticks(count, ready=None):
        for _ in range(count if z.reduce else 0):
            m = clock[0]
            if m >= last_tick or (ready is not None and m >= ready):
                return
            clock[0] = m + 1
            for stage in reversed(range(6)):
                u = m - LAG * stage
                if 0 <= u < period * L:
                    (even_stage if u % 2 == 0 else odd_stage)(u, stage)

    def ticks_in_loop(i, counts, ready):
        for at, count in enumerate(counts):
            if count:

                @pl.when(i == at)
                def _():
                    ticks(count, ready(at))

    def ag_copy(e, full, c, kind):
        chip = other if kind == 2 else xi
        peer = xnb if kind == 0 else sib
        ref = full.at[chip, c, core]
        return remote(ref, ref, r.ags.at[e, kind, c], r.agr.at[e, kind, c], peer, PIECES if kind == 0 else 1)

    def ag_landing(e, full, c, kind):
        chip = xi if kind == 1 else other
        col = core if kind == 0 else 1 - core
        ref = full.at[chip, c, col]
        return remote(ref, ref, r.ags.at[e, kind, c], r.agr.at[e, kind, c], sib)

    def ag_start(e, full, c):
        ag_copy(e, full, c, 0).start()
        ag_copy(e, full, c, 1).start()

    def ag_take_x(e, full, c):
        ag_landing(e, full, c, 0).wait_recv()
        ag_copy(e, full, c, 2).start()

    def rs_copy(e, c, kind):
        return remote(
            r.stage.at[r_side(e), kind, c],
            r.land.at[r_side(e), kind, c],
            r.rss.at[e, kind, c],
            r.rsr.at[e, kind, c],
            xnb if kind == 1 else sib,
            PIECES if kind == 1 else 1,
        )

    def r_side(e):
        return e // (2 * L)

    def rs_other(e, c):
        r.stage[r_side(e), 0, c] = r.psc[1 - core].astype(BF16)
        rs_copy(e, c, 0).start()
        r.xpart[c] = r.psc[core]

    def rs_pass(e, c):
        rs_copy(e, c, 0).wait_recv()
        r.stage[r_side(e), 1, c] = (r.xpart[c] + r.land[r_side(e), 0, c].astype(F32)).astype(BF16)
        rs_copy(e, c, 1).start()

    def rs_own(e, c):
        r.stage[r_side(e), 2, c] = r.psc[1 - core].astype(BF16)
        rs_copy(e, c, 2).start()
        r.opart[r_side(e), c] = r.psc[core]

    def rs_final(e, full, c):
        rs_copy(e, c, 2).wait_recv()
        rs_copy(e, c, 1).wait_recv()
        side = r_side(e)
        total = r.opart[side, c] + r.land[side, 2, c].astype(F32) + r.land[side, 1, c].astype(F32)
        for kind in range(3):
            rs_copy(e, c, kind).wait_send()
            ag_copy(e, full, c, kind).wait_send()
        return total

    def exchange_loop(e, full, order, send, stage, early=False):
        send(order(0))
        if early:

            def take(c):
                ag_landing(e, full, c, 1).wait_recv()
                ag_landing(e, full, c, 2).wait_recv()

            loop(N, take)

        def step(i):
            @pl.when(i + 1 < N)
            def _():
                send(order(i + 1))

            if not early:

                @pl.when(i < N)
                def _():
                    ag_landing(e, full, order(i), 1).wait_recv()

                @pl.when((i >= N - 1) & (i < 2 * N - 1))
                def _():
                    ag_take_x(e, full, order(i - N + 1))

                @pl.when(i >= N)
                def _():
                    ag_landing(e, full, order(i - N), 2).wait_recv()

            stage(i)

        loop(2 * N, step)

    def chip_chunk(i, order, own_first):
        first = i < N
        chunk = order(jnp.where(first, i, i - N))
        return jnp.where(first, xi, other) if own_first else jnp.where(first, other, xi), chunk

    def rs_step(e, i, order, own_first):
        first = i < N
        chunk = order(jnp.where(first, i, i - N))

        @pl.when(first if own_first else i >= N)
        def _():
            rs_own(e, chunk)

        @pl.when(i >= N if own_first else first)
        def _():
            rs_other(e, chunk)

        behind = (i - N if own_first else i) - 1

        @pl.when((behind >= 0) & (behind < N))
        def _():
            rs_pass(e, order(behind))

    ascending = lambda j: j
    descending = lambda j: N - 1 - j

    def norm_rows(s):
        return lax.rsqrt(jnp.mean(s * s, axis=-1, keepdims=True) + EPS_NORM)

    def group_sum(v):
        high = v.astype(BF16)
        rest = (v - high.astype(F32)).astype(BF16)
        weight = r.gsum[...]
        return (mm(high, weight) + mm(rest, weight)) * (1.0 / (2 * GROUP_CH))

    def fold(v):
        return jnp.sum(v.reshape(v.shape[0] // SEGS, SEGS, v.shape[1]), axis=0)

    def flat(v):
        return v.reshape(-1, v.shape[-1])

    w_copies = []
    for l in range(L):
        parts = (r.inw.at[l, 0], r.inw.at[l, 1], r.fw.at[l], r.gw.at[l, 0], r.gw.at[l, 1])
        pairs = [(part, r.wmix.at[l, pl.ds(k * C, ch), :]) for k, part in enumerate(parts)]
        pairs += [(r.ow.at[l, k], r.wout.at[l, pl.ds(k * C, ch), :]) for k in range(2)]
        pairs += [(r.ffw.at[l, k], r.wffn.at[l, :, pl.ds(k * F, F)]) for k in range(2)]
        pairs += [(r.dw.at[l], r.wdown.at[l])]
        w_copies += [
            pltpu.make_async_copy(src, dst, r.wsem.at[l, k]) for k, (src, dst) in enumerate(pairs)
        ]
    for copy in w_copies:
        copy.start()

    tokens = N * R
    r.st[0] = mm(permutation(tokens), r.x[...]).reshape(N, R, D)
    r.ngf[...] = r.ng[...].astype(F32)

    def send_first(c):
        s = r.st[0, c]
        r.mixfull[0, xi, c, core] = (s * norm_rows(s) * r.ngf[0, 0:1, :]).astype(BF16)
        ag_start(0, r.mixfull.at[0], c)

    loop(N, send_first)

    r.grad[...] = mm(permutation(tokens), r.ct[...]).reshape(N, R, D)
    first_grad = r.gfull.at[0]

    def keep_cotangent(c):
        first_grad[xi, c, core] = r.grad[c].astype(BF16)

    loop(N, keep_cotangent)
    width = tokens // SEGS
    for k in range(5):
        r.wmix[:, k * C + ch : (k + 1) * C, :] = jnp.zeros((L, C - ch, D), BF16)
    for k in range(2):
        r.wout[:, k * C + ch : (k + 1) * C, :] = jnp.zeros((L, C - ch, D), BF16)
    r.par[...] = jnp.zeros_like(r.par)
    r.gacc[...] = jnp.zeros_like(r.gacc)
    r.sacc[...] = jnp.zeros_like(r.sacc)
    for l in range(L):
        angle = r.ph[l : l + 1, :]
        turn_cos, turn_sin = jnp.cos(angle), jnp.sin(angle)
        r.par[l, 0:1, 0:ch] = turn_cos
        r.par[l, 1:2, 0:ch] = turn_sin
        r.par[l, 2:3, 0:ch] = sigmoid(r.bl[l : l + 1, :])
        r.par[l, 3:4, 0:ch] = r.gg[l, 0:1, :].astype(F32)
        r.par[l, 4:5, 0:ch] = r.gg[l, 1:2, :].astype(F32)
        for _ in range(width.bit_length() - 1):
            turn_cos, turn_sin = (
                turn_cos * turn_cos - turn_sin * turn_sin,
                2.0 * turn_cos * turn_sin,
            )
        r.par[l, 5:6, 0:ch] = turn_cos
        r.par[l, 6:7, 0:ch] = turn_sin
    gi, gj = iota((C, C), 0), iota((C, C), 1)
    same = (gi // GROUP_CH == gj // GROUP_CH) & (gi < ch) & (gj < ch)
    r.gsum[...] = jnp.where(same, 1.0, 0.0).astype(BF16)

    def rows_of(q):
        return slice(q * SEGS, (q + 1) * SEGS)

    def scan_local(l, chip, c, turn_cos, turn_sin):
        for k in range(2):
            h_re, h_im, prod = r.seg[0, chip, k], r.seg[1, chip, k], r.seg[2, chip, k]
            for q in range(Q):
                rate = r.keep[chip, c, k, rows_of(q), :]
                h_re, h_im = (
                    rate * (turn_cos * h_re - turn_sin * h_im) + r.drive[0, chip, c, k, rows_of(q), :],
                    rate * (turn_cos * h_im + turn_sin * h_re) + r.drive[1, chip, c, k, rows_of(q), :],
                )
                prod = prod * rate
            r.seg[0, chip, k], r.seg[1, chip, k], r.seg[2, chip, k] = h_re, h_im, prod

    def scan_final(l, chip, c, turn_cos, turn_sin):
        base = SEGS + c * R
        for k in range(2):
            h_re, h_im = r.cur[0, chip, k], r.cur[1, chip, k]
            for q in range(Q):
                rate = r.keep[chip, c, k, rows_of(q), :]
                h_re, h_im = (
                    rate * (turn_cos * h_re - turn_sin * h_im) + r.drive[0, chip, c, k, rows_of(q), :],
                    rate * (turn_cos * h_im + turn_sin * h_re) + r.drive[1, chip, c, k, rows_of(q), :],
                )
                at = pl.ds(pl.multiple_of(base + q * SEGS, SEGS), SEGS)
                r.state[l, 0, chip, k, at, :] = h_re
                r.state[l, 1, chip, k, at, :] = h_im
            r.cur[0, chip, k], r.cur[1, chip, k] = h_re, h_im

    def scan_back_local(l, chip, c, turn_cos, turn_sin):
        for k in range(2):
            u_re, u_im = r.seg[0, chip, k], r.seg[1, chip, k]
            for q in reversed(range(Q)):
                rate = r.keep[chip, c, k, rows_of(q), :]
                t_re = r.drive[0, chip, c, k, rows_of(q), :] + u_re
                t_im = r.drive[1, chip, c, k, rows_of(q), :] + u_im
                u_re = rate * (turn_cos * t_re + turn_sin * t_im)
                u_im = rate * (turn_cos * t_im - turn_sin * t_re)
            r.seg[0, chip, k], r.seg[1, chip, k] = u_re, u_im

    def scan_back_final(l, chip, c, turn_cos, turn_sin):
        for k in range(2):
            u_re, u_im = r.cur[0, chip, k], r.cur[1, chip, k]
            for q in reversed(range(Q)):
                rate = r.keep[chip, c, k, rows_of(q), :]
                t_re = r.drive[0, chip, c, k, rows_of(q), :] + u_re
                t_im = r.drive[1, chip, c, k, rows_of(q), :] + u_im
                r.tot[0, k, rows_of(q), :] = t_re
                r.tot[1, k, rows_of(q), :] = t_im
                u_re = rate * (turn_cos * t_re + turn_sin * t_im)
                u_im = rate * (turn_cos * t_im - turn_sin * t_re)
            r.cur[0, chip, k], r.cur[1, chip, k] = u_re, u_im

    def carry_over(l, back):
        all_cos, all_sin = r.par[l, 5:6, :], r.par[l, 6:7, :]
        if back:
            all_sin = -all_sin
        c_re = jnp.zeros((1, C), F32)
        c_im = jnp.zeros((1, C), F32)
        order = [(chip, k, s) for chip in range(2) for k in range(2) for s in range(SEGS)]
        for chip, k, s in reversed(order) if back else order:
            one = slice(s, s + 1)
            r.cur[0, chip, k, one, :] = c_re
            r.cur[1, chip, k, one, :] = c_im
            prod = r.segk[l, chip, k, one, :]
            c_re, c_im = (
                prod * (all_cos * c_re - all_sin * c_im) + r.seg[0, chip, k, one, :],
                prod * (all_cos * c_im + all_sin * c_re) + r.seg[1, chip, k, one, :],
            )

    def forward_layer(l):
        turn_cos, turn_sin, lower = r.par[l, 0:1, :], r.par[l, 1:2, :], r.par[l, 2:3, :]
        gain_re, gain_im = r.par[l, 3:4, :], r.par[l, 4:5, :]
        e = 2 * l
        full = r.mixfull.at[l]

        def send_mix(c):
            @pl.when(l > 0)
            def _():
                s = r.st[2 * l - 1, c] + rs_final(e - 1, r.ffnfull.at[l - 1], c)
                r.st[2 * l, c] = s
                full[xi, c, core] = (s * norm_rows(s) * r.ngf[l, 0:1, :]).astype(BF16)
                ag_start(e, full, c)

        @pl.when(l == 0)
        def _():
            for copy in w_copies:
                copy.wait()

        r.seg[0:2] = jnp.zeros((2, 2, 2, SEGS, C), F32)
        r.seg[2] = jnp.ones((2, 2, SEGS, C), F32)

        def project(j):
            chip, c = chip_chunk(j, ascending, True)
            proj = mm_nt(flat(full[chip, c]), r.wmix[l])
            r.proj[l, chip, c] = proj.reshape(2, R, 5 * C)
            in_re, in_im, pre = proj[:, 0:C], proj[:, C : 2 * C], proj[:, 2 * C : 3 * C]
            rate = lower + (1.0 - lower) * sigmoid(pre)
            r.keep[chip, c] = rate.reshape(2, R, C)
            r.drive[0, chip, c] = ((1.0 - rate) * in_re * sigmoid(in_re)).reshape(2, R, C)
            r.drive[1, chip, c] = ((1.0 - rate) * in_im * sigmoid(in_im)).reshape(2, R, C)
            scan_local(l, chip, c, turn_cos, turn_sin)

        exchange_loop(e, full, ascending, send_mix, project)

        def send_cotangent(i):
            ag_start(2 * L, first_grad, l * z.early + i)

        loop(z.early, send_cotangent)
        r.segk[l] = r.seg[2]
        carry_over(l, False)
        for part in range(2):
            r.state[l, part, :, :, 0:SEGS, :] = r.cur[part]

        def mix(j):
            chip, c = chip_chunk(j, ascending, False)
            scan_final(l, chip, c, turn_cos, turn_sin)
            at = pl.ds(pl.multiple_of(SEGS + c * R, SEGS), R)
            s_re = flat(r.state[l, 0, chip, :, at, :])
            s_im = flat(r.state[l, 1, chip, :, at, :])
            centre = group_sum(s_re + s_im)
            d_re, d_im = s_re - centre, s_im - centre
            scale = lax.rsqrt(group_sum(d_re * d_re + d_im * d_im) + EPS_GROUP)
            u_re, u_im = d_re * scale, d_im * scale
            r.unit[l, 0, chip, c] = u_re.reshape(2, R, C)
            r.unit[l, 1, chip, c] = u_im.reshape(2, R, C)
            r.inv[l, chip, c] = scale.reshape(2, R, C)
            gate_re = flat(r.proj[l, chip, c, :, :, 3 * C : 4 * C])
            gate_im = flat(r.proj[l, chip, c, :, :, 4 * C : 5 * C])
            m_re = (u_re * gain_re * sigmoid(gate_re)).astype(BF16)
            m_im = (u_im * gain_im * sigmoid(gate_im)).astype(BF16)
            r.mixed[l, chip, c, :, :, 0:C] = m_re.reshape(2, R, C)
            r.mixed[l, chip, c, :, :, C : 2 * C] = m_im.reshape(2, R, C)
            r.psc[...] = mm(flat(r.mixed[l, chip, c]), r.wout[l]).reshape(2, R, D)

            rs_step(e, j, ascending, False)

        loop(2 * N, mix)

        def take_cotangent(i):
            ag_take_x(2 * L, first_grad, l * z.early + i)

        loop(z.early, take_cotangent)
        e2 = e + 1
        full2 = r.ffnfull.at[l]

        def send_ffn(c):
            s = r.st[2 * l, c] + rs_final(e, full, c)
            r.st[2 * l + 1, c] = s
            full2[xi, c, core] = (s * norm_rows(s) * r.ngf[l, 1:2, :]).astype(BF16)
            ag_start(e2, full2, c)

        def feed(j):
            chip, c = chip_chunk(j, ascending, True)
            both = mm(flat(full2[chip, c]), r.wffn[l])
            r.gup[l, chip, c] = both.astype(BF16).reshape(2, R, 2 * F)
            gate, up = both[:, 0:F], both[:, F : 2 * F]
            hidden = (gate * sigmoid(gate) * up).astype(BF16)
            r.hidden[l, chip, c] = hidden.reshape(2, R, F)
            r.psc[...] = mm(hidden, r.wdown[l]).reshape(2, R, D)

            rs_step(e2, j, ascending, True)

        exchange_loop(e2, full2, ascending, send_ffn, feed)
        rs_pass(e2, N - 1)

    loop(L, forward_layer)

    def last_sum(c):
        e = 2 * L - 1
        s = r.st[2 * L - 1, c] + rs_final(e, r.ffnfull.at[L - 1], c)
        r.out[pl.ds(pl.multiple_of(c * R, R), R), :] = s.astype(BF16)

    def norm_back(l, which, c, grad_out):
        s = r.st[2 * l + which, c]
        scale = norm_rows(s)
        r.gacc[l, which] += fold(grad_out * s * scale)
        scaled = grad_out * r.ngf[l, which : which + 1, :]
        back = scale * scaled - s * (scale * scale * scale) * jnp.mean(
            scaled * s, axis=-1, keepdims=True
        )
        r.grad[c] = r.grad[c] + back

    def backward_layer(step):
        l = L - 1 - step
        e = 2 * L + 2 * step
        full = r.gfull.at[0]

        base = step * period
        pace = PACE[min(step, 1)]

        def send_ffn(c):
            if step > 0:
                norm_back(l + 1, 0, c, rs_final(e - 1, r.gfull.at[1], c))
                full[xi, c, core] = r.grad[c].astype(BF16)
                ag_start(e, full, c)

        def feed_back(j):
            chip, c = chip_chunk(j, descending, step > 0)
            g_hidden = mm_nt(flat(full[chip, c]), r.wdown[l])
            both = flat(r.gup[l, chip, c]).astype(F32)
            gate, up = both[:, 0:F], both[:, F : 2 * F]
            s = sigmoid(gate)
            g_gate = (g_hidden * up * s * (1.0 + gate * (1.0 - s))).astype(BF16)
            g_up = (g_hidden * gate * s).astype(BF16)
            r.dgu[chip, c, :, :, 0:F] = g_gate.reshape(2, R, F)
            r.dgu[chip, c, :, :, F : 2 * F] = g_up.reshape(2, R, F)
            r.psc[...] = mm_nt(flat(r.dgu[chip, c]), r.wffn[l]).reshape(2, R, D)

            rs_step(e, j, descending, step > 0)

            @pl.when(j == (2 * N - 1 if step > 0 else 0))
            def _():
                part = mm_tn(flat(r.hidden[l]), flat(full[...])).astype(BF16)
                r.wg[l, n_ffn - z.fu : n_ffn] = part.reshape(z.fu, 2, z.blk, D)

            ticks_in_loop(j, pace["feed"], lambda at: base + (4 if step == 0 or at == 2 * N - 1 else 0))

        exchange_loop(e, full, descending, send_ffn, feed_back, step == 0)
        if step > 0:
            rs_pass(e, 0)
        else:
            loop(N, last_sum)

        def ffn_tile(i):
            cols = pl.ds(pl.multiple_of(i * F, LANES), F)
            part = mm_tn(flat(r.ffnfull[l, :, :, :, :, cols]), flat(r.dgu[...])).astype(BF16)
            r.wg[l, pl.ds(i * z.fu, z.fu)] = part.reshape(z.fu, 2, z.blk, D)

        ticks(pace["feed_end"], base + 4)
        loop(D // F, ffn_tile)
        ticks(pace["ffn_end"], base + 12)

        turn_cos, turn_sin, lower = r.par[l, 0:1, :], r.par[l, 1:2, :], r.par[l, 2:3, :]
        gain_re, gain_im = r.par[l, 3:4, :], r.par[l, 4:5, :]
        e2 = e + 1
        full2 = r.gfull.at[1]

        def send_mix(c):
            norm_back(l, 1, c, rs_final(e, full, c))
            full2[xi, c, core] = r.grad[c].astype(BF16)
            ag_start(e2, full2, c)

        r.seg[0:2] = jnp.zeros((2, 2, 2, SEGS, C), F32)

        def mix_back(j):
            chip, c = chip_chunk(j, descending, True)
            g_both = mm_nt(flat(full2[chip, c]), r.wout[l])
            g_re, g_im = g_both[:, 0:C], g_both[:, C : 2 * C]
            s_re = sigmoid(flat(r.proj[l, chip, c, :, :, 3 * C : 4 * C]))
            s_im = sigmoid(flat(r.proj[l, chip, c, :, :, 4 * C : 5 * C]))
            u_re, u_im = flat(r.unit[l, 0, chip, c]), flat(r.unit[l, 1, chip, c])
            n_re, n_im = g_re * s_re, g_im * s_im
            r.sacc[l, 0] += fold(n_re * u_re)
            r.sacc[l, 1] += fold(n_im * u_im)
            x_re, x_im = n_re * gain_re, n_im * gain_im
            cross_re, cross_im = x_re * u_re, x_im * u_im
            r.dproj[chip, c, :, :, 3 * C : 4 * C] = (cross_re * (1.0 - s_re)).astype(BF16).reshape(2, R, C)
            r.dproj[chip, c, :, :, 4 * C : 5 * C] = (cross_im * (1.0 - s_im)).astype(BF16).reshape(2, R, C)
            mean_one = group_sum(x_re + x_im)
            mean_two = group_sum(cross_re + cross_im)
            scale = flat(r.inv[l, chip, c])
            r.drive[0, chip, c] = (scale * (x_re - mean_one - u_re * mean_two)).reshape(2, R, C)
            r.drive[1, chip, c] = (scale * (x_im - mean_one - u_im * mean_two)).reshape(2, R, C)
            pre = flat(r.proj[l, chip, c, :, :, 2 * C : 3 * C])
            r.keep[chip, c] = (lower + (1.0 - lower) * sigmoid(pre)).reshape(2, R, C)
            scan_back_local(l, chip, c, turn_cos, turn_sin)

            ticks_in_loop(j, pace["mix"], lambda at: base + 12)

        exchange_loop(e2, full2, descending, send_mix, mix_back)
        carry_over(l, True)

        def scan_back(j):
            chip, c = chip_chunk(j, descending, False)
            scan_back_final(l, chip, c, turn_cos, turn_sin)
            t_re, t_im = flat(r.tot[0]), flat(r.tot[1])
            at = pl.ds(pl.multiple_of(c * R, SEGS), R)
            p_re = flat(r.state[l, 0, chip, :, at, :])
            p_im = flat(r.state[l, 1, chip, :, at, :])
            in_re = flat(r.proj[l, chip, c, :, :, 0:C])
            in_im = flat(r.proj[l, chip, c, :, :, C : 2 * C])
            fs = sigmoid(flat(r.proj[l, chip, c, :, :, 2 * C : 3 * C]))
            rate = lower + (1.0 - lower) * fs
            s_re, s_im = sigmoid(in_re), sigmoid(in_im)
            gc_re = t_re * p_re + t_im * p_im
            gc_im = t_im * p_re - t_re * p_im
            g_keep = gc_re * turn_cos + gc_im * turn_sin - (t_re * in_re * s_re + t_im * in_im * s_im)
            r.sacc[l, 2] += fold(rate * (gc_im * turn_cos - gc_re * turn_sin))
            r.sacc[l, 3] += fold(g_keep * (1.0 - fs))
            d_re = t_re * (1.0 - rate) * s_re * (1.0 + in_re * (1.0 - s_re))
            d_im = t_im * (1.0 - rate) * s_im * (1.0 + in_im * (1.0 - s_im))
            d_f = g_keep * (1.0 - lower) * fs * (1.0 - fs)
            r.dproj[chip, c, :, :, 0:C] = d_re.astype(BF16).reshape(2, R, C)
            r.dproj[chip, c, :, :, C : 2 * C] = d_im.astype(BF16).reshape(2, R, C)
            r.dproj[chip, c, :, :, 2 * C : 3 * C] = d_f.astype(BF16).reshape(2, R, C)
            r.psc[...] = mm(flat(r.dproj[chip, c]), r.wmix[l]).reshape(2, R, D)

            rs_step(e2, j, descending, False)

            @pl.when(j == N)
            def _():
                loop(2, out_tile)
                loop(2, gate_tile)

            ticks_in_loop(j, pace["scan"], lambda at: base + (12 if at < N else 16))

        base_unit = z.units - 4

        def out_tile(i):
            cols = pl.ds(pl.multiple_of(i * C, LANES), C)
            part = mm_tn(flat(r.mixed[l, :, :, :, :, cols]), flat(full2[...])).astype(BF16)
            r.wg[l, base_unit, i] = part[0:ch]

        def proj_tile(k, unit, block):
            cols = pl.ds(pl.multiple_of(k * C, LANES), C)
            part = mm_tn(flat(r.dproj[:, :, :, :, cols]), flat(r.mixfull[l])).astype(BF16)
            r.wg[l, unit, block] = part[0:ch]

        def gate_tile(i):
            proj_tile(3 + i, base_unit + 1, i)

        def in_tile(i):
            proj_tile(i, base_unit + 2, i)

        def forget_tile():
            part = mm_tn(flat(r.dproj[:, :, :, :, 2 * C : 3 * C]), flat(r.mixfull[l])).astype(BF16)
            for half in range(2):
                r.wg[l, base_unit + 3, half, 0 : z.sub] = part[half * z.sub : (half + 1) * z.sub]

        loop(2 * N, scan_back)
        loop(2, in_tile)
        forget_tile()
        ticks(pace["end"], base + period)

    for step in range(L):
        backward_layer(step)

    def last_grad(j):
        c = descending(j)
        norm_back(0, 0, c, rs_final(4 * L - 1, r.gfull.at[1], c))

    ticks(AHEAD)
    loop(N, last_grad)
    r.ig[...] = r.grad[...].reshape(tokens, D).astype(BF16)

    r.swork[...] = jnp.zeros_like(r.swork)
    for l in range(L):
        for which in range(2):
            at = 2 * l + which
            r.swork[at : at + 1, :] = jnp.sum(r.gacc[l, which], axis=0, keepdims=True)

    for l in range(L):
        for k in range(4):
            value = jnp.sum(r.sacc[l, k], axis=0, keepdims=True)
            if k == 3:
                lower = r.par[l, 2:3, :]
                value = value * lower * (1.0 - lower)
            at = 2 * L + 4 * l + k
            r.swork[at : at + 1, 0:C] = value

    swap_peers = [sib, xnb] + ([y_peer, pair_peer, cross_peer] if z.reduce else [])
    n_swaps = len(swap_peers)

    def swap(k):
        return remote(r.swork, r.sland.at[k], r.ss.at[k], r.sr.at[k], swap_peers[k])

    for i in range(max(n_swaps + 1, last_tick - clock[0])):
        if 1 <= i <= n_swaps:
            k = i - 1
            swap(k).wait()
            rows = 2 * L if k < 2 else 2 * SEGS
            r.swork[0:rows, :] = r.swork[0:rows, :] + r.sland[k, 0:rows, :]
        if i < n_swaps:
            swap(i).start()
        ticks(1)
    r.sums[...] = r.swork[...]

    for u in range(period * L):
        if not z.reduce:
            unit_out(u).start()
        unit_out(u).wait()


def finish(z, n_tensor, out, ig, sums, w_in, w_forget, w_gate, w_out, w_ffn, w_down, *o):
    L, ch, F = z.L, z.ch, z.F
    l, i = pl.program_id(0), pl.program_id(1)
    tokens = out.shape[0]

    @pl.when((l == 0) & (i == 0))
    def _():
        o[0][...] = mm_tn(permutation(tokens), out[...]).astype(BF16)
        me = lax.axis_index("tensor")
        piece = z.D // n_tensor
        for t in range(n_tensor):

            @pl.when(me == t)
            def _():
                for k in range(L):
                    o[2][k] = sums[2 * k : 2 * k + 2, t * piece : (t + 1) * piece]

        for k in range(L):
            at = 2 * L + 4 * k
            o[7][k : k + 1, :] = sums[at + 2 : at + 3, 0:ch]
            o[8][k : k + 1, :] = sums[at + 3 : at + 4, 0:ch]
            o[9][k] = sums[at : at + 2, 0:ch]

    @pl.when((l == 0) & (i == 1))
    def _():
        o[1][...] = mm_tn(permutation(tokens), ig[...]).astype(BF16)

    o[3][...] = w_in[...].astype(F32)
    o[4][...] = w_forget[...].astype(F32)
    o[5][...] = w_gate[...].astype(F32)
    o[6][...] = w_out[...].astype(F32)
    o[10][0, 0] = w_ffn[0, :, 0:F].astype(F32)
    o[10][0, 1] = w_ffn[0, :, F : 2 * F].astype(F32)
    o[11][...] = w_down[...].astype(F32)


def local(*args):
    x, ct, ng, inw, fw, gw, ow, ph, bl, gg, ffw, dw = args
    L, D = ng.shape[0], ng.shape[2]
    ch = fw.shape[2]
    F = dw.shape[1]
    C = -(-ch // LANES) * LANES
    n_dp = lax.axis_size("dp")
    reduce = n_dp % 8 == 0
    fu = F // (2 * ch)
    units = fu * (1 + D // F) + 4
    sub = ch // 2
    period = 2 * units - 1
    z = types.SimpleNamespace(
        L=L, D=D, C=C, F=F, ch=ch, R=x.shape[0] // CHUNKS, reduce=reduce, blk=ch, fu=fu, units=units, sub=sub, period=period
    )
    z.early = CHUNKS // L
    names, scratch = scratch_of(z)
    vmem = pl.BlockSpec(memory_space=pltpu.VMEM)
    anywhere = pl.BlockSpec(memory_space=pl.ANY)
    in_specs = [vmem] * 12
    for k in (3, 4, 5, 6, 10, 11):
        in_specs[k] = anywhere
    shape = jax.ShapeDtypeStruct
    out, ig, wg, sums = pl.pallas_call(
        functools.partial(mega, z, names),
        out_shape=(
            shape(x.shape, BF16),
            shape(x.shape, BF16),
            shape((L, units, 2, ch, D), BF16),
            shape((2 * SEGS, D), F32),
        ),
        in_specs=in_specs,
        out_specs=[vmem, vmem, anywhere, vmem],
        scratch_shapes=scratch,
        compiler_params=pltpu.CompilerParams(
            collective_id=0, has_side_effects=True, vmem_limit_bytes=VMEM_BYTES
        ),
        name="layers",
    )(x, ct, ng, jnp.swapaxes(inw, 2, 3), jnp.swapaxes(fw, 1, 2), jnp.swapaxes(gw, 2, 3), ow, ph, bl, gg, ffw, dw)

    if not reduce:
        wg, sums = lax.psum((wg, sums), "dp")
    elif n_dp > 8:
        groups = [list(range(k, n_dp, 8)) for k in range(8)]
        wg, sums = lax.psum((wg, sums), "dp", axis_index_groups=groups)
    n_tensor = lax.axis_size("tensor")
    blocks = wg.reshape(L, 2 * units, ch, D)
    rows = wg.reshape(L, 2 * units * ch, D)
    G = 3
    piece = ch // G

    def block_spec(count, index):
        return pl.BlockSpec((1, count, piece, D), lambda l, i: (l, index, i, 0))

    def part_spec(index):
        return pl.BlockSpec((1, 2, sub // G, D), lambda l, i: (l, index, i, 0))

    def row_spec(size, index):
        return pl.BlockSpec((1, size, D), lambda l, i: (l, index + i, 0))

    def whole(*dims):
        return pl.BlockSpec(dims, lambda l, i: (0,) * len(dims))

    first = 2 * (units - 4)
    res = pl.pallas_call(
        functools.partial(finish, z, n_tensor),
        grid=(L, G),
        out_shape=(
            shape(x.shape, BF16),
            shape(x.shape, BF16),
            shape((L, 2, D // n_tensor), F32),
            shape((L, 2, ch, D), F32),
            shape((L, 2, sub, D), F32),
            shape((L, 2, ch, D), F32),
            shape((L, 2, ch, D), F32),
            shape((L, ch), F32),
            shape((L, ch), F32),
            shape((L, 2, ch), F32),
            shape((L, 2, D, F), F32),
            shape((L, F, D), F32),
        ),
        in_specs=[
            whole(*x.shape),
            whole(*x.shape),
            whole(2 * SEGS, D),
            block_spec(2, first // 2 + 2),
            part_spec(first // 2 + 3),
            block_spec(2, first // 2 + 1),
            block_spec(2, first // 2),
            row_spec(D // G, 0),
            row_spec(F // G, D // (F // G)),
        ],
        out_specs=[
            whole(*x.shape),
            whole(*x.shape),
            whole(L, 2, D // n_tensor),
            block_spec(2, 0),
            part_spec(0),
            block_spec(2, 0),
            block_spec(2, 0),
            whole(L, ch),
            whole(L, ch),
            whole(L, 2, ch),
            pl.BlockSpec((1, 2, D // G, F), lambda l, i: (l, 0, i, 0)),
            row_spec(F // G, 0),
        ],
        compiler_params=pltpu.CompilerParams(vmem_limit_bytes=VMEM_BYTES),
        name="finish",
    )(out, ig, sums, blocks, blocks, blocks, blocks, rows, rows)
    res = list(res)
    res[3] = jnp.swapaxes(res[3], 2, 3)
    res[4] = jnp.swapaxes(res[4].reshape(L, ch, D), 1, 2)
    res[5] = jnp.swapaxes(res[5], 2, 3)
    return tuple(res)


def solution(mesh):
    tokens = P(("dp", "tensor"), None)
    return jax.shard_map(
        local,
        mesh=mesh,
        in_specs=(
            tokens,
            tokens,
            P(),
            P(None, None, None, "tensor"),
            P(None, None, "tensor"),
            P(None, None, None, "tensor"),
            P(None, None, "tensor", None),
            P(None, "tensor"),
            P(None, "tensor"),
            P(None, None, "tensor"),
            P(None, None, None, "tensor"),
            P(None, "tensor", None),
        ),
        out_specs=(
            tokens,
            tokens,
            P(None, None, "tensor"),
            P(None, None, None, "tensor"),
            P(None, None, "tensor"),
            P(None, None, None, "tensor"),
            P(None, None, "tensor", None),
            P(None, "tensor"),
            P(None, "tensor"),
            P(None, None, "tensor"),
            P(None, None, None, "tensor"),
            P(None, "tensor", None),
        ),
        check_vma=False,
    )
```

```python
import functools
import types

import jax
import jax.numpy as jnp
from jax import lax
from jax.experimental import pallas as pl
from jax.experimental.pallas import tpu as pltpu
from jax.sharding import PartitionSpec as P

MESH = pl.DeviceIdType.MESH
F32 = jnp.float32
BF16 = jnp.bfloat16

GROUP_CH = 48
EPS_NORM = 1e-06
EPS_GROUP = 1e-05
LANES = 128
SEGS = 8
CHUNKS = 4
LAG = 2
PACE = (
    dict(feed=(1, 0, 0, 0, 1, 0, 0, 1), feed_end=0, ffn_end=1, mix=(1, 0, 1, 0, 1, 1, 1, 1), scan=(0, 1, 0, 1, 1, 0, 1, 0), end=2),
    dict(feed=(1, 0, 1, 0, 1, 0, 0, 1), feed_end=1, ffn_end=2, mix=(1, 0, 1, 0, 1, 1, 1, 1), scan=(0, 1, 0, 1, 1, 0, 1, 0), end=2),
)
AHEAD = 4
PIECES = 2
SLOTS = 10
VMEM_BYTES = 63 * 1024 * 1024


def sigmoid(v):
    return 0.5 * jnp.tanh(0.5 * v) + 0.5


def mm(left, right):
    return jnp.dot(left, right, preferred_element_type=F32)


def mm_nt(left, right):
    return lax.dot_general(left, right, (((1,), (1,)), ((), ())), preferred_element_type=F32)


def mm_tn(left, right):
    return lax.dot_general(left, right, (((0,), (0,)), ((), ())), preferred_element_type=F32)


def loop(count, body):
    def step(index, carry):
        body(index)
        return carry

    lax.fori_loop(0, count, step, 0)


def iota(shape, dim):
    return lax.broadcasted_iota(jnp.int32, shape, dim)


def permutation(tokens):
    width = tokens // SEGS
    row = iota((tokens, tokens), 0)
    place = lax.rem(row, SEGS) * width + row // SEGS
    return jnp.where(iota((tokens, tokens), 1) == place, 1.0, 0.0).astype(BF16)


def scratch_of(z):
    L, D, C, F, R, N = z.L, z.D, z.C, z.F, z.R, CHUNKS
    rows = (2, N, 2, R)
    own = (N, R)
    bufs = dict(
        wmix=((L, 5 * C, D), BF16),
        wout=((L, 2 * C, D), BF16),
        wffn=((L, D, 2 * F), BF16),
        par=((L, 8, C), F32),
        ngf=((L, 2, D), F32),
        gsum=((C, C), BF16),
        st=((2 * L, *own, D), F32),
        mixfull=((L, *rows, D), BF16),
        ffnfull=((L, *rows, D), BF16),
        gfull=((2, *rows, D), BF16),
        proj=((L, *rows, 5 * C), F32),
        state=((L, 2, 2, 2, SEGS + N * R, C), F32),
        unit=((L, 2, *rows, C), F32),
        inv=((L, *rows, C), F32),
        mixed=((L, *rows, 2 * C), BF16),
        gup=((L, *rows, 2 * F), BF16),
        hidden=((L, *rows, F), BF16),
        keep=((*rows, C), F32),
        drive=((2, *rows, C), F32),
        seg=((3, 2, 2, SEGS, C), F32),
        segk=((L, 2, 2, SEGS, C), F32),
        cur=((2, 2, 2, SEGS, C), F32),
        tot=((2, 2, R, C), F32),
        dgu=((*rows, 2 * F), BF16),
        dproj=((*rows, 5 * C), BF16),
        psc=((2, R, D), F32),
        xpart=((2, *own, D), F32),
        opart=((2, *own, D), F32),
        grad=((*own, D), F32),
        stage=((2, 3, *own, D), BF16),
        land=((2, 3, *own, D), BF16),
        gacc=((L, 2, SEGS, D), F32),
        sacc=((L, 4, SEGS, C), F32),
        wdown=((L, F, D), BF16),
        wg=((L, z.units, 2, z.blk, D), BF16),
        swork=((2 * SEGS, D), F32),
        sland=((5, 2 * SEGS, D), F32),
    )
    if z.reduce:
        unit = (SLOTS, z.sub, D)
        bufs.update(yland=(unit, BF16), mland=(unit, BF16))
        bufs.update(zland=(unit, BF16), zfold=((SLOTS, 2, z.sub, D), BF16))
    sems = dict(
        ags=(4 * L, 3, N),
        agr=(4 * L, 3, N),
        rss=(4 * L, 3, N),
        rsr=(4 * L, 3, N),
        wsem=(L, 10),
        ss=(5,),
        sr=(5,),
        outs=(z.period * L,),
    )
    if z.reduce:
        sems.update(us=(z.period * L, 5), ur=(z.period * L, 5))
    names = list(bufs) + list(sems)
    shapes = [pltpu.VMEM(s, d) for s, d in bufs.values()]
    shapes += [pltpu.SemaphoreType.DMA(s) for s in sems.values()]
    names.append("freed")
    shapes.append(pltpu.SemaphoreType.REGULAR((3,)))
    return names, shapes


IN_NAMES = ("x", "ct", "ng", "inw", "fw", "gw", "ow", "ph", "bl", "gg", "ffw", "dw")
OUT_NAMES = ("out", "ig", "wgout", "sums")


def mega(z, names, *refs):
    r = types.SimpleNamespace(**dict(zip(IN_NAMES + OUT_NAMES + tuple(names), refs)))
    L, D, C, F, R, N = z.L, z.D, z.C, z.F, z.R, CHUNKS
    ch = z.ch
    Q = R // SEGS
    dp = lax.axis_index("dp")
    me = lax.axis_index("tensor")
    core = lax.rem(me, 2)
    xi = me // 2
    other = 1 - xi
    sib = xi * 2 + 1 - core
    xnb = other * 2 + core

    inner = lax.rem(dp, 8)
    base = dp - inner
    y = lax.rem(inner, 2)
    line = inner // 2
    middle = (line == 1) | (line == 2)

    def on_line(place, row):
        return (base + 2 * place + row, me)

    y_peer = on_line(line, 1 - y)
    pair_peer = on_line(line + 1 - 2 * lax.rem(line, 2), y)
    cross_peer = on_line(3 - line, y)

    peers = [(dp, sib), (dp, xnb)]
    if z.reduce:
        peers += [y_peer, pair_peer, cross_peer]
    barrier = pltpu.get_barrier_semaphore()
    for peer in peers:
        pl.semaphore_signal(barrier, inc=1, device_id=peer, device_id_type=MESH)

    def remote(src, dst, send, recv, peer, pieces=1):
        def copy(source, target):
            return pltpu.make_async_remote_copy(
                src_ref=source,
                dst_ref=target,
                send_sem=send,
                recv_sem=recv,
                device_id=peer if isinstance(peer, tuple) else (dp, peer),
                device_id_type=MESH,
            )

        def start():
            lead = src.shape[0] if len(src.shape) == 3 else 1
            size = src.shape[-2] // pieces
            for first in range(lead):
                for k in range(pieces):
                    at = pl.ds(k * size, size)
                    if len(src.shape) == 3:
                        copy(src.at[first, at], dst.at[first, at]).start()
                    else:
                        copy(src.at[at], dst.at[at]).start()

        return types.SimpleNamespace(
            start=start,
            wait_recv=lambda: copy(src, dst).wait_recv(),
            wait_send=lambda: copy(src, dst).wait_send(),
            wait=lambda: copy(src, dst).wait(),
        )

    n_ffn = z.units - 4
    period = z.period

    def unit_of(u):
        s = u % period
        k = s // 2
        k = (k + n_ffn - z.fu) % n_ffn if k < n_ffn else k
        return L - 1 - u // period, k, slice((s % 2) * z.sub, (s % 2 + 1) * z.sub)

    half = line // 2

    def unit_copy(u, stage, even):
        l, k, rows = unit_of(u)
        slot = u % SLOTS
        both = r.wg.at[l, k, :, rows]
        if even:
            part = r.wg.at[l, k, half, rows]
            src, dst, peer = (
                (both, r.zfold.at[slot], pair_peer),
                (r.wg.at[l, k, 1 - half, rows], r.mland.at[slot], cross_peer),
                (part, r.yland.at[slot], y_peer),
                (part, part, cross_peer),
                (both, both, pair_peer),
            )[stage]
        else:
            mine = r.wg.at[l, k, y, rows]
            src, dst, peer = (
                (r.wg.at[l, k, 1 - y, rows], r.yland.at[slot], y_peer),
                (mine, r.zland.at[slot], pair_peer),
                (mine, r.mland.at[slot], cross_peer),
                (mine, r.zland.at[slot], pair_peer),
                (mine, mine, y_peer),
            )[stage]
        return remote(src, dst, r.us.at[u, stage], r.ur.at[u, stage], peer)

    def unit_land(u, stage, ref, peer):
        return remote(ref, ref, r.us.at[u, stage], r.ur.at[u, stage], peer)

    def unit_add(u, part, landed):
        l, k, rows = unit_of(u)
        r.wg[l, k, part, rows] = (r.wg[l, k, part, rows].astype(F32) + landed.astype(F32)).astype(BF16)

    def tell(sem, peer):
        pl.semaphore_signal(sem, inc=1, device_id=peer, device_id_type=MESH)

    def on_middle(body):
        pl.when(middle)(body)

    def on_end(body):
        pl.when(jnp.logical_not(middle))(body)

    def odd_stage(u, stage):
        copy = lambda n: unit_copy(u, n, False)
        slot = u % SLOTS
        l, k, rows = unit_of(u)
        if stage == 0:
            copy(0).start()
        if stage == 1:
            copy(0).wait_send()
            tell(r.freed.at[0], y_peer)
            copy(0).wait_recv()
            unit_add(u, y, r.yland[slot])
            on_end(lambda: copy(1).start())
        if stage == 2:

            @on_middle
            def _():
                copy(1).wait_recv()
                unit_add(u, y, r.zland[slot])
                copy(2).start()

        if stage == 3:

            @on_middle
            def _():
                copy(2).wait_recv()
                copy(2).wait_send()
                unit_add(u, y, r.mland[slot])
                copy(3).start()

        if stage == 4:

            @on_end
            def _():
                copy(1).wait_send()
                copy(3).wait_recv()
                r.wg[l, k, y, rows] = r.zland[slot]

            pl.semaphore_wait(r.freed.at[0], 1)
            copy(4).start()
        if stage == 5:
            unit_land(u, 4, r.wg.at[l, k, 1 - y, rows], y_peer).wait_recv()
            copy(4).wait_send()
            on_middle(lambda: copy(3).wait_send())
            unit_out(u).start()

    def even_stage(u, stage):
        copy = lambda n: unit_copy(u, n, True)
        slot = u % SLOTS
        l, k, rows = unit_of(u)
        if stage == 0:
            on_end(lambda: copy(0).start())
        if stage == 1:

            @on_end
            def _():
                copy(0).wait_send()
                tell(r.freed.at[1], pair_peer)

            @on_middle
            def _():
                copy(0).wait_recv()
                for part in range(2):
                    unit_add(u, part, r.zfold[slot, part])
                copy(1).start()

        if stage == 2:

            @on_middle
            def _():
                copy(1).wait_send()
                tell(r.freed.at[2], cross_peer)
                copy(1).wait_recv()
                unit_add(u, half, r.mland[slot])
                copy(2).start()

        if stage == 3:

            @on_middle
            def _():
                copy(2).wait_send()
                copy(2).wait_recv()
                unit_add(u, half, r.yland[slot])
                pl.semaphore_wait(r.freed.at[2], 1)
                copy(3).start()

        if stage == 4:

            @on_middle
            def _():
                unit_land(u, 3, r.wg.at[l, k, 1 - half, rows], cross_peer).wait_recv()
                pl.semaphore_wait(r.freed.at[1], 1)
                copy(4).start()

        if stage == 5:
            on_end(lambda: copy(4).wait_recv())

            @on_middle
            def _():
                copy(3).wait_send()
                copy(4).wait_send()

            unit_out(u).start()

    def unit_out(u):
        l, k, rows = unit_of(u)
        return pltpu.make_async_copy(r.wg.at[l, k, :, rows], r.wgout.at[l, k, :, rows], r.outs.at[u])

    clock = [0]
    last_tick = period * L + 5 * LAG

    def ticks(count, ready=None):
        for _ in range(count if z.reduce else 0):
            m = clock[0]
            if m >= last_tick or (ready is not None and m >= ready):
                return
            clock[0] = m + 1
            for stage in reversed(range(6)):
                u = m - LAG * stage
                if 0 <= u < period * L:
                    (even_stage if u % 2 == 0 else odd_stage)(u, stage)

    def ticks_in_loop(i, counts, ready):
        for at, count in enumerate(counts):
            if count:

                @pl.when(i == at)
                def _():
                    ticks(count, ready(at))

    def ag_copy(e, full, c, kind):
        chip = other if kind == 2 else xi
        peer = xnb if kind == 0 else sib
        ref = full.at[chip, c, core]
        return remote(ref, ref, r.ags.at[e, kind, c], r.agr.at[e, kind, c], peer, PIECES if kind == 0 else 1)

    def ag_landing(e, full, c, kind):
        chip = xi if kind == 1 else other
        col = core if kind == 0 else 1 - core
        ref = full.at[chip, c, col]
        return remote(ref, ref, r.ags.at[e, kind, c], r.agr.at[e, kind, c], sib)

    def ag_start(e, full, c):
        ag_copy(e, full, c, 0).start()
        ag_copy(e, full, c, 1).start()

    def ag_take_x(e, full, c):
        ag_landing(e, full, c, 0).wait_recv()
        ag_copy(e, full, c, 2).start()

    def rs_copy(e, c, kind):
        return remote(
            r.stage.at[r_side(e), kind, c],
            r.land.at[r_side(e), kind, c],
            r.rss.at[e, kind, c],
            r.rsr.at[e, kind, c],
            xnb if kind == 1 else sib,
            PIECES if kind == 1 else 1,
        )

    def r_side(e):
        return e // (2 * L)

    def rs_other(e, c):
        r.stage[r_side(e), 0, c] = r.psc[1 - core].astype(BF16)
        rs_copy(e, c, 0).start()
        r.xpart[r_side(e), c] = r.psc[core]

    def rs_pass(e, c):
        rs_copy(e, c, 0).wait_recv()
        r.stage[r_side(e), 1, c] = (r.xpart[r_side(e), c] + r.land[r_side(e), 0, c].astype(F32)).astype(BF16)
        rs_copy(e, c, 1).start()

    def rs_own(e, c):
        r.stage[r_side(e), 2, c] = r.psc[1 - core].astype(BF16)
        rs_copy(e, c, 2).start()
        r.opart[r_side(e), c] = r.psc[core]

    def rs_final(e, full, c):
        rs_copy(e, c, 2).wait_recv()
        rs_copy(e, c, 1).wait_recv()
        side = r_side(e)
        total = r.opart[side, c] + r.land[side, 2, c].astype(F32) + r.land[side, 1, c].astype(F32)
        for kind in range(3):
            rs_copy(e, c, kind).wait_send()
            ag_copy(e, full, c, kind).wait_send()
        return total

    def exchange_loop(e, full, order, send, stage, early=False):
        send(order(0))
        if early:

            def take(c):
                ag_landing(e, full, c, 1).wait_recv()
                ag_landing(e, full, c, 2).wait_recv()

            loop(N, take)

        def step(i):
            @pl.when(i + 1 < N)
            def _():
                send(order(i + 1))

            if not early:

                @pl.when(i < N)
                def _():
                    ag_landing(e, full, order(i), 1).wait_recv()

                @pl.when((i >= N - 1) & (i < 2 * N - 1))
                def _():
                    ag_take_x(e, full, order(i - N + 1))

                @pl.when(i >= N)
                def _():
                    ag_landing(e, full, order(i - N), 2).wait_recv()

            stage(i)

        loop(2 * N, step)

    def chip_chunk(i, order, own_first):
        first = i < N
        chunk = order(jnp.where(first, i, i - N))
        return jnp.where(first, xi, other) if own_first else jnp.where(first, other, xi), chunk

    def rs_step(e, i, order, own_first, go=True):
        first = i < N
        chunk = order(jnp.where(first, i, i - N))

        @pl.when(first if own_first else i >= N)
        def _():
            rs_own(e, chunk)

        @pl.when(i >= N if own_first else first)
        def _():
            rs_other(e, chunk)

        behind = (i - N if own_first else i) - 1

        @pl.when((behind >= 0) & (behind < N) & go)
        def _():
            rs_pass(e, order(behind))

    ascending = lambda j: j
    descending = lambda j: N - 1 - j

    def norm_rows(s):
        return lax.rsqrt(jnp.mean(s * s, axis=-1, keepdims=True) + EPS_NORM)

    def group_sum(v):
        high = v.astype(BF16)
        rest = (v - high.astype(F32)).astype(BF16)
        weight = r.gsum[...]
        return (mm(high, weight) + mm(rest, weight)) * (1.0 / (2 * GROUP_CH))

    def fold(v):
        return jnp.sum(v.reshape(v.shape[0] // SEGS, SEGS, v.shape[1]), axis=0)

    def flat(v):
        return v.reshape(-1, v.shape[-1])

    w_copies = []
    for l in range(L):
        parts = (r.inw.at[l, 0], r.inw.at[l, 1], r.fw.at[l], r.gw.at[l, 0], r.gw.at[l, 1])
        pairs = [(part, r.wmix.at[l, pl.ds(k * C, ch), :]) for k, part in enumerate(parts)]
        pairs += [(r.ow.at[l, k], r.wout.at[l, pl.ds(k * C, ch), :]) for k in range(2)]
        pairs += [(r.ffw.at[l, k], r.wffn.at[l, :, pl.ds(k * F, F)]) for k in range(2)]
        pairs += [(r.dw.at[l], r.wdown.at[l])]
        w_copies += [
            pltpu.make_async_copy(src, dst, r.wsem.at[l, k]) for k, (src, dst) in enumerate(pairs)
        ]
    for copy in w_copies:
        copy.start()

    tokens = N * R
    r.st[0] = mm(permutation(tokens), r.x[...]).reshape(N, R, D)
    r.ngf[...] = r.ng[...].astype(F32)

    def norm_first(c):
        s = r.st[0, c]
        r.mixfull[0, xi, c, core] = (s * norm_rows(s) * r.ngf[0, 0:1, :]).astype(BF16)

    loop(N, norm_first)
    pl.semaphore_wait(barrier, len(peers))
    loop(N, lambda c: ag_start(0, r.mixfull.at[0], c))

    r.grad[...] = mm(permutation(tokens), r.ct[...]).reshape(N, R, D)
    first_grad = r.gfull.at[0]

    def keep_cotangent(c):
        first_grad[xi, c, core] = r.grad[c].astype(BF16)

    loop(N, keep_cotangent)
    width = tokens // SEGS
    for k in range(5):
        r.wmix[:, k * C + ch : (k + 1) * C, :] = jnp.zeros((L, C - ch, D), BF16)
    for k in range(2):
        r.wout[:, k * C + ch : (k + 1) * C, :] = jnp.zeros((L, C - ch, D), BF16)
    r.par[...] = jnp.zeros_like(r.par)
    r.gacc[...] = jnp.zeros_like(r.gacc)
    r.sacc[...] = jnp.zeros_like(r.sacc)
    for l in range(L):
        angle = r.ph[l : l + 1, :]
        turn_cos, turn_sin = jnp.cos(angle), jnp.sin(angle)
        r.par[l, 0:1, 0:ch] = turn_cos
        r.par[l, 1:2, 0:ch] = turn_sin
        r.par[l, 2:3, 0:ch] = sigmoid(r.bl[l : l + 1, :])
        r.par[l, 3:4, 0:ch] = r.gg[l, 0:1, :].astype(F32)
        r.par[l, 4:5, 0:ch] = r.gg[l, 1:2, :].astype(F32)
        for _ in range(width.bit_length() - 1):
            turn_cos, turn_sin = (
                turn_cos * turn_cos - turn_sin * turn_sin,
                2.0 * turn_cos * turn_sin,
            )
        r.par[l, 5:6, 0:ch] = turn_cos
        r.par[l, 6:7, 0:ch] = turn_sin
    gi, gj = iota((C, C), 0), iota((C, C), 1)
    same = (gi // GROUP_CH == gj // GROUP_CH) & (gi < ch) & (gj < ch)
    r.gsum[...] = jnp.where(same, 1.0, 0.0).astype(BF16)

    def rows_of(q):
        return slice(q * SEGS, (q + 1) * SEGS)

    def scan_local(l, chip, c, turn_cos, turn_sin):
        for k in range(2):
            h_re, h_im, prod = r.seg[0, chip, k], r.seg[1, chip, k], r.seg[2, chip, k]
            for q in range(Q):
                rate = r.keep[chip, c, k, rows_of(q), :]
                h_re, h_im = (
                    rate * (turn_cos * h_re - turn_sin * h_im) + r.drive[0, chip, c, k, rows_of(q), :],
                    rate * (turn_cos * h_im + turn_sin * h_re) + r.drive[1, chip, c, k, rows_of(q), :],
                )
                prod = prod * rate
            r.seg[0, chip, k], r.seg[1, chip, k], r.seg[2, chip, k] = h_re, h_im, prod

    def scan_final(l, chip, c, turn_cos, turn_sin):
        base = SEGS + c * R
        for k in range(2):
            h_re, h_im = r.cur[0, chip, k], r.cur[1, chip, k]
            for q in range(Q):
                rate = r.keep[chip, c, k, rows_of(q), :]
                h_re, h_im = (
                    rate * (turn_cos * h_re - turn_sin * h_im) + r.drive[0, chip, c, k, rows_of(q), :],
                    rate * (turn_cos * h_im + turn_sin * h_re) + r.drive[1, chip, c, k, rows_of(q), :],
                )
                at = pl.ds(pl.multiple_of(base + q * SEGS, SEGS), SEGS)
                r.state[l, 0, chip, k, at, :] = h_re
                r.state[l, 1, chip, k, at, :] = h_im
            r.cur[0, chip, k], r.cur[1, chip, k] = h_re, h_im

    def scan_back_local(l, chip, c, turn_cos, turn_sin):
        for k in range(2):
            u_re, u_im = r.seg[0, chip, k], r.seg[1, chip, k]
            for q in reversed(range(Q)):
                rate = r.keep[chip, c, k, rows_of(q), :]
                t_re = r.drive[0, chip, c, k, rows_of(q), :] + u_re
                t_im = r.drive[1, chip, c, k, rows_of(q), :] + u_im
                u_re = rate * (turn_cos * t_re + turn_sin * t_im)
                u_im = rate * (turn_cos * t_im - turn_sin * t_re)
            r.seg[0, chip, k], r.seg[1, chip, k] = u_re, u_im

    def scan_back_final(l, chip, c, turn_cos, turn_sin):
        for k in range(2):
            u_re, u_im = r.cur[0, chip, k], r.cur[1, chip, k]
            for q in reversed(range(Q)):
                rate = r.keep[chip, c, k, rows_of(q), :]
                t_re = r.drive[0, chip, c, k, rows_of(q), :] + u_re
                t_im = r.drive[1, chip, c, k, rows_of(q), :] + u_im
                r.tot[0, k, rows_of(q), :] = t_re
                r.tot[1, k, rows_of(q), :] = t_im
                u_re = rate * (turn_cos * t_re + turn_sin * t_im)
                u_im = rate * (turn_cos * t_im - turn_sin * t_re)
            r.cur[0, chip, k], r.cur[1, chip, k] = u_re, u_im

    def carry_over(l, back):
        all_cos, all_sin = r.par[l, 5:6, :], r.par[l, 6:7, :]
        if back:
            all_sin = -all_sin
        c_re = jnp.zeros((1, C), F32)
        c_im = jnp.zeros((1, C), F32)
        order = [(chip, k, s) for chip in range(2) for k in range(2) for s in range(SEGS)]
        for chip, k, s in reversed(order) if back else order:
            one = slice(s, s + 1)
            r.cur[0, chip, k, one, :] = c_re
            r.cur[1, chip, k, one, :] = c_im
            prod = r.segk[l, chip, k, one, :]
            c_re, c_im = (
                prod * (all_cos * c_re - all_sin * c_im) + r.seg[0, chip, k, one, :],
                prod * (all_cos * c_im + all_sin * c_re) + r.seg[1, chip, k, one, :],
            )

    def forward_layer(l):
        turn_cos, turn_sin, lower = r.par[l, 0:1, :], r.par[l, 1:2, :], r.par[l, 2:3, :]
        gain_re, gain_im = r.par[l, 3:4, :], r.par[l, 4:5, :]
        e = 2 * l
        full = r.mixfull.at[l]

        def send_mix(c):
            @pl.when(l > 0)
            def _():
                s = r.st[2 * l - 1, c] + rs_final(e - 1, r.ffnfull.at[l - 1], c)
                r.st[2 * l, c] = s
                full[xi, c, core] = (s * norm_rows(s) * r.ngf[l, 0:1, :]).astype(BF16)
                ag_start(e, full, c)

        @pl.when(l == 0)
        def _():
            for copy in w_copies:
                copy.wait()

        r.seg[0:2] = jnp.zeros((2, 2, 2, SEGS, C), F32)
        r.seg[2] = jnp.ones((2, 2, SEGS, C), F32)

        def project(j):
            chip, c = chip_chunk(j, ascending, True)
            proj = mm_nt(flat(full[chip, c]), r.wmix[l])
            r.proj[l, chip, c] = proj.reshape(2, R, 5 * C)
            in_re, in_im, pre = proj[:, 0:C], proj[:, C : 2 * C], proj[:, 2 * C : 3 * C]
            rate = lower + (1.0 - lower) * sigmoid(pre)
            r.keep[chip, c] = rate.reshape(2, R, C)
            r.drive[0, chip, c] = ((1.0 - rate) * in_re * sigmoid(in_re)).reshape(2, R, C)
            r.drive[1, chip, c] = ((1.0 - rate) * in_im * sigmoid(in_im)).reshape(2, R, C)
            scan_local(l, chip, c, turn_cos, turn_sin)

        exchange_loop(e, full, ascending, send_mix, project)

        def send_cotangent(i):
            ag_start(2 * L, first_grad, l * z.early + i)

        loop(z.early, send_cotangent)
        r.segk[l] = r.seg[2]
        carry_over(l, False)
        for part in range(2):
            r.state[l, part, :, :, 0:SEGS, :] = r.cur[part]

        def mix(j):
            chip, c = chip_chunk(j, ascending, False)
            scan_final(l, chip, c, turn_cos, turn_sin)
            at = pl.ds(pl.multiple_of(SEGS + c * R, SEGS), R)
            s_re = flat(r.state[l, 0, chip, :, at, :])
            s_im = flat(r.state[l, 1, chip, :, at, :])
            centre = group_sum(s_re + s_im)
            d_re, d_im = s_re - centre, s_im - centre
            scale = lax.rsqrt(group_sum(d_re * d_re + d_im * d_im) + EPS_GROUP)
            u_re, u_im = d_re * scale, d_im * scale
            r.unit[l, 0, chip, c] = u_re.reshape(2, R, C)
            r.unit[l, 1, chip, c] = u_im.reshape(2, R, C)
            r.inv[l, chip, c] = scale.reshape(2, R, C)
            gate_re = flat(r.proj[l, chip, c, :, :, 3 * C : 4 * C])
            gate_im = flat(r.proj[l, chip, c, :, :, 4 * C : 5 * C])
            m_re = (u_re * gain_re * sigmoid(gate_re)).astype(BF16)
            m_im = (u_im * gain_im * sigmoid(gate_im)).astype(BF16)
            r.mixed[l, chip, c, :, :, 0:C] = m_re.reshape(2, R, C)
            r.mixed[l, chip, c, :, :, C : 2 * C] = m_im.reshape(2, R, C)
            r.psc[...] = mm(flat(r.mixed[l, chip, c]), r.wout[l]).reshape(2, R, D)

            rs_step(e, j, ascending, False)

        loop(2 * N, mix)

        def take_cotangent(i):
            ag_take_x(2 * L, first_grad, l * z.early + i)

        loop(z.early, take_cotangent)
        e2 = e + 1
        full2 = r.ffnfull.at[l]

        def send_ffn(c):
            s = r.st[2 * l, c] + rs_final(e, full, c)
            r.st[2 * l + 1, c] = s
            full2[xi, c, core] = (s * norm_rows(s) * r.ngf[l, 1:2, :]).astype(BF16)
            ag_start(e2, full2, c)

        def feed(j):
            chip, c = chip_chunk(j, ascending, True)
            both = mm(flat(full2[chip, c]), r.wffn[l])
            r.gup[l, chip, c] = both.astype(BF16).reshape(2, R, 2 * F)
            gate, up = both[:, 0:F], both[:, F : 2 * F]
            hidden = (gate * sigmoid(gate) * up).astype(BF16)
            r.hidden[l, chip, c] = hidden.reshape(2, R, F)
            r.psc[...] = mm(hidden, r.wdown[l]).reshape(2, R, D)

            rs_step(e2, j, ascending, True, l < L - 1)

        exchange_loop(e2, full2, ascending, send_ffn, feed)

        @pl.when(l < L - 1)
        def _():
            rs_pass(e2, N - 1)

    loop(L, forward_layer)

    def last_sum(c):
        e = 2 * L - 1
        s = r.st[2 * L - 1, c] + rs_final(e, r.ffnfull.at[L - 1], c)
        r.out[pl.ds(pl.multiple_of(c * R, R), R), :] = s.astype(BF16)

    def norm_back(l, which, c, grad_out):
        s = r.st[2 * l + which, c]
        scale = norm_rows(s)
        r.gacc[l, which] += fold(grad_out * s * scale)
        scaled = grad_out * r.ngf[l, which : which + 1, :]
        back = scale * scaled - s * (scale * scale * scale) * jnp.mean(
            scaled * s, axis=-1, keepdims=True
        )
        r.grad[c] = r.grad[c] + back

    def backward_layer(step):
        l = L - 1 - step
        e = 2 * L + 2 * step
        full = r.gfull.at[0]

        base = step * period
        pace = PACE[min(step, 1)]

        def send_ffn(c):
            if step > 0:
                norm_back(l + 1, 0, c, rs_final(e - 1, r.gfull.at[1], c))
                full[xi, c, core] = r.grad[c].astype(BF16)
                ag_start(e, full, c)

        def feed_back(j):
            chip, c = chip_chunk(j, descending, step > 0)
            g_hidden = mm_nt(flat(full[chip, c]), r.wdown[l])
            both = flat(r.gup[l, chip, c]).astype(F32)
            gate, up = both[:, 0:F], both[:, F : 2 * F]
            s = sigmoid(gate)
            g_gate = (g_hidden * up * s * (1.0 + gate * (1.0 - s))).astype(BF16)
            g_up = (g_hidden * gate * s).astype(BF16)
            r.dgu[chip, c, :, :, 0:F] = g_gate.reshape(2, R, F)
            r.dgu[chip, c, :, :, F : 2 * F] = g_up.reshape(2, R, F)
            r.psc[...] = mm_nt(flat(r.dgu[chip, c]), r.wffn[l]).reshape(2, R, D)

            rs_step(e, j, descending, step > 0)

            @pl.when(j == (2 * N - 1 if step > 0 else 0))
            def _():
                part = mm_tn(flat(r.hidden[l]), flat(full[...])).astype(BF16)
                r.wg[l, n_ffn - z.fu : n_ffn] = part.reshape(z.fu, 2, z.blk, D)

            ticks_in_loop(j, pace["feed"], lambda at: base + (4 if step == 0 or at == 2 * N - 1 else 0))

        exchange_loop(e, full, descending, send_ffn, feed_back, step == 0)
        if step > 0:
            rs_pass(e, 0)

        def ffn_tile(i):
            cols = pl.ds(pl.multiple_of(i * F, LANES), F)
            part = mm_tn(flat(r.ffnfull[l, :, :, :, :, cols]), flat(r.dgu[...])).astype(BF16)
            r.wg[l, pl.ds(i * z.fu, z.fu)] = part.reshape(z.fu, 2, z.blk, D)

        ticks(pace["feed_end"], base + 4)
        loop(D // F, ffn_tile)
        ticks(pace["ffn_end"], base + 12)

        turn_cos, turn_sin, lower = r.par[l, 0:1, :], r.par[l, 1:2, :], r.par[l, 2:3, :]
        gain_re, gain_im = r.par[l, 3:4, :], r.par[l, 4:5, :]
        e2 = e + 1
        full2 = r.gfull.at[1]

        def send_mix(c):
            norm_back(l, 1, c, rs_final(e, full, c))
            full2[xi, c, core] = r.grad[c].astype(BF16)
            ag_start(e2, full2, c)

        r.seg[0:2] = jnp.zeros((2, 2, 2, SEGS, C), F32)

        def mix_back(j):
            chip, c = chip_chunk(j, descending, True)
            g_both = mm_nt(flat(full2[chip, c]), r.wout[l])
            g_re, g_im = g_both[:, 0:C], g_both[:, C : 2 * C]
            s_re = sigmoid(flat(r.proj[l, chip, c, :, :, 3 * C : 4 * C]))
            s_im = sigmoid(flat(r.proj[l, chip, c, :, :, 4 * C : 5 * C]))
            u_re, u_im = flat(r.unit[l, 0, chip, c]), flat(r.unit[l, 1, chip, c])
            n_re, n_im = g_re * s_re, g_im * s_im
            r.sacc[l, 0] += fold(n_re * u_re)
            r.sacc[l, 1] += fold(n_im * u_im)
            x_re, x_im = n_re * gain_re, n_im * gain_im
            cross_re, cross_im = x_re * u_re, x_im * u_im
            r.dproj[chip, c, :, :, 3 * C : 4 * C] = (cross_re * (1.0 - s_re)).astype(BF16).reshape(2, R, C)
            r.dproj[chip, c, :, :, 4 * C : 5 * C] = (cross_im * (1.0 - s_im)).astype(BF16).reshape(2, R, C)
            mean_one = group_sum(x_re + x_im)
            mean_two = group_sum(cross_re + cross_im)
            scale = flat(r.inv[l, chip, c])
            r.drive[0, chip, c] = (scale * (x_re - mean_one - u_re * mean_two)).reshape(2, R, C)
            r.drive[1, chip, c] = (scale * (x_im - mean_one - u_im * mean_two)).reshape(2, R, C)
            pre = flat(r.proj[l, chip, c, :, :, 2 * C : 3 * C])
            r.keep[chip, c] = (lower + (1.0 - lower) * sigmoid(pre)).reshape(2, R, C)
            scan_back_local(l, chip, c, turn_cos, turn_sin)

            ticks_in_loop(j, pace["mix"], lambda at: base + 12)

        exchange_loop(e2, full2, descending, send_mix, mix_back)
        carry_over(l, True)

        def scan_back(j):
            chip, c = chip_chunk(j, descending, False)
            scan_back_final(l, chip, c, turn_cos, turn_sin)
            t_re, t_im = flat(r.tot[0]), flat(r.tot[1])
            at = pl.ds(pl.multiple_of(c * R, SEGS), R)
            p_re = flat(r.state[l, 0, chip, :, at, :])
            p_im = flat(r.state[l, 1, chip, :, at, :])
            in_re = flat(r.proj[l, chip, c, :, :, 0:C])
            in_im = flat(r.proj[l, chip, c, :, :, C : 2 * C])
            fs = sigmoid(flat(r.proj[l, chip, c, :, :, 2 * C : 3 * C]))
            rate = lower + (1.0 - lower) * fs
            s_re, s_im = sigmoid(in_re), sigmoid(in_im)
            gc_re = t_re * p_re + t_im * p_im
            gc_im = t_im * p_re - t_re * p_im
            g_keep = gc_re * turn_cos + gc_im * turn_sin - (t_re * in_re * s_re + t_im * in_im * s_im)
            r.sacc[l, 2] += fold(rate * (gc_im * turn_cos - gc_re * turn_sin))
            r.sacc[l, 3] += fold(g_keep * (1.0 - fs))
            d_re = t_re * (1.0 - rate) * s_re * (1.0 + in_re * (1.0 - s_re))
            d_im = t_im * (1.0 - rate) * s_im * (1.0 + in_im * (1.0 - s_im))
            d_f = g_keep * (1.0 - lower) * fs * (1.0 - fs)
            r.dproj[chip, c, :, :, 0:C] = d_re.astype(BF16).reshape(2, R, C)
            r.dproj[chip, c, :, :, C : 2 * C] = d_im.astype(BF16).reshape(2, R, C)
            r.dproj[chip, c, :, :, 2 * C : 3 * C] = d_f.astype(BF16).reshape(2, R, C)
            r.psc[...] = mm(flat(r.dproj[chip, c]), r.wmix[l]).reshape(2, R, D)

            rs_step(e2, j, descending, False)

            @pl.when(j == N)
            def _():
                loop(2, out_tile)
                loop(2, gate_tile)

            ticks_in_loop(j, pace["scan"], lambda at: base + (12 if at < N else 16))

        base_unit = z.units - 4

        def out_tile(i):
            cols = pl.ds(pl.multiple_of(i * C, LANES), C)
            part = mm_tn(flat(r.mixed[l, :, :, :, :, cols]), flat(full2[...])).astype(BF16)
            r.wg[l, base_unit, i] = part[0:ch]

        def proj_tile(k, unit, block):
            cols = pl.ds(pl.multiple_of(k * C, LANES), C)
            part = mm_tn(flat(r.dproj[:, :, :, :, cols]), flat(r.mixfull[l])).astype(BF16)
            r.wg[l, unit, block] = part[0:ch]

        def gate_tile(i):
            proj_tile(3 + i, base_unit + 1, i)

        def in_tile(i):
            proj_tile(i, base_unit + 2, i)

        def forget_tile():
            part = mm_tn(flat(r.dproj[:, :, :, :, 2 * C : 3 * C]), flat(r.mixfull[l])).astype(BF16)
            for half in range(2):
                r.wg[l, base_unit + 3, half, 0 : z.sub] = part[half * z.sub : (half + 1) * z.sub]

        loop(2 * N, scan_back)
        loop(2, in_tile)
        forget_tile()
        if step == L - 1:
            loop(N, lambda c: rs_pass(2 * L - 1, c))
        ticks(pace["end"], base + period)

    for step in range(L):
        backward_layer(step)

    def last_grad(j):
        c = descending(j)
        norm_back(0, 0, c, rs_final(4 * L - 1, r.gfull.at[1], c))

    ticks(AHEAD)
    loop(N, last_grad)
    r.ig[...] = r.grad[...].reshape(tokens, D).astype(BF16)

    r.swork[...] = jnp.zeros_like(r.swork)
    for l in range(L):
        for which in range(2):
            at = 2 * l + which
            r.swork[at : at + 1, :] = jnp.sum(r.gacc[l, which], axis=0, keepdims=True)

    for l in range(L):
        for k in range(4):
            value = jnp.sum(r.sacc[l, k], axis=0, keepdims=True)
            if k == 3:
                lower = r.par[l, 2:3, :]
                value = value * lower * (1.0 - lower)
            at = 2 * L + 4 * l + k
            r.swork[at : at + 1, 0:C] = value

    swap_peers = [sib, xnb] + ([y_peer, pair_peer, cross_peer] if z.reduce else [])
    n_swaps = len(swap_peers)

    def swap(k):
        return remote(r.swork, r.sland.at[k], r.ss.at[k], r.sr.at[k], swap_peers[k])

    for i in range(max(n_swaps + 1, last_tick - clock[0])):
        if 1 <= i <= n_swaps:
            k = i - 1
            swap(k).wait()
            rows = 2 * L if k < 2 else 2 * SEGS
            r.swork[0:rows, :] = r.swork[0:rows, :] + r.sland[k, 0:rows, :]
        if i < n_swaps:
            swap(i).start()
        ticks(1)
    loop(N, last_sum)
    r.sums[...] = r.swork[...]

    for u in range(period * L):
        if not z.reduce:
            unit_out(u).start()
        unit_out(u).wait()


def finish(z, n_tensor, out, ig, sums, w_in, w_forget, w_gate, w_out, w_ffn, w_down, *o):
    L, ch, F = z.L, z.ch, z.F
    l, i = pl.program_id(0), pl.program_id(1)
    tokens = out.shape[0]

    @pl.when((l == 0) & (i == 0))
    def _():
        o[0][...] = mm_tn(permutation(tokens), out[...]).astype(BF16)
        me = lax.axis_index("tensor")
        piece = z.D // n_tensor
        for t in range(n_tensor):

            @pl.when(me == t)
            def _():
                for k in range(L):
                    o[2][k] = sums[2 * k : 2 * k + 2, t * piece : (t + 1) * piece]

        for k in range(L):
            at = 2 * L + 4 * k
            o[7][k : k + 1, :] = sums[at + 2 : at + 3, 0:ch]
            o[8][k : k + 1, :] = sums[at + 3 : at + 4, 0:ch]
            o[9][k] = sums[at : at + 2, 0:ch]

    @pl.when((l == L - 1) & (i == 0))
    def _():
        o[1][...] = mm_tn(permutation(tokens), ig[...]).astype(BF16)

    o[3][...] = w_in[...].astype(F32)
    o[4][...] = w_forget[...].astype(F32)
    o[5][...] = w_gate[...].astype(F32)
    o[6][...] = w_out[...].astype(F32)
    o[10][0, 0] = w_ffn[0, :, 0:F].astype(F32)
    o[10][0, 1] = w_ffn[0, :, F : 2 * F].astype(F32)
    o[11][...] = w_down[...].astype(F32)


def local(*args):
    x, ct, ng, inw, fw, gw, ow, ph, bl, gg, ffw, dw = args
    L, D = ng.shape[0], ng.shape[2]
    ch = fw.shape[2]
    F = dw.shape[1]
    C = -(-ch // LANES) * LANES
    n_dp = lax.axis_size("dp")
    reduce = n_dp % 8 == 0
    fu = F // (2 * ch)
    units = fu * (1 + D // F) + 4
    sub = ch // 2
    period = 2 * units - 1
    z = types.SimpleNamespace(
        L=L, D=D, C=C, F=F, ch=ch, R=x.shape[0] // CHUNKS, reduce=reduce, blk=ch, fu=fu, units=units, sub=sub, period=period
    )
    z.early = CHUNKS // L
    names, scratch = scratch_of(z)
    vmem = pl.BlockSpec(memory_space=pltpu.VMEM)
    anywhere = pl.BlockSpec(memory_space=pl.ANY)
    in_specs = [vmem] * 12
    for k in (3, 4, 5, 6, 10, 11):
        in_specs[k] = anywhere
    shape = jax.ShapeDtypeStruct
    out, ig, wg, sums = pl.pallas_call(
        functools.partial(mega, z, names),
        out_shape=(
            shape(x.shape, BF16),
            shape(x.shape, BF16),
            shape((L, units, 2, ch, D), BF16),
            shape((2 * SEGS, D), F32),
        ),
        in_specs=in_specs,
        out_specs=[vmem, vmem, anywhere, vmem],
        scratch_shapes=scratch,
        compiler_params=pltpu.CompilerParams(
            collective_id=0, has_side_effects=True, vmem_limit_bytes=VMEM_BYTES
        ),
        name="layers",
    )(x, ct, ng, jnp.swapaxes(inw, 2, 3), jnp.swapaxes(fw, 1, 2), jnp.swapaxes(gw, 2, 3), ow, ph, bl, gg, ffw, dw)

    if not reduce:
        wg, sums = lax.psum((wg, sums), "dp")
    elif n_dp > 8:
        groups = [list(range(k, n_dp, 8)) for k in range(8)]
        wg, sums = lax.psum((wg, sums), "dp", axis_index_groups=groups)
    n_tensor = lax.axis_size("tensor")
    blocks = wg.reshape(L, 2 * units, ch, D)
    rows = wg.reshape(L, 2 * units * ch, D)
    G = 1
    piece = ch // G

    def block_spec(count, index):
        return pl.BlockSpec((1, count, piece, D), lambda l, i: (l, index, i, 0))

    def part_spec(index):
        return pl.BlockSpec((1, 2, sub // G, D), lambda l, i: (l, index, i, 0))

    def row_spec(size, index):
        return pl.BlockSpec((1, size, D), lambda l, i: (l, index + i, 0))

    def whole(*dims):
        return pl.BlockSpec(dims, lambda l, i: (0,) * len(dims))

    first = 2 * (units - 4)
    res = pl.pallas_call(
        functools.partial(finish, z, n_tensor),
        grid=(L, G),
        out_shape=(
            shape(x.shape, BF16),
            shape(x.shape, BF16),
            shape((L, 2, D // n_tensor), F32),
            shape((L, 2, ch, D), F32),
            shape((L, 2, sub, D), F32),
            shape((L, 2, ch, D), F32),
            shape((L, 2, ch, D), F32),
            shape((L, ch), F32),
            shape((L, ch), F32),
            shape((L, 2, ch), F32),
            shape((L, 2, D, F), F32),
            shape((L, F, D), F32),
        ),
        in_specs=[
            whole(*x.shape),
            whole(*x.shape),
            whole(2 * SEGS, D),
            block_spec(2, first // 2 + 2),
            part_spec(first // 2 + 3),
            block_spec(2, first // 2 + 1),
            block_spec(2, first // 2),
            row_spec(D // G, 0),
            row_spec(F // G, D // (F // G)),
        ],
        out_specs=[
            whole(*x.shape),
            whole(*x.shape),
            whole(L, 2, D // n_tensor),
            block_spec(2, 0),
            part_spec(0),
            block_spec(2, 0),
            block_spec(2, 0),
            whole(L, ch),
            whole(L, ch),
            whole(L, 2, ch),
            pl.BlockSpec((1, 2, D // G, F), lambda l, i: (l, 0, i, 0)),
            row_spec(F // G, 0),
        ],
        compiler_params=pltpu.CompilerParams(vmem_limit_bytes=VMEM_BYTES),
        name="finish",
    )(out, ig, sums, blocks, blocks, blocks, blocks, rows, rows)
    res = list(res)
    res[3] = jnp.swapaxes(res[3], 2, 3)
    res[4] = jnp.swapaxes(res[4].reshape(L, ch, D), 1, 2)
    res[5] = jnp.swapaxes(res[5], 2, 3)
    return tuple(res)


def solution(mesh):
    tokens = P(("dp", "tensor"), None)
    return jax.shard_map(
        local,
        mesh=mesh,
        in_specs=(
            tokens,
            tokens,
            P(),
            P(None, None, None, "tensor"),
            P(None, None, "tensor"),
            P(None, None, None, "tensor"),
            P(None, None, "tensor", None),
            P(None, "tensor"),
            P(None, "tensor"),
            P(None, None, "tensor"),
            P(None, None, None, "tensor"),
            P(None, "tensor", None),
        ),
        out_specs=(
            tokens,
            tokens,
            P(None, None, "tensor"),
            P(None, None, None, "tensor"),
            P(None, None, "tensor"),
            P(None, None, None, "tensor"),
            P(None, None, "tensor", None),
            P(None, "tensor"),
            P(None, "tensor"),
            P(None, None, "tensor"),
            P(None, None, None, "tensor"),
            P(None, "tensor", None),
        ),
        check_vma=False,
    )
```

```python
import functools
import types

import jax
import jax.numpy as jnp
from jax import lax
from jax.experimental import pallas as pl
from jax.experimental.pallas import tpu as pltpu
from jax.sharding import PartitionSpec as P

MESH = pl.DeviceIdType.MESH
F32 = jnp.float32
BF16 = jnp.bfloat16

GROUP_CH = 48
EPS_NORM = 1e-06
EPS_GROUP = 1e-05
LANES = 128
SEGS = 8
CHUNKS = 4
LAG = 2
PACE = (
    dict(feed=(1, 0, 0, 0, 1, 0, 0, 1), feed_end=0, ffn_end=1, mix=(1, 0, 1, 0, 1, 1, 1, 1), scan=(0, 0, 1, 1, 0, 1, 1, 0), end=1),
    dict(feed=(1, 1, 1, 0, 1, 0, 0, 1), feed_end=1, ffn_end=2, mix=(1, 0, 1, 0, 1, 1, 1, 1), scan=(0, 1, 0, 1, 1, 0, 1, 0), end=2),
)
AHEAD = 6
PIECES = 2
SLOTS = 10
VMEM_BYTES = 63 * 1024 * 1024


def sigmoid(v):
    return 0.5 * jnp.tanh(0.5 * v) + 0.5


def mm(left, right):
    return jnp.dot(left, right, preferred_element_type=F32)


def mm_nt(left, right):
    return lax.dot_general(left, right, (((1,), (1,)), ((), ())), preferred_element_type=F32)


def mm_tn(left, right):
    return lax.dot_general(left, right, (((0,), (0,)), ((), ())), preferred_element_type=F32)


def loop(count, body):
    def step(index, carry):
        body(index)
        return carry

    lax.fori_loop(0, count, step, 0)


def iota(shape, dim):
    return lax.broadcasted_iota(jnp.int32, shape, dim)


def permutation(tokens):
    width = tokens // SEGS
    row = iota((tokens, tokens), 0)
    place = lax.rem(row, SEGS) * width + row // SEGS
    return jnp.where(iota((tokens, tokens), 1) == place, 1.0, 0.0).astype(BF16)


def scratch_of(z):
    L, D, C, F, R, N = z.L, z.D, z.C, z.F, z.R, CHUNKS
    rows = (2, N, 2, R)
    own = (N, R)
    bufs = dict(
        wmix=((L, 5 * C, D), BF16),
        wout=((L, 2 * C, D), BF16),
        wffn=((L, D, 2 * F), BF16),
        par=((L, 8, C), F32),
        ngf=((L, 2, D), F32),
        gsum=((C, C), BF16),
        st=((2 * L, *own, D), F32),
        mixfull=((L, *rows, D), BF16),
        ffnfull=((L, *rows, D), BF16),
        gfull=((2, *rows, D), BF16),
        proj=((L, *rows, 5 * C), F32),
        state=((L, 2, 2, 2, SEGS + N * R, C), F32),
        unit=((L, 2, *rows, C), F32),
        inv=((L, *rows, C), F32),
        mixed=((L, *rows, 2 * C), BF16),
        gup=((L, *rows, 2 * F), BF16),
        hidden=((L, *rows, F), BF16),
        keep=((*rows, C), F32),
        drive=((2, *rows, C), F32),
        seg=((3, 2, 2, SEGS, C), F32),
        segk=((L, 2, 2, SEGS, C), F32),
        cur=((2, 2, 2, SEGS, C), F32),
        tot=((2, 2, R, C), F32),
        dgu=((*rows, 2 * F), BF16),
        dproj=((*rows, 5 * C), BF16),
        psc=((2, R, D), F32),
        xpart=((2, *own, D), F32),
        opart=((2, *own, D), F32),
        grad=((*own, D), F32),
        stage=((2, 3, *own, D), BF16),
        land=((2, 3, *own, D), BF16),
        gacc=((L, 2, SEGS, D), F32),
        sacc=((L, 4, SEGS, C), F32),
        wdown=((L, F, D), BF16),
        wg=((L, z.units, 2, z.blk, D), BF16),
        swork=((2 * SEGS, D), F32),
        sland=((5, 2 * SEGS, D), F32),
    )
    if z.reduce:
        unit = (SLOTS, z.sub, D)
        bufs.update(yland=(unit, BF16), mland=(unit, BF16))
        bufs.update(zland=(unit, BF16), zfold=((SLOTS, 2, z.sub, D), BF16))
    sems = dict(
        ags=(4 * L, 3, N),
        agr=(4 * L, 3, N),
        rss=(4 * L, 3, N),
        rsr=(4 * L, 3, N),
        wsem=(L, 10),
        ss=(5,),
        sr=(5,),
        outs=(z.period * L,),
    )
    if z.reduce:
        sems.update(us=(z.period * L, 5), ur=(z.period * L, 5))
    names = list(bufs) + list(sems)
    shapes = [pltpu.VMEM(s, d) for s, d in bufs.values()]
    shapes += [pltpu.SemaphoreType.DMA(s) for s in sems.values()]
    names.append("freed")
    shapes.append(pltpu.SemaphoreType.REGULAR((3,)))
    return names, shapes


IN_NAMES = ("x", "ct", "ng", "inw", "fw", "gw", "ow", "ph", "bl", "gg", "ffw", "dw")
OUT_NAMES = ("out", "ig", "wgout", "sums")


def mega(z, names, *refs):
    r = types.SimpleNamespace(**dict(zip(IN_NAMES + OUT_NAMES + tuple(names), refs)))
    L, D, C, F, R, N = z.L, z.D, z.C, z.F, z.R, CHUNKS
    ch = z.ch
    Q = R // SEGS
    dp = lax.axis_index("dp")
    me = lax.axis_index("tensor")
    core = lax.rem(me, 2)
    xi = me // 2
    other = 1 - xi
    sib = xi * 2 + 1 - core
    xnb = other * 2 + core

    inner = lax.rem(dp, 8)
    base = dp - inner
    y = lax.rem(inner, 2)
    line = inner // 2
    middle = (line == 1) | (line == 2)

    def on_line(place, row):
        return (base + 2 * place + row, me)

    y_peer = on_line(line, 1 - y)
    pair_peer = on_line(line + 1 - 2 * lax.rem(line, 2), y)
    cross_peer = on_line(3 - line, y)

    peers = [(dp, sib), (dp, xnb)]
    if z.reduce:
        peers += [y_peer, pair_peer, cross_peer]
    barrier = pltpu.get_barrier_semaphore()
    for peer in peers:
        pl.semaphore_signal(barrier, inc=1, device_id=peer, device_id_type=MESH)

    def remote(src, dst, send, recv, peer, pieces=1):
        def copy(source, target):
            return pltpu.make_async_remote_copy(
                src_ref=source,
                dst_ref=target,
                send_sem=send,
                recv_sem=recv,
                device_id=peer if isinstance(peer, tuple) else (dp, peer),
                device_id_type=MESH,
            )

        def start():
            lead = src.shape[0] if len(src.shape) == 3 else 1
            size = src.shape[-2] // pieces
            for first in range(lead):
                for k in range(pieces):
                    at = pl.ds(k * size, size)
                    if len(src.shape) == 3:
                        copy(src.at[first, at], dst.at[first, at]).start()
                    else:
                        copy(src.at[at], dst.at[at]).start()

        return types.SimpleNamespace(
            start=start,
            wait_recv=lambda: copy(src, dst).wait_recv(),
            wait_send=lambda: copy(src, dst).wait_send(),
            wait=lambda: copy(src, dst).wait(),
        )

    n_ffn = z.units - 4
    period = z.period

    def unit_of(u):
        s = u % period
        k = s // 2
        k = (k + n_ffn - z.fu) % n_ffn if k < n_ffn else k
        return L - 1 - u // period, k, slice((s % 2) * z.sub, (s % 2 + 1) * z.sub)

    half = line // 2

    def unit_copy(u, stage, even):
        l, k, rows = unit_of(u)
        slot = u % SLOTS
        both = r.wg.at[l, k, :, rows]
        if even:
            part = r.wg.at[l, k, half, rows]
            src, dst, peer = (
                (both, r.zfold.at[slot], pair_peer),
                (r.wg.at[l, k, 1 - half, rows], r.mland.at[slot], cross_peer),
                (part, r.yland.at[slot], y_peer),
                (part, part, cross_peer),
                (both, both, pair_peer),
            )[stage]
        else:
            mine = r.wg.at[l, k, y, rows]
            src, dst, peer = (
                (r.wg.at[l, k, 1 - y, rows], r.yland.at[slot], y_peer),
                (mine, r.zland.at[slot], pair_peer),
                (mine, r.mland.at[slot], cross_peer),
                (mine, r.zland.at[slot], pair_peer),
                (mine, mine, y_peer),
            )[stage]
        return remote(src, dst, r.us.at[u, stage], r.ur.at[u, stage], peer)

    def unit_land(u, stage, ref, peer):
        return remote(ref, ref, r.us.at[u, stage], r.ur.at[u, stage], peer)

    def unit_add(u, part, landed):
        l, k, rows = unit_of(u)
        r.wg[l, k, part, rows] = (r.wg[l, k, part, rows].astype(F32) + landed.astype(F32)).astype(BF16)

    def tell(sem, peer):
        pl.semaphore_signal(sem, inc=1, device_id=peer, device_id_type=MESH)

    def on_middle(body):
        pl.when(middle)(body)

    def on_end(body):
        pl.when(jnp.logical_not(middle))(body)

    def odd_stage(u, stage):
        copy = lambda n: unit_copy(u, n, False)
        slot = u % SLOTS
        l, k, rows = unit_of(u)
        if stage == 0:
            copy(0).start()
        if stage == 1:
            copy(0).wait_send()
            tell(r.freed.at[0], y_peer)
            copy(0).wait_recv()
            unit_add(u, y, r.yland[slot])
            on_end(lambda: copy(1).start())
        if stage == 2:

            @on_middle
            def _():
                copy(1).wait_recv()
                unit_add(u, y, r.zland[slot])
                copy(2).start()

        if stage == 3:

            @on_middle
            def _():
                copy(2).wait_recv()
                copy(2).wait_send()
                unit_add(u, y, r.mland[slot])
                copy(3).start()

        if stage == 4:

            @on_end
            def _():
                copy(1).wait_send()
                copy(3).wait_recv()
                r.wg[l, k, y, rows] = r.zland[slot]

            pl.semaphore_wait(r.freed.at[0], 1)
            copy(4).start()
        if stage == 5:
            unit_land(u, 4, r.wg.at[l, k, 1 - y, rows], y_peer).wait_recv()
            copy(4).wait_send()
            on_middle(lambda: copy(3).wait_send())
            unit_out(u).start()

    def even_stage(u, stage):
        copy = lambda n: unit_copy(u, n, True)
        slot = u % SLOTS
        l, k, rows = unit_of(u)
        if stage == 0:
            on_end(lambda: copy(0).start())
        if stage == 1:

            @on_end
            def _():
                copy(0).wait_send()
                tell(r.freed.at[1], pair_peer)

            @on_middle
            def _():
                copy(0).wait_recv()
                for part in range(2):
                    unit_add(u, part, r.zfold[slot, part])
                copy(1).start()

        if stage == 2:

            @on_middle
            def _():
                copy(1).wait_send()
                tell(r.freed.at[2], cross_peer)
                copy(1).wait_recv()
                unit_add(u, half, r.mland[slot])
                copy(2).start()

        if stage == 3:

            @on_middle
            def _():
                copy(2).wait_send()
                copy(2).wait_recv()
                unit_add(u, half, r.yland[slot])
                pl.semaphore_wait(r.freed.at[2], 1)
                copy(3).start()

        if stage == 4:

            @on_middle
            def _():
                unit_land(u, 3, r.wg.at[l, k, 1 - half, rows], cross_peer).wait_recv()
                pl.semaphore_wait(r.freed.at[1], 1)
                copy(4).start()

        if stage == 5:
            on_end(lambda: copy(4).wait_recv())

            @on_middle
            def _():
                copy(3).wait_send()
                copy(4).wait_send()

            unit_out(u).start()

    def unit_out(u):
        l, k, rows = unit_of(u)
        return pltpu.make_async_copy(r.wg.at[l, k, :, rows], r.wgout.at[l, k, :, rows], r.outs.at[u])

    clock = [0]
    last_tick = period * L + 5 * LAG

    def ticks(count, ready=None):
        for _ in range(count if z.reduce else 0):
            m = clock[0]
            if m >= last_tick or (ready is not None and m >= ready):
                return
            clock[0] = m + 1
            for stage in reversed(range(6)):
                u = m - LAG * stage
                if 0 <= u < period * L:
                    (even_stage if u % 2 == 0 else odd_stage)(u, stage)

    def ticks_in_loop(i, counts, ready):
        for at, count in enumerate(counts):
            if count:

                @pl.when(i == at)
                def _():
                    ticks(count, ready(at))

    def ag_copy(e, full, c, kind):
        chip = other if kind == 2 else xi
        peer = xnb if kind == 0 else sib
        ref = full.at[chip, c, core]
        return remote(ref, ref, r.ags.at[e, kind, c], r.agr.at[e, kind, c], peer, PIECES if kind == 0 else 1)

    def ag_landing(e, full, c, kind):
        chip = xi if kind == 1 else other
        col = core if kind == 0 else 1 - core
        ref = full.at[chip, c, col]
        return remote(ref, ref, r.ags.at[e, kind, c], r.agr.at[e, kind, c], sib)

    def ag_start(e, full, c):
        ag_copy(e, full, c, 0).start()
        ag_copy(e, full, c, 1).start()

    def ag_take_x(e, full, c):
        ag_landing(e, full, c, 0).wait_recv()
        ag_copy(e, full, c, 2).start()

    def rs_copy(e, c, kind):
        return remote(
            r.stage.at[r_side(e), kind, c],
            r.land.at[r_side(e), kind, c],
            r.rss.at[e, kind, c],
            r.rsr.at[e, kind, c],
            xnb if kind == 1 else sib,
            PIECES if kind == 1 else 1,
        )

    def r_side(e):
        return e // (2 * L)

    def rs_other(e, c):
        r.stage[r_side(e), 0, c] = r.psc[1 - core].astype(BF16)
        rs_copy(e, c, 0).start()
        r.xpart[r_side(e), c] = r.psc[core]

    def rs_pass(e, c):
        rs_copy(e, c, 0).wait_recv()
        r.stage[r_side(e), 1, c] = (r.xpart[r_side(e), c] + r.land[r_side(e), 0, c].astype(F32)).astype(BF16)
        rs_copy(e, c, 1).start()

    def rs_own(e, c):
        r.stage[r_side(e), 2, c] = r.psc[1 - core].astype(BF16)
        rs_copy(e, c, 2).start()
        r.opart[r_side(e), c] = r.psc[core]

    def rs_final(e, full, c):
        rs_copy(e, c, 2).wait_recv()
        rs_copy(e, c, 1).wait_recv()
        side = r_side(e)
        total = r.opart[side, c] + r.land[side, 2, c].astype(F32) + r.land[side, 1, c].astype(F32)
        for kind in range(3):
            rs_copy(e, c, kind).wait_send()
            ag_copy(e, full, c, kind).wait_send()
        return total

    def exchange_loop(e, full, order, send, stage, early=False):
        send(order(0))
        if early:

            def take(c):
                ag_landing(e, full, c, 1).wait_recv()
                ag_landing(e, full, c, 2).wait_recv()

            loop(N, take)

        def step(i):
            @pl.when(i + 1 < N)
            def _():
                send(order(i + 1))

            if not early:

                @pl.when(i < N)
                def _():
                    ag_landing(e, full, order(i), 1).wait_recv()

                @pl.when((i >= N - 1) & (i < 2 * N - 1))
                def _():
                    ag_take_x(e, full, order(i - N + 1))

                @pl.when(i >= N)
                def _():
                    ag_landing(e, full, order(i - N), 2).wait_recv()

            stage(i)

        loop(2 * N, step)

    def chip_chunk(i, order, own_first):
        first = i < N
        chunk = order(jnp.where(first, i, i - N))
        return jnp.where(first, xi, other) if own_first else jnp.where(first, other, xi), chunk

    def rs_step(e, i, order, own_first, go=True):
        first = i < N
        chunk = order(jnp.where(first, i, i - N))

        @pl.when(first if own_first else i >= N)
        def _():
            rs_own(e, chunk)

        @pl.when(i >= N if own_first else first)
        def _():
            rs_other(e, chunk)

        behind = (i - N if own_first else i) - 1

        @pl.when((behind >= 0) & (behind < N) & go)
        def _():
            rs_pass(e, order(behind))

    ascending = lambda j: j
    descending = lambda j: N - 1 - j

    def norm_rows(s):
        return lax.rsqrt(jnp.mean(s * s, axis=-1, keepdims=True) + EPS_NORM)

    def group_sum(v):
        high = v.astype(BF16)
        rest = (v - high.astype(F32)).astype(BF16)
        weight = r.gsum[...]
        return (mm(high, weight) + mm(rest, weight)) * (1.0 / (2 * GROUP_CH))

    def fold(v):
        return jnp.sum(v.reshape(v.shape[0] // SEGS, SEGS, v.shape[1]), axis=0)

    def flat(v):
        return v.reshape(-1, v.shape[-1])

    w_copies = []
    for l in range(L):
        parts = (r.inw.at[l, 0], r.inw.at[l, 1], r.fw.at[l], r.gw.at[l, 0], r.gw.at[l, 1])
        pairs = [(part, r.wmix.at[l, pl.ds(k * C, ch), :]) for k, part in enumerate(parts)]
        pairs += [(r.ow.at[l, k], r.wout.at[l, pl.ds(k * C, ch), :]) for k in range(2)]
        pairs += [(r.ffw.at[l, k], r.wffn.at[l, :, pl.ds(k * F, F)]) for k in range(2)]
        pairs += [(r.dw.at[l], r.wdown.at[l])]
        w_copies += [
            pltpu.make_async_copy(src, dst, r.wsem.at[l, k]) for k, (src, dst) in enumerate(pairs)
        ]
    for copy in w_copies:
        copy.start()

    tokens = N * R
    r.st[0] = mm(permutation(tokens), r.x[...]).reshape(N, R, D)
    r.ngf[...] = r.ng[...].astype(F32)

    def norm_first(c):
        s = r.st[0, c]
        r.mixfull[0, xi, c, core] = (s * norm_rows(s) * r.ngf[0, 0:1, :]).astype(BF16)

    loop(N, norm_first)
    pl.semaphore_wait(barrier, len(peers))
    loop(N, lambda c: ag_start(0, r.mixfull.at[0], c))

    r.grad[...] = mm(permutation(tokens), r.ct[...]).reshape(N, R, D)
    first_grad = r.gfull.at[0]

    def keep_cotangent(c):
        first_grad[xi, c, core] = r.grad[c].astype(BF16)

    loop(N, keep_cotangent)
    width = tokens // SEGS
    for k in range(5):
        r.wmix[:, k * C + ch : (k + 1) * C, :] = jnp.zeros((L, C - ch, D), BF16)
    for k in range(2):
        r.wout[:, k * C + ch : (k + 1) * C, :] = jnp.zeros((L, C - ch, D), BF16)
    r.par[...] = jnp.zeros_like(r.par)
    r.gacc[...] = jnp.zeros_like(r.gacc)
    r.sacc[...] = jnp.zeros_like(r.sacc)
    for l in range(L):
        angle = r.ph[l : l + 1, :]
        turn_cos, turn_sin = jnp.cos(angle), jnp.sin(angle)
        r.par[l, 0:1, 0:ch] = turn_cos
        r.par[l, 1:2, 0:ch] = turn_sin
        r.par[l, 2:3, 0:ch] = sigmoid(r.bl[l : l + 1, :])
        r.par[l, 3:4, 0:ch] = r.gg[l, 0:1, :].astype(F32)
        r.par[l, 4:5, 0:ch] = r.gg[l, 1:2, :].astype(F32)
        for _ in range(width.bit_length() - 1):
            turn_cos, turn_sin = (
                turn_cos * turn_cos - turn_sin * turn_sin,
                2.0 * turn_cos * turn_sin,
            )
        r.par[l, 5:6, 0:ch] = turn_cos
        r.par[l, 6:7, 0:ch] = turn_sin
    gi, gj = iota((C, C), 0), iota((C, C), 1)
    same = (gi // GROUP_CH == gj // GROUP_CH) & (gi < ch) & (gj < ch)
    r.gsum[...] = jnp.where(same, 1.0, 0.0).astype(BF16)

    def rows_of(q):
        return slice(q * SEGS, (q + 1) * SEGS)

    def scan_local(l, chip, c, turn_cos, turn_sin):
        for k in range(2):
            h_re, h_im, prod = r.seg[0, chip, k], r.seg[1, chip, k], r.seg[2, chip, k]
            for q in range(Q):
                rate = r.keep[chip, c, k, rows_of(q), :]
                h_re, h_im = (
                    rate * (turn_cos * h_re - turn_sin * h_im) + r.drive[0, chip, c, k, rows_of(q), :],
                    rate * (turn_cos * h_im + turn_sin * h_re) + r.drive[1, chip, c, k, rows_of(q), :],
                )
                prod = prod * rate
            r.seg[0, chip, k], r.seg[1, chip, k], r.seg[2, chip, k] = h_re, h_im, prod

    def scan_final(l, chip, c, turn_cos, turn_sin):
        base = SEGS + c * R
        for k in range(2):
            h_re, h_im = r.cur[0, chip, k], r.cur[1, chip, k]
            for q in range(Q):
                rate = r.keep[chip, c, k, rows_of(q), :]
                h_re, h_im = (
                    rate * (turn_cos * h_re - turn_sin * h_im) + r.drive[0, chip, c, k, rows_of(q), :],
                    rate * (turn_cos * h_im + turn_sin * h_re) + r.drive[1, chip, c, k, rows_of(q), :],
                )
                at = pl.ds(pl.multiple_of(base + q * SEGS, SEGS), SEGS)
                r.state[l, 0, chip, k, at, :] = h_re
                r.state[l, 1, chip, k, at, :] = h_im
            r.cur[0, chip, k], r.cur[1, chip, k] = h_re, h_im

    def scan_back_local(l, chip, c, turn_cos, turn_sin):
        for k in range(2):
            u_re, u_im = r.seg[0, chip, k], r.seg[1, chip, k]
            for q in reversed(range(Q)):
                rate = r.keep[chip, c, k, rows_of(q), :]
                t_re = r.drive[0, chip, c, k, rows_of(q), :] + u_re
                t_im = r.drive[1, chip, c, k, rows_of(q), :] + u_im
                u_re = rate * (turn_cos * t_re + turn_sin * t_im)
                u_im = rate * (turn_cos * t_im - turn_sin * t_re)
            r.seg[0, chip, k], r.seg[1, chip, k] = u_re, u_im

    def scan_back_final(l, chip, c, turn_cos, turn_sin):
        for k in range(2):
            u_re, u_im = r.cur[0, chip, k], r.cur[1, chip, k]
            for q in reversed(range(Q)):
                rate = r.keep[chip, c, k, rows_of(q), :]
                t_re = r.drive[0, chip, c, k, rows_of(q), :] + u_re
                t_im = r.drive[1, chip, c, k, rows_of(q), :] + u_im
                r.tot[0, k, rows_of(q), :] = t_re
                r.tot[1, k, rows_of(q), :] = t_im
                u_re = rate * (turn_cos * t_re + turn_sin * t_im)
                u_im = rate * (turn_cos * t_im - turn_sin * t_re)
            r.cur[0, chip, k], r.cur[1, chip, k] = u_re, u_im

    def carry_over(l, back):
        all_cos, all_sin = r.par[l, 5:6, :], r.par[l, 6:7, :]
        if back:
            all_sin = -all_sin
        c_re = jnp.zeros((1, C), F32)
        c_im = jnp.zeros((1, C), F32)
        order = [(chip, k, s) for chip in range(2) for k in range(2) for s in range(SEGS)]
        for chip, k, s in reversed(order) if back else order:
            one = slice(s, s + 1)
            r.cur[0, chip, k, one, :] = c_re
            r.cur[1, chip, k, one, :] = c_im
            prod = r.segk[l, chip, k, one, :]
            c_re, c_im = (
                prod * (all_cos * c_re - all_sin * c_im) + r.seg[0, chip, k, one, :],
                prod * (all_cos * c_im + all_sin * c_re) + r.seg[1, chip, k, one, :],
            )

    def forward_layer(l):
        turn_cos, turn_sin, lower = r.par[l, 0:1, :], r.par[l, 1:2, :], r.par[l, 2:3, :]
        gain_re, gain_im = r.par[l, 3:4, :], r.par[l, 4:5, :]
        e = 2 * l
        full = r.mixfull.at[l]

        def send_mix(c):
            @pl.when(l > 0)
            def _():
                s = r.st[2 * l - 1, c] + rs_final(e - 1, r.ffnfull.at[l - 1], c)
                r.st[2 * l, c] = s
                full[xi, c, core] = (s * norm_rows(s) * r.ngf[l, 0:1, :]).astype(BF16)
                ag_start(e, full, c)

        @pl.when(l == 0)
        def _():
            for copy in w_copies:
                copy.wait()

        r.seg[0:2] = jnp.zeros((2, 2, 2, SEGS, C), F32)
        r.seg[2] = jnp.ones((2, 2, SEGS, C), F32)

        def project(j):
            chip, c = chip_chunk(j, ascending, True)
            proj = mm_nt(flat(full[chip, c]), r.wmix[l])
            r.proj[l, chip, c] = proj.reshape(2, R, 5 * C)
            in_re, in_im, pre = proj[:, 0:C], proj[:, C : 2 * C], proj[:, 2 * C : 3 * C]
            rate = lower + (1.0 - lower) * sigmoid(pre)
            r.keep[chip, c] = rate.reshape(2, R, C)
            r.drive[0, chip, c] = ((1.0 - rate) * in_re * sigmoid(in_re)).reshape(2, R, C)
            r.drive[1, chip, c] = ((1.0 - rate) * in_im * sigmoid(in_im)).reshape(2, R, C)
            scan_local(l, chip, c, turn_cos, turn_sin)

        exchange_loop(e, full, ascending, send_mix, project)

        def send_cotangent(i):
            ag_start(2 * L, first_grad, l * z.early + i)

        loop(z.early, send_cotangent)
        r.segk[l] = r.seg[2]
        carry_over(l, False)
        for part in range(2):
            r.state[l, part, :, :, 0:SEGS, :] = r.cur[part]

        def mix(j):
            chip, c = chip_chunk(j, ascending, False)
            scan_final(l, chip, c, turn_cos, turn_sin)
            at = pl.ds(pl.multiple_of(SEGS + c * R, SEGS), R)
            s_re = flat(r.state[l, 0, chip, :, at, :])
            s_im = flat(r.state[l, 1, chip, :, at, :])
            centre = group_sum(s_re + s_im)
            d_re, d_im = s_re - centre, s_im - centre
            scale = lax.rsqrt(group_sum(d_re * d_re + d_im * d_im) + EPS_GROUP)
            u_re, u_im = d_re * scale, d_im * scale
            r.unit[l, 0, chip, c] = u_re.reshape(2, R, C)
            r.unit[l, 1, chip, c] = u_im.reshape(2, R, C)
            r.inv[l, chip, c] = scale.reshape(2, R, C)
            gate_re = flat(r.proj[l, chip, c, :, :, 3 * C : 4 * C])
            gate_im = flat(r.proj[l, chip, c, :, :, 4 * C : 5 * C])
            m_re = (u_re * gain_re * sigmoid(gate_re)).astype(BF16)
            m_im = (u_im * gain_im * sigmoid(gate_im)).astype(BF16)
            r.mixed[l, chip, c, :, :, 0:C] = m_re.reshape(2, R, C)
            r.mixed[l, chip, c, :, :, C : 2 * C] = m_im.reshape(2, R, C)
            r.psc[...] = mm(flat(r.mixed[l, chip, c]), r.wout[l]).reshape(2, R, D)

            rs_step(e, j, ascending, False)

        loop(2 * N, mix)

        def take_cotangent(i):
            ag_take_x(2 * L, first_grad, l * z.early + i)

        loop(z.early, take_cotangent)
        e2 = e + 1
        full2 = r.ffnfull.at[l]

        def send_ffn(c):
            s = r.st[2 * l, c] + rs_final(e, full, c)
            r.st[2 * l + 1, c] = s
            full2[xi, c, core] = (s * norm_rows(s) * r.ngf[l, 1:2, :]).astype(BF16)
            ag_start(e2, full2, c)

        def feed(j):
            chip, c = chip_chunk(j, ascending, True)
            both = mm(flat(full2[chip, c]), r.wffn[l])
            r.gup[l, chip, c] = both.astype(BF16).reshape(2, R, 2 * F)
            gate, up = both[:, 0:F], both[:, F : 2 * F]
            hidden = (gate * sigmoid(gate) * up).astype(BF16)
            r.hidden[l, chip, c] = hidden.reshape(2, R, F)
            r.psc[...] = mm(hidden, r.wdown[l]).reshape(2, R, D)

            rs_step(e2, j, ascending, True, l < L - 1)

        exchange_loop(e2, full2, ascending, send_ffn, feed)

        @pl.when(l < L - 1)
        def _():
            rs_pass(e2, N - 1)

    loop(L, forward_layer)

    def last_sum(c):
        e = 2 * L - 1
        s = r.st[2 * L - 1, c] + rs_final(e, r.ffnfull.at[L - 1], c)
        r.out[pl.ds(pl.multiple_of(c * R, R), R), :] = s.astype(BF16)

    def norm_back(l, which, c, grad_out):
        s = r.st[2 * l + which, c]
        scale = norm_rows(s)
        r.gacc[l, which] += fold(grad_out * s * scale)
        scaled = grad_out * r.ngf[l, which : which + 1, :]
        back = scale * scaled - s * (scale * scale * scale) * jnp.mean(
            scaled * s, axis=-1, keepdims=True
        )
        r.grad[c] = r.grad[c] + back

    def backward_layer(step):
        l = L - 1 - step
        e = 2 * L + 2 * step
        full = r.gfull.at[0]

        base = step * period
        pace = PACE[min(step, 1)]

        def send_ffn(c):
            if step > 0:
                norm_back(l + 1, 0, c, rs_final(e - 1, r.gfull.at[1], c))
                full[xi, c, core] = r.grad[c].astype(BF16)
                ag_start(e, full, c)

        def feed_back(j):
            chip, c = chip_chunk(j, descending, step > 0)
            g_hidden = mm_nt(flat(full[chip, c]), r.wdown[l])
            both = flat(r.gup[l, chip, c]).astype(F32)
            gate, up = both[:, 0:F], both[:, F : 2 * F]
            s = sigmoid(gate)
            g_gate = (g_hidden * up * s * (1.0 + gate * (1.0 - s))).astype(BF16)
            g_up = (g_hidden * gate * s).astype(BF16)
            r.dgu[chip, c, :, :, 0:F] = g_gate.reshape(2, R, F)
            r.dgu[chip, c, :, :, F : 2 * F] = g_up.reshape(2, R, F)
            r.psc[...] = mm_nt(flat(r.dgu[chip, c]), r.wffn[l]).reshape(2, R, D)

            rs_step(e, j, descending, step > 0)

            @pl.when(j == (2 * N - 1 if step > 0 else 0))
            def _():
                part = mm_tn(flat(r.hidden[l]), flat(full[...])).astype(BF16)
                r.wg[l, n_ffn - z.fu : n_ffn] = part.reshape(z.fu, 2, z.blk, D)

            ticks_in_loop(j, pace["feed"], lambda at: base + (4 if step == 0 or at == 2 * N - 1 else 0))

        exchange_loop(e, full, descending, send_ffn, feed_back, step == 0)
        if step > 0:
            rs_pass(e, 0)

        def ffn_tile(i):
            cols = pl.ds(pl.multiple_of(i * F, LANES), F)
            part = mm_tn(flat(r.ffnfull[l, :, :, :, :, cols]), flat(r.dgu[...])).astype(BF16)
            r.wg[l, pl.ds(i * z.fu, z.fu)] = part.reshape(z.fu, 2, z.blk, D)

        ticks(pace["feed_end"], base + 4)
        loop(D // F, ffn_tile)
        ticks(pace["ffn_end"], base + 12)

        turn_cos, turn_sin, lower = r.par[l, 0:1, :], r.par[l, 1:2, :], r.par[l, 2:3, :]
        gain_re, gain_im = r.par[l, 3:4, :], r.par[l, 4:5, :]
        e2 = e + 1
        full2 = r.gfull.at[1]

        def send_mix(c):
            norm_back(l, 1, c, rs_final(e, full, c))
            full2[xi, c, core] = r.grad[c].astype(BF16)
            ag_start(e2, full2, c)

        r.seg[0:2] = jnp.zeros((2, 2, 2, SEGS, C), F32)

        def mix_back(j):
            chip, c = chip_chunk(j, descending, True)
            g_both = mm_nt(flat(full2[chip, c]), r.wout[l])
            g_re, g_im = g_both[:, 0:C], g_both[:, C : 2 * C]
            s_re = sigmoid(flat(r.proj[l, chip, c, :, :, 3 * C : 4 * C]))
            s_im = sigmoid(flat(r.proj[l, chip, c, :, :, 4 * C : 5 * C]))
            u_re, u_im = flat(r.unit[l, 0, chip, c]), flat(r.unit[l, 1, chip, c])
            n_re, n_im = g_re * s_re, g_im * s_im
            r.sacc[l, 0] += fold(n_re * u_re)
            r.sacc[l, 1] += fold(n_im * u_im)
            x_re, x_im = n_re * gain_re, n_im * gain_im
            cross_re, cross_im = x_re * u_re, x_im * u_im
            r.dproj[chip, c, :, :, 3 * C : 4 * C] = (cross_re * (1.0 - s_re)).astype(BF16).reshape(2, R, C)
            r.dproj[chip, c, :, :, 4 * C : 5 * C] = (cross_im * (1.0 - s_im)).astype(BF16).reshape(2, R, C)
            mean_one = group_sum(x_re + x_im)
            mean_two = group_sum(cross_re + cross_im)
            scale = flat(r.inv[l, chip, c])
            r.drive[0, chip, c] = (scale * (x_re - mean_one - u_re * mean_two)).reshape(2, R, C)
            r.drive[1, chip, c] = (scale * (x_im - mean_one - u_im * mean_two)).reshape(2, R, C)
            pre = flat(r.proj[l, chip, c, :, :, 2 * C : 3 * C])
            r.keep[chip, c] = (lower + (1.0 - lower) * sigmoid(pre)).reshape(2, R, C)
            scan_back_local(l, chip, c, turn_cos, turn_sin)

            ticks_in_loop(j, pace["mix"], lambda at: base + 12)

        exchange_loop(e2, full2, descending, send_mix, mix_back)
        carry_over(l, True)

        def scan_back(j):
            chip, c = chip_chunk(j, descending, False)
            scan_back_final(l, chip, c, turn_cos, turn_sin)
            t_re, t_im = flat(r.tot[0]), flat(r.tot[1])
            at = pl.ds(pl.multiple_of(c * R, SEGS), R)
            p_re = flat(r.state[l, 0, chip, :, at, :])
            p_im = flat(r.state[l, 1, chip, :, at, :])
            in_re = flat(r.proj[l, chip, c, :, :, 0:C])
            in_im = flat(r.proj[l, chip, c, :, :, C : 2 * C])
            fs = sigmoid(flat(r.proj[l, chip, c, :, :, 2 * C : 3 * C]))
            rate = lower + (1.0 - lower) * fs
            s_re, s_im = sigmoid(in_re), sigmoid(in_im)
            gc_re = t_re * p_re + t_im * p_im
            gc_im = t_im * p_re - t_re * p_im
            g_keep = gc_re * turn_cos + gc_im * turn_sin - (t_re * in_re * s_re + t_im * in_im * s_im)
            r.sacc[l, 2] += fold(rate * (gc_im * turn_cos - gc_re * turn_sin))
            r.sacc[l, 3] += fold(g_keep * (1.0 - fs))
            d_re = t_re * (1.0 - rate) * s_re * (1.0 + in_re * (1.0 - s_re))
            d_im = t_im * (1.0 - rate) * s_im * (1.0 + in_im * (1.0 - s_im))
            d_f = g_keep * (1.0 - lower) * fs * (1.0 - fs)
            r.dproj[chip, c, :, :, 0:C] = d_re.astype(BF16).reshape(2, R, C)
            r.dproj[chip, c, :, :, C : 2 * C] = d_im.astype(BF16).reshape(2, R, C)
            r.dproj[chip, c, :, :, 2 * C : 3 * C] = d_f.astype(BF16).reshape(2, R, C)
            r.psc[...] = mm(flat(r.dproj[chip, c]), r.wmix[l]).reshape(2, R, D)

            rs_step(e2, j, descending, False)

            @pl.when(j == N)
            def _():
                loop(2, out_tile)
                loop(2, gate_tile)

            ticks_in_loop(j, pace["scan"], lambda at: base + (12 if at < N else 16))

        base_unit = z.units - 4

        def out_tile(i):
            cols = pl.ds(pl.multiple_of(i * C, LANES), C)
            part = mm_tn(flat(r.mixed[l, :, :, :, :, cols]), flat(full2[...])).astype(BF16)
            r.wg[l, base_unit, i] = part[0:ch]

        def proj_tile(k, unit, block):
            cols = pl.ds(pl.multiple_of(k * C, LANES), C)
            part = mm_tn(flat(r.dproj[:, :, :, :, cols]), flat(r.mixfull[l])).astype(BF16)
            r.wg[l, unit, block] = part[0:ch]

        def gate_tile(i):
            proj_tile(3 + i, base_unit + 1, i)

        def in_tile(i):
            proj_tile(i, base_unit + 2, i)

        def forget_tile():
            part = mm_tn(flat(r.dproj[:, :, :, :, 2 * C : 3 * C]), flat(r.mixfull[l])).astype(BF16)
            for half in range(2):
                r.wg[l, base_unit + 3, half, 0 : z.sub] = part[half * z.sub : (half + 1) * z.sub]

        loop(2 * N, scan_back)
        loop(2, in_tile)
        forget_tile()
        ticks(pace["end"], base + period)
        if step == L - 1:
            loop(N, lambda c: rs_pass(2 * L - 1, c))

    for step in range(L):
        backward_layer(step)

    def last_grad(j):
        c = descending(j)
        norm_back(0, 0, c, rs_final(4 * L - 1, r.gfull.at[1], c))

    ticks(AHEAD)
    loop(N, last_grad)
    r.ig[...] = r.grad[...].reshape(tokens, D).astype(BF16)

    r.swork[...] = jnp.zeros_like(r.swork)
    for l in range(L):
        for which in range(2):
            at = 2 * l + which
            r.swork[at : at + 1, :] = jnp.sum(r.gacc[l, which], axis=0, keepdims=True)

    for l in range(L):
        for k in range(4):
            value = jnp.sum(r.sacc[l, k], axis=0, keepdims=True)
            if k == 3:
                lower = r.par[l, 2:3, :]
                value = value * lower * (1.0 - lower)
            at = 2 * L + 4 * l + k
            r.swork[at : at + 1, 0:C] = value

    swap_peers = [sib, xnb] + ([y_peer, pair_peer, cross_peer] if z.reduce else [])
    n_swaps = len(swap_peers)

    def swap(k):
        return remote(r.swork, r.sland.at[k], r.ss.at[k], r.sr.at[k], swap_peers[k])

    for i in range(max(n_swaps + 1, last_tick - clock[0])):
        if 1 <= i <= n_swaps:
            k = i - 1
            swap(k).wait()
            rows = 2 * L if k < 2 else 2 * SEGS
            r.swork[0:rows, :] = r.swork[0:rows, :] + r.sland[k, 0:rows, :]
        if i < n_swaps:
            swap(i).start()
        ticks(1)
    loop(N, last_sum)
    r.sums[...] = r.swork[...]

    for u in range(period * L):
        if not z.reduce:
            unit_out(u).start()
        unit_out(u).wait()


def finish(z, n_tensor, out, ig, sums, w_in, w_forget, w_gate, w_out, w_ffn, w_down, *o):
    L, ch, F = z.L, z.ch, z.F
    l, i = pl.program_id(0), pl.program_id(1)
    tokens = out.shape[0]

    @pl.when((l == 0) & (i == 0))
    def _():
        o[0][...] = mm_tn(permutation(tokens), out[...]).astype(BF16)
        me = lax.axis_index("tensor")
        piece = z.D // n_tensor
        for t in range(n_tensor):

            @pl.when(me == t)
            def _():
                for k in range(L):
                    o[2][k] = sums[2 * k : 2 * k + 2, t * piece : (t + 1) * piece]

        for k in range(L):
            at = 2 * L + 4 * k
            o[7][k : k + 1, :] = sums[at + 2 : at + 3, 0:ch]
            o[8][k : k + 1, :] = sums[at + 3 : at + 4, 0:ch]
            o[9][k] = sums[at : at + 2, 0:ch]

    @pl.when((l == L - 1) & (i == 0))
    def _():
        o[1][...] = mm_tn(permutation(tokens), ig[...]).astype(BF16)

    o[3][...] = w_in[...].astype(F32)
    o[4][...] = w_forget[...].astype(F32)
    o[5][...] = w_gate[...].astype(F32)
    o[6][...] = w_out[...].astype(F32)
    o[10][0, 0] = w_ffn[0, :, 0:F].astype(F32)
    o[10][0, 1] = w_ffn[0, :, F : 2 * F].astype(F32)
    o[11][...] = w_down[...].astype(F32)


def local(*args):
    x, ct, ng, inw, fw, gw, ow, ph, bl, gg, ffw, dw = args
    L, D = ng.shape[0], ng.shape[2]
    ch = fw.shape[2]
    F = dw.shape[1]
    C = -(-ch // LANES) * LANES
    n_dp = lax.axis_size("dp")
    reduce = n_dp % 8 == 0
    fu = F // (2 * ch)
    units = fu * (1 + D // F) + 4
    sub = ch // 2
    period = 2 * units - 1
    z = types.SimpleNamespace(
        L=L, D=D, C=C, F=F, ch=ch, R=x.shape[0] // CHUNKS, reduce=reduce, blk=ch, fu=fu, units=units, sub=sub, period=period
    )
    z.early = CHUNKS // L
    names, scratch = scratch_of(z)
    vmem = pl.BlockSpec(memory_space=pltpu.VMEM)
    anywhere = pl.BlockSpec(memory_space=pl.ANY)
    in_specs = [vmem] * 12
    for k in (3, 4, 5, 6, 10, 11):
        in_specs[k] = anywhere
    shape = jax.ShapeDtypeStruct
    out, ig, wg, sums = pl.pallas_call(
        functools.partial(mega, z, names),
        out_shape=(
            shape(x.shape, BF16),
            shape(x.shape, BF16),
            shape((L, units, 2, ch, D), BF16),
            shape((2 * SEGS, D), F32),
        ),
        in_specs=in_specs,
        out_specs=[vmem, vmem, anywhere, vmem],
        scratch_shapes=scratch,
        compiler_params=pltpu.CompilerParams(
            collective_id=0, has_side_effects=True, vmem_limit_bytes=VMEM_BYTES
        ),
        name="layers",
    )(x, ct, ng, jnp.swapaxes(inw, 2, 3), jnp.swapaxes(fw, 1, 2), jnp.swapaxes(gw, 2, 3), ow, ph, bl, gg, ffw, dw)

    if not reduce:
        wg, sums = lax.psum((wg, sums), "dp")
    elif n_dp > 8:
        groups = [list(range(k, n_dp, 8)) for k in range(8)]
        wg, sums = lax.psum((wg, sums), "dp", axis_index_groups=groups)
    n_tensor = lax.axis_size("tensor")
    blocks = wg.reshape(L, 2 * units, ch, D)
    rows = wg.reshape(L, 2 * units * ch, D)
    G = 1
    piece = ch // G

    def block_spec(count, index):
        return pl.BlockSpec((1, count, piece, D), lambda l, i: (l, index, i, 0))

    def part_spec(index):
        return pl.BlockSpec((1, 2, sub // G, D), lambda l, i: (l, index, i, 0))

    def row_spec(size, index):
        return pl.BlockSpec((1, size, D), lambda l, i: (l, index + i, 0))

    def whole(*dims):
        return pl.BlockSpec(dims, lambda l, i: (0,) * len(dims))

    first = 2 * (units - 4)
    res = pl.pallas_call(
        functools.partial(finish, z, n_tensor),
        grid=(L, G),
        out_shape=(
            shape(x.shape, BF16),
            shape(x.shape, BF16),
            shape((L, 2, D // n_tensor), F32),
            shape((L, 2, ch, D), F32),
            shape((L, 2, sub, D), F32),
            shape((L, 2, ch, D), F32),
            shape((L, 2, ch, D), F32),
            shape((L, ch), F32),
            shape((L, ch), F32),
            shape((L, 2, ch), F32),
            shape((L, 2, D, F), F32),
            shape((L, F, D), F32),
        ),
        in_specs=[
            whole(*x.shape),
            whole(*x.shape),
            whole(2 * SEGS, D),
            block_spec(2, first // 2 + 2),
            part_spec(first // 2 + 3),
            block_spec(2, first // 2 + 1),
            block_spec(2, first // 2),
            row_spec(D // G, 0),
            row_spec(F // G, D // (F // G)),
        ],
        out_specs=[
            whole(*x.shape),
            whole(*x.shape),
            whole(L, 2, D // n_tensor),
            block_spec(2, 0),
            part_spec(0),
            block_spec(2, 0),
            block_spec(2, 0),
            whole(L, ch),
            whole(L, ch),
            whole(L, 2, ch),
            pl.BlockSpec((1, 2, D // G, F), lambda l, i: (l, 0, i, 0)),
            row_spec(F // G, 0),
        ],
        compiler_params=pltpu.CompilerParams(vmem_limit_bytes=VMEM_BYTES),
        name="finish",
    )(out, ig, sums, blocks, blocks, blocks, blocks, rows, rows)
    res = list(res)
    res[3] = jnp.swapaxes(res[3], 2, 3)
    res[4] = jnp.swapaxes(res[4].reshape(L, ch, D), 1, 2)
    res[5] = jnp.swapaxes(res[5], 2, 3)
    return tuple(res)


def solution(mesh):
    tokens = P(("dp", "tensor"), None)
    return jax.shard_map(
        local,
        mesh=mesh,
        in_specs=(
            tokens,
            tokens,
            P(),
            P(None, None, None, "tensor"),
            P(None, None, "tensor"),
            P(None, None, None, "tensor"),
            P(None, None, "tensor", None),
            P(None, "tensor"),
            P(None, "tensor"),
            P(None, None, "tensor"),
            P(None, None, None, "tensor"),
            P(None, "tensor", None),
        ),
        out_specs=(
            tokens,
            tokens,
            P(None, None, "tensor"),
            P(None, None, None, "tensor"),
            P(None, None, "tensor"),
            P(None, None, None, "tensor"),
            P(None, None, "tensor", None),
            P(None, "tensor"),
            P(None, "tensor"),
            P(None, None, "tensor"),
            P(None, None, None, "tensor"),
            P(None, "tensor", None),
        ),
        check_vma=False,
    )
```

```python
import functools
import types

import jax
import jax.numpy as jnp
from jax import lax
from jax.experimental import pallas as pl
from jax.experimental.pallas import tpu as pltpu
from jax.sharding import PartitionSpec as P

MESH = pl.DeviceIdType.MESH
F32 = jnp.float32
BF16 = jnp.bfloat16

GROUP_CH = 48
EPS_NORM = 1e-06
EPS_GROUP = 1e-05
LANES = 128
SEGS = 8
CHUNKS = 4
LAG = 2
PACE = (
    dict(feed=(0, 0, 0, 0, 1, 0, 0, 1), feed_end=0, ffn_end=1, mix=(1, 0, 1, 0, 1, 1, 1, 1), scan=(0, 0, 1, 1, 0, 1, 1, 0), end=1),
    dict(feed=(1, 1, 1, 0, 1, 0, 0, 1), feed_end=1, ffn_end=2, mix=(1, 0, 1, 0, 1, 1, 1, 1), scan=(0, 1, 0, 1, 1, 0, 1, 0), end=2),
)
AHEAD = 6
PIECES = 2
SLOTS = 10
VMEM_BYTES = 63 * 1024 * 1024


def sigmoid(v):
    return 0.5 * jnp.tanh(0.5 * v) + 0.5


def mm(left, right):
    return jnp.dot(left, right, preferred_element_type=F32)


def mm_nt(left, right):
    return lax.dot_general(left, right, (((1,), (1,)), ((), ())), preferred_element_type=F32)


def mm_tn(left, right):
    return lax.dot_general(left, right, (((0,), (0,)), ((), ())), preferred_element_type=F32)


def loop(count, body):
    def step(index, carry):
        body(index)
        return carry

    lax.fori_loop(0, count, step, 0)


def iota(shape, dim):
    return lax.broadcasted_iota(jnp.int32, shape, dim)


def permutation(tokens):
    width = tokens // SEGS
    row = iota((tokens, tokens), 0)
    place = lax.rem(row, SEGS) * width + row // SEGS
    return jnp.where(iota((tokens, tokens), 1) == place, 1.0, 0.0).astype(BF16)


def scratch_of(z):
    L, D, C, F, R, N = z.L, z.D, z.C, z.F, z.R, CHUNKS
    rows = (2, N, 2, R)
    own = (N, R)
    bufs = dict(
        wmix=((L, 5 * C, D), BF16),
        wout=((L, 2 * C, D), BF16),
        wffn=((L, D, 2 * F), BF16),
        par=((L, 8, C), F32),
        ngf=((L, 2, D), F32),
        gsum=((C, C), BF16),
        st=((2 * L, *own, D), F32),
        mixfull=((L, *rows, D), BF16),
        ffnfull=((L, *rows, D), BF16),
        gfull=((2, *rows, D), BF16),
        proj=((L, *rows, 5 * C), F32),
        state=((L, 2, 2, 2, SEGS + N * R, C), F32),
        unit=((L, 2, *rows, C), F32),
        inv=((L, *rows, C), F32),
        mixed=((L, *rows, 2 * C), BF16),
        gup=((L, *rows, 2 * F), BF16),
        hidden=((L, *rows, F), BF16),
        keep=((*rows, C), F32),
        drive=((2, *rows, C), F32),
        seg=((3, 2, 2, SEGS, C), F32),
        segk=((L, 2, 2, SEGS, C), F32),
        cur=((2, 2, 2, SEGS, C), F32),
        tot=((2, 2, R, C), F32),
        dgu=((*rows, 2 * F), BF16),
        dproj=((*rows, 5 * C), BF16),
        psc=((2, R, D), F32),
        xpart=((2, *own, D), F32),
        opart=((2, *own, D), F32),
        grad=((*own, D), F32),
        stage=((2, 3, *own, D), BF16),
        land=((2, 3, *own, D), BF16),
        gacc=((L, 2, SEGS, D), F32),
        sacc=((L, 4, SEGS, C), F32),
        wdown=((L, F, D), BF16),
        wg=((L, z.units, 2, z.blk, D), BF16),
        swork=((2 * SEGS, D), F32),
        sland=((5, 2 * SEGS, D), F32),
    )
    if z.reduce:
        unit = (SLOTS, z.sub, D)
        bufs.update(yland=(unit, BF16), mland=(unit, BF16))
        bufs.update(zland=(unit, BF16), zfold=((SLOTS, 2, z.sub, D), BF16))
    sems = dict(
        ags=(4 * L, 3, N),
        agr=(4 * L, 3, N),
        rss=(4 * L, 3, N),
        rsr=(4 * L, 3, N),
        wsem=(L, 10),
        ss=(5,),
        sr=(5,),
        outs=(z.period * L,),
    )
    if z.reduce:
        sems.update(us=(z.period * L, 5), ur=(z.period * L, 5))
    names = list(bufs) + list(sems)
    shapes = [pltpu.VMEM(s, d) for s, d in bufs.values()]
    shapes += [pltpu.SemaphoreType.DMA(s) for s in sems.values()]
    names.append("freed")
    shapes.append(pltpu.SemaphoreType.REGULAR((3,)))
    return names, shapes


IN_NAMES = ("x", "ct", "ng", "inw", "fw", "gw", "ow", "ph", "bl", "gg", "ffw", "dw")
OUT_NAMES = ("out", "ig", "wgout", "sums")


def mega(z, names, *refs):
    r = types.SimpleNamespace(**dict(zip(IN_NAMES + OUT_NAMES + tuple(names), refs)))
    L, D, C, F, R, N = z.L, z.D, z.C, z.F, z.R, CHUNKS
    ch = z.ch
    Q = R // SEGS
    dp = lax.axis_index("dp")
    me = lax.axis_index("tensor")
    core = lax.rem(me, 2)
    xi = me // 2
    other = 1 - xi
    sib = xi * 2 + 1 - core
    xnb = other * 2 + core

    inner = lax.rem(dp, 8)
    base = dp - inner
    y = lax.rem(inner, 2)
    line = inner // 2
    middle = (line == 1) | (line == 2)

    def on_line(place, row):
        return (base + 2 * place + row, me)

    y_peer = on_line(line, 1 - y)
    pair_peer = on_line(line + 1 - 2 * lax.rem(line, 2), y)
    cross_peer = on_line(3 - line, y)

    peers = [(dp, sib), (dp, xnb)]
    if z.reduce:
        peers += [y_peer, pair_peer, cross_peer]
    barrier = pltpu.get_barrier_semaphore()
    for peer in peers:
        pl.semaphore_signal(barrier, inc=1, device_id=peer, device_id_type=MESH)

    def remote(src, dst, send, recv, peer, pieces=1):
        def copy(source, target):
            return pltpu.make_async_remote_copy(
                src_ref=source,
                dst_ref=target,
                send_sem=send,
                recv_sem=recv,
                device_id=peer if isinstance(peer, tuple) else (dp, peer),
                device_id_type=MESH,
            )

        def start():
            lead = src.shape[0] if len(src.shape) == 3 else 1
            size = src.shape[-2] // pieces
            for first in range(lead):
                for k in range(pieces):
                    at = pl.ds(k * size, size)
                    if len(src.shape) == 3:
                        copy(src.at[first, at], dst.at[first, at]).start()
                    else:
                        copy(src.at[at], dst.at[at]).start()

        return types.SimpleNamespace(
            start=start,
            wait_recv=lambda: copy(src, dst).wait_recv(),
            wait_send=lambda: copy(src, dst).wait_send(),
            wait=lambda: copy(src, dst).wait(),
        )

    n_ffn = z.units - 4
    period = z.period

    def unit_of(u):
        s = u % period
        k = s // 2
        k = (k + n_ffn - z.fu) % n_ffn if k < n_ffn else k
        return L - 1 - u // period, k, slice((s % 2) * z.sub, (s % 2 + 1) * z.sub)

    half = line // 2

    def unit_copy(u, stage, even):
        l, k, rows = unit_of(u)
        slot = u % SLOTS
        both = r.wg.at[l, k, :, rows]
        if even:
            part = r.wg.at[l, k, half, rows]
            src, dst, peer = (
                (both, r.zfold.at[slot], pair_peer),
                (r.wg.at[l, k, 1 - half, rows], r.mland.at[slot], cross_peer),
                (part, r.yland.at[slot], y_peer),
                (part, part, cross_peer),
                (both, both, pair_peer),
            )[stage]
        else:
            mine = r.wg.at[l, k, y, rows]
            src, dst, peer = (
                (r.wg.at[l, k, 1 - y, rows], r.yland.at[slot], y_peer),
                (mine, r.zland.at[slot], pair_peer),
                (mine, r.mland.at[slot], cross_peer),
                (mine, r.zland.at[slot], pair_peer),
                (mine, mine, y_peer),
            )[stage]
        return remote(src, dst, r.us.at[u, stage], r.ur.at[u, stage], peer)

    def unit_land(u, stage, ref, peer):
        return remote(ref, ref, r.us.at[u, stage], r.ur.at[u, stage], peer)

    def unit_add(u, part, landed):
        l, k, rows = unit_of(u)
        r.wg[l, k, part, rows] = (r.wg[l, k, part, rows].astype(F32) + landed.astype(F32)).astype(BF16)

    def tell(sem, peer):
        pl.semaphore_signal(sem, inc=1, device_id=peer, device_id_type=MESH)

    def on_middle(body):
        pl.when(middle)(body)

    def on_end(body):
        pl.when(jnp.logical_not(middle))(body)

    def odd_stage(u, stage):
        copy = lambda n: unit_copy(u, n, False)
        slot = u % SLOTS
        l, k, rows = unit_of(u)
        if stage == 0:
            copy(0).start()
        if stage == 1:
            copy(0).wait_send()
            tell(r.freed.at[0], y_peer)
            copy(0).wait_recv()
            unit_add(u, y, r.yland[slot])
            on_end(lambda: copy(1).start())
        if stage == 2:

            @on_middle
            def _():
                copy(1).wait_recv()
                unit_add(u, y, r.zland[slot])
                copy(2).start()

        if stage == 3:

            @on_middle
            def _():
                copy(2).wait_recv()
                copy(2).wait_send()
                unit_add(u, y, r.mland[slot])
                copy(3).start()

        if stage == 4:

            @on_end
            def _():
                copy(1).wait_send()
                copy(3).wait_recv()
                r.wg[l, k, y, rows] = r.zland[slot]

            pl.semaphore_wait(r.freed.at[0], 1)
            copy(4).start()
        if stage == 5:
            unit_land(u, 4, r.wg.at[l, k, 1 - y, rows], y_peer).wait_recv()
            copy(4).wait_send()
            on_middle(lambda: copy(3).wait_send())
            unit_out(u).start()

    def even_stage(u, stage):
        copy = lambda n: unit_copy(u, n, True)
        slot = u % SLOTS
        l, k, rows = unit_of(u)
        if stage == 0:
            on_end(lambda: copy(0).start())
        if stage == 1:

            @on_end
            def _():
                copy(0).wait_send()
                tell(r.freed.at[1], pair_peer)

            @on_middle
            def _():
                copy(0).wait_recv()
                for part in range(2):
                    unit_add(u, part, r.zfold[slot, part])
                copy(1).start()

        if stage == 2:

            @on_middle
            def _():
                copy(1).wait_send()
                tell(r.freed.at[2], cross_peer)
                copy(1).wait_recv()
                unit_add(u, half, r.mland[slot])
                copy(2).start()

        if stage == 3:

            @on_middle
            def _():
                copy(2).wait_send()
                copy(2).wait_recv()
                unit_add(u, half, r.yland[slot])
                pl.semaphore_wait(r.freed.at[2], 1)
                copy(3).start()

        if stage == 4:

            @on_middle
            def _():
                unit_land(u, 3, r.wg.at[l, k, 1 - half, rows], cross_peer).wait_recv()
                pl.semaphore_wait(r.freed.at[1], 1)
                copy(4).start()

        if stage == 5:
            on_end(lambda: copy(4).wait_recv())

            @on_middle
            def _():
                copy(3).wait_send()
                copy(4).wait_send()

            unit_out(u).start()

    def unit_out(u):
        l, k, rows = unit_of(u)
        return pltpu.make_async_copy(r.wg.at[l, k, :, rows], r.wgout.at[l, k, :, rows], r.outs.at[u])

    clock = [0]
    last_tick = period * L + 5 * LAG

    def ticks(count, ready=None):
        for _ in range(count if z.reduce else 0):
            m = clock[0]
            if m >= last_tick or (ready is not None and m >= ready):
                return
            clock[0] = m + 1
            for stage in reversed(range(6)):
                u = m - LAG * stage
                if 0 <= u < period * L:
                    (even_stage if u % 2 == 0 else odd_stage)(u, stage)

    def ticks_in_loop(i, counts, ready):
        for at, count in enumerate(counts):
            if count:

                @pl.when(i == at)
                def _():
                    ticks(count, ready(at))

    def ag_copy(e, full, c, kind):
        chip = other if kind == 2 else xi
        peer = xnb if kind == 0 else sib
        ref = full.at[chip, c, core]
        return remote(ref, ref, r.ags.at[e, kind, c], r.agr.at[e, kind, c], peer, PIECES if kind == 0 else 1)

    def ag_landing(e, full, c, kind):
        chip = xi if kind == 1 else other
        col = core if kind == 0 else 1 - core
        ref = full.at[chip, c, col]
        return remote(ref, ref, r.ags.at[e, kind, c], r.agr.at[e, kind, c], sib)

    def ag_start(e, full, c):
        ag_copy(e, full, c, 0).start()
        ag_copy(e, full, c, 1).start()

    def ag_take_x(e, full, c):
        ag_landing(e, full, c, 0).wait_recv()
        ag_copy(e, full, c, 2).start()

    def rs_copy(e, c, kind):
        return remote(
            r.stage.at[r_side(e), kind, c],
            r.land.at[r_side(e), kind, c],
            r.rss.at[e, kind, c],
            r.rsr.at[e, kind, c],
            xnb if kind == 1 else sib,
            PIECES if kind == 1 else 1,
        )

    def r_side(e):
        return e // (2 * L)

    def rs_other(e, c):
        r.stage[r_side(e), 0, c] = r.psc[1 - core].astype(BF16)
        rs_copy(e, c, 0).start()
        r.xpart[r_side(e), c] = r.psc[core]

    def rs_pass(e, c):
        rs_copy(e, c, 0).wait_recv()
        r.stage[r_side(e), 1, c] = (r.xpart[r_side(e), c] + r.land[r_side(e), 0, c].astype(F32)).astype(BF16)
        rs_copy(e, c, 1).start()

    def rs_own(e, c):
        r.stage[r_side(e), 2, c] = r.psc[1 - core].astype(BF16)
        rs_copy(e, c, 2).start()
        r.opart[r_side(e), c] = r.psc[core]

    def rs_final(e, full, c):
        rs_copy(e, c, 2).wait_recv()
        rs_copy(e, c, 1).wait_recv()
        side = r_side(e)
        total = r.opart[side, c] + r.land[side, 2, c].astype(F32) + r.land[side, 1, c].astype(F32)
        for kind in range(3):
            rs_copy(e, c, kind).wait_send()
            ag_copy(e, full, c, kind).wait_send()
        return total

    def exchange_loop(e, full, order, send, stage, early=False):
        send(order(0))
        if early:

            def take(c):
                ag_landing(e, full, c, 1).wait_recv()
                ag_landing(e, full, c, 2).wait_recv()

            loop(N, take)

        def step(i):
            @pl.when(i + 1 < N)
            def _():
                send(order(i + 1))

            if not early:

                @pl.when(i < N)
                def _():
                    ag_landing(e, full, order(i), 1).wait_recv()

                @pl.when((i >= N - 1) & (i < 2 * N - 1))
                def _():
                    ag_take_x(e, full, order(i - N + 1))

                @pl.when(i >= N)
                def _():
                    ag_landing(e, full, order(i - N), 2).wait_recv()

            stage(i)

        loop(2 * N, step)

    def chip_chunk(i, order, own_first):
        first = i < N
        chunk = order(jnp.where(first, i, i - N))
        return jnp.where(first, xi, other) if own_first else jnp.where(first, other, xi), chunk

    def rs_step(e, i, order, own_first, go=True):
        first = i < N
        chunk = order(jnp.where(first, i, i - N))

        @pl.when(first if own_first else i >= N)
        def _():
            rs_own(e, chunk)

        @pl.when(i >= N if own_first else first)
        def _():
            rs_other(e, chunk)

        behind = (i - N if own_first else i) - 1

        @pl.when((behind >= 0) & (behind < N) & go)
        def _():
            rs_pass(e, order(behind))

    ascending = lambda j: j
    descending = lambda j: N - 1 - j

    def norm_rows(s):
        return lax.rsqrt(jnp.mean(s * s, axis=-1, keepdims=True) + EPS_NORM)

    def group_sum(v):
        high = v.astype(BF16)
        rest = (v - high.astype(F32)).astype(BF16)
        weight = r.gsum[...]
        return (mm(high, weight) + mm(rest, weight)) * (1.0 / (2 * GROUP_CH))

    def fold(v):
        return jnp.sum(v.reshape(v.shape[0] // SEGS, SEGS, v.shape[1]), axis=0)

    def flat(v):
        return v.reshape(-1, v.shape[-1])

    w_copies = []
    for l in range(L):
        parts = (r.inw.at[l, 0], r.inw.at[l, 1], r.fw.at[l], r.gw.at[l, 0], r.gw.at[l, 1])
        pairs = [(part, r.wmix.at[l, pl.ds(k * C, ch), :]) for k, part in enumerate(parts)]
        pairs += [(r.ow.at[l, k], r.wout.at[l, pl.ds(k * C, ch), :]) for k in range(2)]
        pairs += [(r.ffw.at[l, k], r.wffn.at[l, :, pl.ds(k * F, F)]) for k in range(2)]
        pairs += [(r.dw.at[l], r.wdown.at[l])]
        w_copies += [
            pltpu.make_async_copy(src, dst, r.wsem.at[l, k]) for k, (src, dst) in enumerate(pairs)
        ]
    for copy in w_copies:
        copy.start()

    tokens = N * R
    r.st[0] = mm(permutation(tokens), r.x[...]).reshape(N, R, D)
    r.ngf[...] = r.ng[...].astype(F32)

    def norm_first(c):
        s = r.st[0, c]
        r.mixfull[0, xi, c, core] = (s * norm_rows(s) * r.ngf[0, 0:1, :]).astype(BF16)

    loop(N, norm_first)
    pl.semaphore_wait(barrier, len(peers))
    loop(N, lambda c: ag_start(0, r.mixfull.at[0], c))

    r.grad[...] = mm(permutation(tokens), r.ct[...]).reshape(N, R, D)
    first_grad = r.gfull.at[0]

    def keep_cotangent(c):
        first_grad[xi, c, core] = r.grad[c].astype(BF16)

    loop(N, keep_cotangent)
    width = tokens // SEGS
    for k in range(5):
        r.wmix[:, k * C + ch : (k + 1) * C, :] = jnp.zeros((L, C - ch, D), BF16)
    for k in range(2):
        r.wout[:, k * C + ch : (k + 1) * C, :] = jnp.zeros((L, C - ch, D), BF16)
    r.par[...] = jnp.zeros_like(r.par)
    r.gacc[...] = jnp.zeros_like(r.gacc)
    r.sacc[...] = jnp.zeros_like(r.sacc)
    for l in range(L):
        angle = r.ph[l : l + 1, :]
        turn_cos, turn_sin = jnp.cos(angle), jnp.sin(angle)
        r.par[l, 0:1, 0:ch] = turn_cos
        r.par[l, 1:2, 0:ch] = turn_sin
        r.par[l, 2:3, 0:ch] = sigmoid(r.bl[l : l + 1, :])
        r.par[l, 3:4, 0:ch] = r.gg[l, 0:1, :].astype(F32)
        r.par[l, 4:5, 0:ch] = r.gg[l, 1:2, :].astype(F32)
        for _ in range(width.bit_length() - 1):
            turn_cos, turn_sin = (
                turn_cos * turn_cos - turn_sin * turn_sin,
                2.0 * turn_cos * turn_sin,
            )
        r.par[l, 5:6, 0:ch] = turn_cos
        r.par[l, 6:7, 0:ch] = turn_sin
    gi, gj = iota((C, C), 0), iota((C, C), 1)
    same = (gi // GROUP_CH == gj // GROUP_CH) & (gi < ch) & (gj < ch)
    r.gsum[...] = jnp.where(same, 1.0, 0.0).astype(BF16)

    def rows_of(q):
        return slice(q * SEGS, (q + 1) * SEGS)

    def scan_local(l, chip, c, turn_cos, turn_sin):
        for k in range(2):
            h_re, h_im, prod = r.seg[0, chip, k], r.seg[1, chip, k], r.seg[2, chip, k]
            for q in range(Q):
                rate = r.keep[chip, c, k, rows_of(q), :]
                h_re, h_im = (
                    rate * (turn_cos * h_re - turn_sin * h_im) + r.drive[0, chip, c, k, rows_of(q), :],
                    rate * (turn_cos * h_im + turn_sin * h_re) + r.drive[1, chip, c, k, rows_of(q), :],
                )
                prod = prod * rate
            r.seg[0, chip, k], r.seg[1, chip, k], r.seg[2, chip, k] = h_re, h_im, prod

    def scan_final(l, chip, c, turn_cos, turn_sin):
        base = SEGS + c * R
        for k in range(2):
            h_re, h_im = r.cur[0, chip, k], r.cur[1, chip, k]
            for q in range(Q):
                rate = r.keep[chip, c, k, rows_of(q), :]
                h_re, h_im = (
                    rate * (turn_cos * h_re - turn_sin * h_im) + r.drive[0, chip, c, k, rows_of(q), :],
                    rate * (turn_cos * h_im + turn_sin * h_re) + r.drive[1, chip, c, k, rows_of(q), :],
                )
                at = pl.ds(pl.multiple_of(base + q * SEGS, SEGS), SEGS)
                r.state[l, 0, chip, k, at, :] = h_re
                r.state[l, 1, chip, k, at, :] = h_im
            r.cur[0, chip, k], r.cur[1, chip, k] = h_re, h_im

    def scan_back_local(l, chip, c, turn_cos, turn_sin):
        for k in range(2):
            u_re, u_im = r.seg[0, chip, k], r.seg[1, chip, k]
            for q in reversed(range(Q)):
                rate = r.keep[chip, c, k, rows_of(q), :]
                t_re = r.drive[0, chip, c, k, rows_of(q), :] + u_re
                t_im = r.drive[1, chip, c, k, rows_of(q), :] + u_im
                u_re = rate * (turn_cos * t_re + turn_sin * t_im)
                u_im = rate * (turn_cos * t_im - turn_sin * t_re)
            r.seg[0, chip, k], r.seg[1, chip, k] = u_re, u_im

    def scan_back_final(l, chip, c, turn_cos, turn_sin):
        for k in range(2):
            u_re, u_im = r.cur[0, chip, k], r.cur[1, chip, k]
            for q in reversed(range(Q)):
                rate = r.keep[chip, c, k, rows_of(q), :]
                t_re = r.drive[0, chip, c, k, rows_of(q), :] + u_re
                t_im = r.drive[1, chip, c, k, rows_of(q), :] + u_im
                r.tot[0, k, rows_of(q), :] = t_re
                r.tot[1, k, rows_of(q), :] = t_im
                u_re = rate * (turn_cos * t_re + turn_sin * t_im)
                u_im = rate * (turn_cos * t_im - turn_sin * t_re)
            r.cur[0, chip, k], r.cur[1, chip, k] = u_re, u_im

    def carry_over(l, back):
        all_cos, all_sin = r.par[l, 5:6, :], r.par[l, 6:7, :]
        if back:
            all_sin = -all_sin
        c_re = jnp.zeros((1, C), F32)
        c_im = jnp.zeros((1, C), F32)
        order = [(chip, k, s) for chip in range(2) for k in range(2) for s in range(SEGS)]
        for chip, k, s in reversed(order) if back else order:
            one = slice(s, s + 1)
            r.cur[0, chip, k, one, :] = c_re
            r.cur[1, chip, k, one, :] = c_im
            prod = r.segk[l, chip, k, one, :]
            c_re, c_im = (
                prod * (all_cos * c_re - all_sin * c_im) + r.seg[0, chip, k, one, :],
                prod * (all_cos * c_im + all_sin * c_re) + r.seg[1, chip, k, one, :],
            )

    def forward_layer(l):
        turn_cos, turn_sin, lower = r.par[l, 0:1, :], r.par[l, 1:2, :], r.par[l, 2:3, :]
        gain_re, gain_im = r.par[l, 3:4, :], r.par[l, 4:5, :]
        e = 2 * l
        full = r.mixfull.at[l]

        def send_mix(c):
            @pl.when(l > 0)
            def _():
                s = r.st[2 * l - 1, c] + rs_final(e - 1, r.ffnfull.at[l - 1], c)
                r.st[2 * l, c] = s
                full[xi, c, core] = (s * norm_rows(s) * r.ngf[l, 0:1, :]).astype(BF16)
                ag_start(e, full, c)

        @pl.when(l == 0)
        def _():
            for copy in w_copies:
                copy.wait()

        r.seg[0:2] = jnp.zeros((2, 2, 2, SEGS, C), F32)
        r.seg[2] = jnp.ones((2, 2, SEGS, C), F32)

        def project(j):
            chip, c = chip_chunk(j, ascending, True)
            proj = mm_nt(flat(full[chip, c]), r.wmix[l])
            r.proj[l, chip, c] = proj.reshape(2, R, 5 * C)
            in_re, in_im, pre = proj[:, 0:C], proj[:, C : 2 * C], proj[:, 2 * C : 3 * C]
            rate = lower + (1.0 - lower) * sigmoid(pre)
            r.keep[chip, c] = rate.reshape(2, R, C)
            r.drive[0, chip, c] = ((1.0 - rate) * in_re * sigmoid(in_re)).reshape(2, R, C)
            r.drive[1, chip, c] = ((1.0 - rate) * in_im * sigmoid(in_im)).reshape(2, R, C)
            scan_local(l, chip, c, turn_cos, turn_sin)

        exchange_loop(e, full, ascending, send_mix, project)

        def send_cotangent(i):
            ag_start(2 * L, first_grad, l * z.early + i)

        loop(z.early, send_cotangent)
        r.segk[l] = r.seg[2]
        carry_over(l, False)
        for part in range(2):
            r.state[l, part, :, :, 0:SEGS, :] = r.cur[part]

        def mix(j):
            chip, c = chip_chunk(j, ascending, False)
            scan_final(l, chip, c, turn_cos, turn_sin)
            at = pl.ds(pl.multiple_of(SEGS + c * R, SEGS), R)
            s_re = flat(r.state[l, 0, chip, :, at, :])
            s_im = flat(r.state[l, 1, chip, :, at, :])
            centre = group_sum(s_re + s_im)
            d_re, d_im = s_re - centre, s_im - centre
            scale = lax.rsqrt(group_sum(d_re * d_re + d_im * d_im) + EPS_GROUP)
            u_re, u_im = d_re * scale, d_im * scale
            r.unit[l, 0, chip, c] = u_re.reshape(2, R, C)
            r.unit[l, 1, chip, c] = u_im.reshape(2, R, C)
            r.inv[l, chip, c] = scale.reshape(2, R, C)
            gate_re = flat(r.proj[l, chip, c, :, :, 3 * C : 4 * C])
            gate_im = flat(r.proj[l, chip, c, :, :, 4 * C : 5 * C])
            m_re = (u_re * gain_re * sigmoid(gate_re)).astype(BF16)
            m_im = (u_im * gain_im * sigmoid(gate_im)).astype(BF16)
            r.mixed[l, chip, c, :, :, 0:C] = m_re.reshape(2, R, C)
            r.mixed[l, chip, c, :, :, C : 2 * C] = m_im.reshape(2, R, C)
            r.psc[...] = mm(flat(r.mixed[l, chip, c]), r.wout[l]).reshape(2, R, D)

            rs_step(e, j, ascending, False)

        loop(2 * N, mix)

        def take_cotangent(i):
            ag_take_x(2 * L, first_grad, l * z.early + i)

        loop(z.early, take_cotangent)
        e2 = e + 1
        full2 = r.ffnfull.at[l]

        def send_ffn(c):
            s = r.st[2 * l, c] + rs_final(e, full, c)
            r.st[2 * l + 1, c] = s
            full2[xi, c, core] = (s * norm_rows(s) * r.ngf[l, 1:2, :]).astype(BF16)
            ag_start(e2, full2, c)

        def feed(j):
            chip, c = chip_chunk(j, ascending, True)
            both = mm(flat(full2[chip, c]), r.wffn[l])
            r.gup[l, chip, c] = both.astype(BF16).reshape(2, R, 2 * F)
            gate, up = both[:, 0:F], both[:, F : 2 * F]
            hidden = (gate * sigmoid(gate) * up).astype(BF16)
            r.hidden[l, chip, c] = hidden.reshape(2, R, F)
            r.psc[...] = mm(hidden, r.wdown[l]).reshape(2, R, D)

            rs_step(e2, j, ascending, True, l < L - 1)

        exchange_loop(e2, full2, ascending, send_ffn, feed)

        @pl.when(l < L - 1)
        def _():
            rs_pass(e2, N - 1)

    loop(L, forward_layer)

    def last_sum(c):
        e = 2 * L - 1
        s = r.st[2 * L - 1, c] + rs_final(e, r.ffnfull.at[L - 1], c)
        r.out[pl.ds(pl.multiple_of(c * R, R), R), :] = s.astype(BF16)

    def norm_back(l, which, c, grad_out):
        s = r.st[2 * l + which, c]
        scale = norm_rows(s)
        r.gacc[l, which] += fold(grad_out * s * scale)
        scaled = grad_out * r.ngf[l, which : which + 1, :]
        back = scale * scaled - s * (scale * scale * scale) * jnp.mean(
            scaled * s, axis=-1, keepdims=True
        )
        r.grad[c] = r.grad[c] + back

    def backward_layer(step):
        l = L - 1 - step
        e = 2 * L + 2 * step
        full = r.gfull.at[0]

        base = step * period
        pace = PACE[min(step, 1)]

        def send_ffn(c):
            if step > 0:
                norm_back(l + 1, 0, c, rs_final(e - 1, r.gfull.at[1], c))
                full[xi, c, core] = r.grad[c].astype(BF16)
                ag_start(e, full, c)

        def down_grad():
            part = mm_tn(flat(r.hidden[l]), flat(full[...])).astype(BF16)
            r.wg[l, n_ffn - z.fu : n_ffn] = part.reshape(z.fu, 2, z.blk, D)

        def feed_back(j):
            if step == 0:

                @pl.when(j == 0)
                def _():
                    down_grad()
                    ticks(2, base + 4)

            chip, c = chip_chunk(j, descending, step > 0)
            g_hidden = mm_nt(flat(full[chip, c]), r.wdown[l])
            both = flat(r.gup[l, chip, c]).astype(F32)
            gate, up = both[:, 0:F], both[:, F : 2 * F]
            s = sigmoid(gate)
            g_gate = (g_hidden * up * s * (1.0 + gate * (1.0 - s))).astype(BF16)
            g_up = (g_hidden * gate * s).astype(BF16)
            r.dgu[chip, c, :, :, 0:F] = g_gate.reshape(2, R, F)
            r.dgu[chip, c, :, :, F : 2 * F] = g_up.reshape(2, R, F)
            r.psc[...] = mm_nt(flat(r.dgu[chip, c]), r.wffn[l]).reshape(2, R, D)

            rs_step(e, j, descending, step > 0)

            if step > 0:

                @pl.when(j == 2 * N - 1)
                def _():
                    down_grad()

            ticks_in_loop(j, pace["feed"], lambda at: base + (4 if step == 0 or at == 2 * N - 1 else 0))

        exchange_loop(e, full, descending, send_ffn, feed_back, step == 0)
        if step > 0:
            rs_pass(e, 0)

        def ffn_tile(i):
            cols = pl.ds(pl.multiple_of(i * F, LANES), F)
            part = mm_tn(flat(r.ffnfull[l, :, :, :, :, cols]), flat(r.dgu[...])).astype(BF16)
            r.wg[l, pl.ds(i * z.fu, z.fu)] = part.reshape(z.fu, 2, z.blk, D)

        ticks(pace["feed_end"], base + 4)
        loop(D // F, ffn_tile)
        ticks(pace["ffn_end"], base + 12)

        turn_cos, turn_sin, lower = r.par[l, 0:1, :], r.par[l, 1:2, :], r.par[l, 2:3, :]
        gain_re, gain_im = r.par[l, 3:4, :], r.par[l, 4:5, :]
        e2 = e + 1
        full2 = r.gfull.at[1]

        def send_mix(c):
            norm_back(l, 1, c, rs_final(e, full, c))
            full2[xi, c, core] = r.grad[c].astype(BF16)
            ag_start(e2, full2, c)

        r.seg[0:2] = jnp.zeros((2, 2, 2, SEGS, C), F32)

        def mix_back(j):
            chip, c = chip_chunk(j, descending, True)
            g_both = mm_nt(flat(full2[chip, c]), r.wout[l])
            g_re, g_im = g_both[:, 0:C], g_both[:, C : 2 * C]
            s_re = sigmoid(flat(r.proj[l, chip, c, :, :, 3 * C : 4 * C]))
            s_im = sigmoid(flat(r.proj[l, chip, c, :, :, 4 * C : 5 * C]))
            u_re, u_im = flat(r.unit[l, 0, chip, c]), flat(r.unit[l, 1, chip, c])
            n_re, n_im = g_re * s_re, g_im * s_im
            r.sacc[l, 0] += fold(n_re * u_re)
            r.sacc[l, 1] += fold(n_im * u_im)
            x_re, x_im = n_re * gain_re, n_im * gain_im
            cross_re, cross_im = x_re * u_re, x_im * u_im
            r.dproj[chip, c, :, :, 3 * C : 4 * C] = (cross_re * (1.0 - s_re)).astype(BF16).reshape(2, R, C)
            r.dproj[chip, c, :, :, 4 * C : 5 * C] = (cross_im * (1.0 - s_im)).astype(BF16).reshape(2, R, C)
            mean_one = group_sum(x_re + x_im)
            mean_two = group_sum(cross_re + cross_im)
            scale = flat(r.inv[l, chip, c])
            r.drive[0, chip, c] = (scale * (x_re - mean_one - u_re * mean_two)).reshape(2, R, C)
            r.drive[1, chip, c] = (scale * (x_im - mean_one - u_im * mean_two)).reshape(2, R, C)
            pre = flat(r.proj[l, chip, c, :, :, 2 * C : 3 * C])
            r.keep[chip, c] = (lower + (1.0 - lower) * sigmoid(pre)).reshape(2, R, C)
            scan_back_local(l, chip, c, turn_cos, turn_sin)

            ticks_in_loop(j, pace["mix"], lambda at: base + 12)

        exchange_loop(e2, full2, descending, send_mix, mix_back)
        carry_over(l, True)

        def scan_back(j):
            chip, c = chip_chunk(j, descending, False)
            scan_back_final(l, chip, c, turn_cos, turn_sin)
            t_re, t_im = flat(r.tot[0]), flat(r.tot[1])
            at = pl.ds(pl.multiple_of(c * R, SEGS), R)
            p_re = flat(r.state[l, 0, chip, :, at, :])
            p_im = flat(r.state[l, 1, chip, :, at, :])
            in_re = flat(r.proj[l, chip, c, :, :, 0:C])
            in_im = flat(r.proj[l, chip, c, :, :, C : 2 * C])
            fs = sigmoid(flat(r.proj[l, chip, c, :, :, 2 * C : 3 * C]))
            rate = lower + (1.0 - lower) * fs
            s_re, s_im = sigmoid(in_re), sigmoid(in_im)
            gc_re = t_re * p_re + t_im * p_im
            gc_im = t_im * p_re - t_re * p_im
            g_keep = gc_re * turn_cos + gc_im * turn_sin - (t_re * in_re * s_re + t_im * in_im * s_im)
            r.sacc[l, 2] += fold(rate * (gc_im * turn_cos - gc_re * turn_sin))
            r.sacc[l, 3] += fold(g_keep * (1.0 - fs))
            d_re = t_re * (1.0 - rate) * s_re * (1.0 + in_re * (1.0 - s_re))
            d_im = t_im * (1.0 - rate) * s_im * (1.0 + in_im * (1.0 - s_im))
            d_f = g_keep * (1.0 - lower) * fs * (1.0 - fs)
            r.dproj[chip, c, :, :, 0:C] = d_re.astype(BF16).reshape(2, R, C)
            r.dproj[chip, c, :, :, C : 2 * C] = d_im.astype(BF16).reshape(2, R, C)
            r.dproj[chip, c, :, :, 2 * C : 3 * C] = d_f.astype(BF16).reshape(2, R, C)
            r.psc[...] = mm(flat(r.dproj[chip, c]), r.wmix[l]).reshape(2, R, D)

            rs_step(e2, j, descending, False)

            @pl.when(j == N)
            def _():
                loop(2, out_tile)
                loop(2, gate_tile)

            ticks_in_loop(j, pace["scan"], lambda at: base + (12 if at < N else 16))

        base_unit = z.units - 4

        def out_tile(i):
            cols = pl.ds(pl.multiple_of(i * C, LANES), C)
            part = mm_tn(flat(r.mixed[l, :, :, :, :, cols]), flat(full2[...])).astype(BF16)
            r.wg[l, base_unit, i] = part[0:ch]

        def proj_tile(k, unit, block):
            cols = pl.ds(pl.multiple_of(k * C, LANES), C)
            part = mm_tn(flat(r.dproj[:, :, :, :, cols]), flat(r.mixfull[l])).astype(BF16)
            r.wg[l, unit, block] = part[0:ch]

        def gate_tile(i):
            proj_tile(3 + i, base_unit + 1, i)

        def in_tile(i):
            proj_tile(i, base_unit + 2, i)

        def forget_tile():
            part = mm_tn(flat(r.dproj[:, :, :, :, 2 * C : 3 * C]), flat(r.mixfull[l])).astype(BF16)
            for half in range(2):
                r.wg[l, base_unit + 3, half, 0 : z.sub] = part[half * z.sub : (half + 1) * z.sub]

        loop(2 * N, scan_back)
        loop(2, in_tile)
        forget_tile()
        ticks(pace["end"], base + period)
        if step == L - 1:
            loop(N, lambda c: rs_pass(2 * L - 1, c))

    for step in range(L):
        backward_layer(step)

    def last_grad(j):
        c = descending(j)
        norm_back(0, 0, c, rs_final(4 * L - 1, r.gfull.at[1], c))

    ticks(AHEAD)
    loop(N, last_grad)
    r.ig[...] = r.grad[...].reshape(tokens, D).astype(BF16)

    r.swork[...] = jnp.zeros_like(r.swork)
    for l in range(L):
        for which in range(2):
            at = 2 * l + which
            r.swork[at : at + 1, :] = jnp.sum(r.gacc[l, which], axis=0, keepdims=True)

    for l in range(L):
        for k in range(4):
            value = jnp.sum(r.sacc[l, k], axis=0, keepdims=True)
            if k == 3:
                lower = r.par[l, 2:3, :]
                value = value * lower * (1.0 - lower)
            at = 2 * L + 4 * l + k
            r.swork[at : at + 1, 0:C] = value

    swap_peers = [sib, xnb] + ([y_peer, pair_peer, cross_peer] if z.reduce else [])
    n_swaps = len(swap_peers)

    def swap(k):
        return remote(r.swork, r.sland.at[k], r.ss.at[k], r.sr.at[k], swap_peers[k])

    for i in range(max(n_swaps + 1, last_tick - clock[0])):
        if 1 <= i <= n_swaps:
            k = i - 1
            swap(k).wait()
            rows = 2 * L if k < 2 else 2 * SEGS
            r.swork[0:rows, :] = r.swork[0:rows, :] + r.sland[k, 0:rows, :]
        if i < n_swaps:
            swap(i).start()
        ticks(1)
    loop(N, last_sum)
    r.sums[...] = r.swork[...]

    for u in range(period * L):
        if not z.reduce:
            unit_out(u).start()
        unit_out(u).wait()


def finish(z, n_tensor, out, ig, sums, w_in, w_forget, w_gate, w_out, w_ffn, w_down, *o):
    L, ch, F = z.L, z.ch, z.F
    l, i = pl.program_id(0), pl.program_id(1)
    tokens = out.shape[0]

    @pl.when((l == 0) & (i == 0))
    def _():
        o[0][...] = mm_tn(permutation(tokens), out[...]).astype(BF16)
        me = lax.axis_index("tensor")
        piece = z.D // n_tensor
        for t in range(n_tensor):

            @pl.when(me == t)
            def _():
                for k in range(L):
                    o[2][k] = sums[2 * k : 2 * k + 2, t * piece : (t + 1) * piece]

        for k in range(L):
            at = 2 * L + 4 * k
            o[7][k : k + 1, :] = sums[at + 2 : at + 3, 0:ch]
            o[8][k : k + 1, :] = sums[at + 3 : at + 4, 0:ch]
            o[9][k] = sums[at : at + 2, 0:ch]

    @pl.when((l == L - 1) & (i == 0))
    def _():
        o[1][...] = mm_tn(permutation(tokens), ig[...]).astype(BF16)

    o[3][...] = w_in[...].astype(F32)
    o[4][...] = w_forget[...].astype(F32)
    o[5][...] = w_gate[...].astype(F32)
    o[6][...] = w_out[...].astype(F32)
    o[10][0, 0] = w_ffn[0, :, 0:F].astype(F32)
    o[10][0, 1] = w_ffn[0, :, F : 2 * F].astype(F32)
    o[11][...] = w_down[...].astype(F32)


def local(*args):
    x, ct, ng, inw, fw, gw, ow, ph, bl, gg, ffw, dw = args
    L, D = ng.shape[0], ng.shape[2]
    ch = fw.shape[2]
    F = dw.shape[1]
    C = -(-ch // LANES) * LANES
    n_dp = lax.axis_size("dp")
    reduce = n_dp % 8 == 0
    fu = F // (2 * ch)
    units = fu * (1 + D // F) + 4
    sub = ch // 2
    period = 2 * units - 1
    z = types.SimpleNamespace(
        L=L, D=D, C=C, F=F, ch=ch, R=x.shape[0] // CHUNKS, reduce=reduce, blk=ch, fu=fu, units=units, sub=sub, period=period
    )
    z.early = CHUNKS // L
    names, scratch = scratch_of(z)
    vmem = pl.BlockSpec(memory_space=pltpu.VMEM)
    anywhere = pl.BlockSpec(memory_space=pl.ANY)
    in_specs = [vmem] * 12
    for k in (3, 4, 5, 6, 10, 11):
        in_specs[k] = anywhere
    shape = jax.ShapeDtypeStruct
    out, ig, wg, sums = pl.pallas_call(
        functools.partial(mega, z, names),
        out_shape=(
            shape(x.shape, BF16),
            shape(x.shape, BF16),
            shape((L, units, 2, ch, D), BF16),
            shape((2 * SEGS, D), F32),
        ),
        in_specs=in_specs,
        out_specs=[vmem, vmem, anywhere, vmem],
        scratch_shapes=scratch,
        compiler_params=pltpu.CompilerParams(
            collective_id=0, has_side_effects=True, vmem_limit_bytes=VMEM_BYTES
        ),
        name="layers",
    )(x, ct, ng, jnp.swapaxes(inw, 2, 3), jnp.swapaxes(fw, 1, 2), jnp.swapaxes(gw, 2, 3), ow, ph, bl, gg, ffw, dw)

    if not reduce:
        wg, sums = lax.psum((wg, sums), "dp")
    elif n_dp > 8:
        groups = [list(range(k, n_dp, 8)) for k in range(8)]
        wg, sums = lax.psum((wg, sums), "dp", axis_index_groups=groups)
    n_tensor = lax.axis_size("tensor")
    blocks = wg.reshape(L, 2 * units, ch, D)
    rows = wg.reshape(L, 2 * units * ch, D)
    G = 1
    piece = ch // G

    def block_spec(count, index):
        return pl.BlockSpec((1, count, piece, D), lambda l, i: (l, index, i, 0))

    def part_spec(index):
        return pl.BlockSpec((1, 2, sub // G, D), lambda l, i: (l, index, i, 0))

    def row_spec(size, index):
        return pl.BlockSpec((1, size, D), lambda l, i: (l, index + i, 0))

    def whole(*dims):
        return pl.BlockSpec(dims, lambda l, i: (0,) * len(dims))

    first = 2 * (units - 4)
    res = pl.pallas_call(
        functools.partial(finish, z, n_tensor),
        grid=(L, G),
        out_shape=(
            shape(x.shape, BF16),
            shape(x.shape, BF16),
            shape((L, 2, D // n_tensor), F32),
            shape((L, 2, ch, D), F32),
            shape((L, 2, sub, D), F32),
            shape((L, 2, ch, D), F32),
            shape((L, 2, ch, D), F32),
            shape((L, ch), F32),
            shape((L, ch), F32),
            shape((L, 2, ch), F32),
            shape((L, 2, D, F), F32),
            shape((L, F, D), F32),
        ),
        in_specs=[
            whole(*x.shape),
            whole(*x.shape),
            whole(2 * SEGS, D),
            block_spec(2, first // 2 + 2),
            part_spec(first // 2 + 3),
            block_spec(2, first // 2 + 1),
            block_spec(2, first // 2),
            row_spec(D // G, 0),
            row_spec(F // G, D // (F // G)),
        ],
        out_specs=[
            whole(*x.shape),
            whole(*x.shape),
            whole(L, 2, D // n_tensor),
            block_spec(2, 0),
            part_spec(0),
            block_spec(2, 0),
            block_spec(2, 0),
            whole(L, ch),
            whole(L, ch),
            whole(L, 2, ch),
            pl.BlockSpec((1, 2, D // G, F), lambda l, i: (l, 0, i, 0)),
            row_spec(F // G, 0),
        ],
        compiler_params=pltpu.CompilerParams(vmem_limit_bytes=VMEM_BYTES),
        name="finish",
    )(out, ig, sums, blocks, blocks, blocks, blocks, rows, rows)
    res = list(res)
    res[3] = jnp.swapaxes(res[3], 2, 3)
    res[4] = jnp.swapaxes(res[4].reshape(L, ch, D), 1, 2)
    res[5] = jnp.swapaxes(res[5], 2, 3)
    return tuple(res)


def solution(mesh):
    tokens = P(("dp", "tensor"), None)
    return jax.shard_map(
        local,
        mesh=mesh,
        in_specs=(
            tokens,
            tokens,
            P(),
            P(None, None, None, "tensor"),
            P(None, None, "tensor"),
            P(None, None, None, "tensor"),
            P(None, None, "tensor", None),
            P(None, "tensor"),
            P(None, "tensor"),
            P(None, None, "tensor"),
            P(None, None, None, "tensor"),
            P(None, "tensor", None),
        ),
        out_specs=(
            tokens,
            tokens,
            P(None, None, "tensor"),
            P(None, None, None, "tensor"),
            P(None, None, "tensor"),
            P(None, None, None, "tensor"),
            P(None, None, "tensor", None),
            P(None, "tensor"),
            P(None, "tensor"),
            P(None, None, "tensor"),
            P(None, None, None, "tensor"),
            P(None, "tensor", None),
        ),
        check_vma=False,
    )
```
